32 devices in a mesh: seq: 16 (over z, y, core), head: 2 (over x).
Axes of the slice: x: 2, y: 2, z: 4, core: 2. Of those that a mesh axis runs over, the one named last changes fastest.
Arguments:
- inputs: bfloat16 [2, 4096, 768], P(None, 'seq'), may hold values from -6 to 6
- qkv_weight: bfloat16 [3, 768, 768], P(None, None, 'head'), may hold values from -0.21875 to 0.21875
- qv_bias: float32 [2, 768], P(None, 'head'), may hold values from -3 to 3
- out_weight: bfloat16 [768, 768], P('head'), may hold values from -0.875 to 0.875
- out_bias: float32 [768], replicated, may hold values from -3 to 3
- ln1_gain: float32 [768], replicated, may hold values from 0.25 to 1.75
- ln1_bias: float32 [768], replicated, may hold values from -2 to 2
- ffn_in: bfloat16 [768, 3072], P(None, 'head'), may hold values from -0.21875 to 0.21875
- ffn_in_bias: float32 [3072], P('head'), may hold values from -3 to 3
- ffn_out: bfloat16 [3072, 768], P('head'), may hold values from -0.15625 to 0.15625
- ffn_out_bias: float32 [768], replicated, may hold values from -3 to 3
- ln2_gain: float32 [768], replicated, may hold values from 0.25 to 1.75
- ln2_bias: float32 [768], replicated, may hold values from -2 to 2
- short_lengths: int32 [8], replicated, may hold values from 256 to 512, as said below
- long_lengths: int32 [2], replicated, may hold values from 1024 to 2048, as said below
- short_random: int32 [64, 3], P('seq'), may hold values from 2 to 7, as said below
- long_random: int32 [64, 3], P('seq'), may hold values from 2 to 31, as said below
- cotangent: bfloat16 [2, 4096, 768], P(None, 'seq'), may hold values from -6 to 6
Outputs:
- output: bfloat16 [2, 4096, 768], P(None, 'seq')
- input_grad: bfloat16 [2, 4096, 768], P(None, 'seq')
- qkv_weight_grad: float32 [3, 768, 768], P(None, None, 'head')
- qv_bias_grad: float32 [2, 768], P(None, 'head')
- out_weight_grad: float32 [768, 768], P('head')
- out_bias_grad: float32 [768], replicated
- ln1_gain_grad: float32 [768], replicated
- ln1_bias_grad: float32 [768], replicated
- ffn_in_grad: float32 [768, 3072], P(None, 'head')
- ffn_in_bias_grad: float32 [3072], P('head')
- ffn_out_grad: float32 [3072, 768], P('head')
- ffn_out_bias_grad: float32 [768], replicated
- ln2_gain_grad: float32 [768], replicated
- ln2_bias_grad: float32 [768], replicated
The draws below stay inside these ranges and needn't reach their ends.
Inputs may be any that keep to these rules, and one draw needn't show every extreme that they name: `short_lengths`: each sequence has between half its padded length 512 and all of it valid; at least one has exactly 512. `long_lengths`: each sequence has between half its padded length 2048 and all of it valid; at least one has exactly 2048. `short_random`: each row holds 3 different block numbers of its own sequence, none below 2 and none within one block of the row's own block. `long_random`: each row holds 3 different block numbers of its own sequence, none below 2 and none within one block of the row's own block.
All inputs are finite; a program needn't handle non-finite values.
Results may differ from the reference program's by a relative error of at most 0.02.
Values may be sent and summed in bfloat16 or wider, within the bound.
A program may use at most 192 MiB of HBM per device.

```python
import jax
import jax.numpy as jnp
from jax import lax

D = 768
HEADS = 12
HDIM = 64
FF = 3072
BLK = 64
GLOB = 2
RAND = 3
SHORT_LEN = 512
LONG_LEN = 2048
SHORT_SEQS = 8
LONG_SEQS = 2
MB_TOKENS = 4096
MB_BLOCKS = 64


def draw_lengths(key, seq_count, longest):
    picked = jax.random.randint(key, (seq_count,), longest // 2, longest + 1)
    chosen = jax.random.randint(jax.random.fold_in(key, 7), (), 0, seq_count)
    return picked.at[chosen].set(longest).astype(jnp.int32)


def draw_blocks(key, row_count, seq_blocks):
    own_block = jnp.arange(row_count, dtype=jnp.int32) % seq_blocks
    candidate = jnp.arange(seq_blocks, dtype=jnp.int32)
    banned = (candidate[None, :] < GLOB) | (jnp.abs(candidate[None, :] - own_block[:, None]) <= 1)
    ranking = jax.random.randint(key, (row_count, seq_blocks), 0, 1 << 20) * seq_blocks + candidate[None, :]
    ranking = jnp.where(banned, ranking + (1 << 30), ranking)
    return jnp.argsort(ranking, axis=1)[:, :RAND].astype(jnp.int32)


def draw_short_lengths(key, part):
    key = jax.random.fold_in(key, 1)
    return draw_lengths(key, SHORT_SEQS, SHORT_LEN)


def draw_long_lengths(key, part):
    key = jax.random.fold_in(key, 2)
    return draw_lengths(key, LONG_SEQS, LONG_LEN)


def draw_short_random(key, part):
    key = jax.random.fold_in(key, 3)
    return draw_blocks(key, MB_BLOCKS, SHORT_LEN // BLK)


def draw_long_random(key, part):
    key = jax.random.fold_in(key, 4)
    return draw_blocks(key, MB_BLOCKS, LONG_LEN // BLK)


def shard_levels(stream_key, extent, cuts, low, top_value):
    loudness, own = 1.0, jax.random.fold_in(stream_key, 6)
    for dim, parts in cuts:
        draws = jnp.exp(jax.random.uniform(jax.random.fold_in(own, dim), (parts,), jnp.float32, low / len(cuts), top_value / len(cuts)))
        loudness = loudness * jnp.repeat(draws, extent[dim] // parts).reshape([-1 if axis == dim else 1 for axis in range(len(extent))])
    return loudness


def gaussian(stream_key, dims, deviation, reach, split=(), kind=jnp.bfloat16):
    level = shard_levels(stream_key, dims, split, -0.22, 0.18) if split else 1.0
    values = jax.random.normal(stream_key, dims, jnp.float32) * deviation * level
    return jnp.minimum(jnp.maximum(values, -reach), reach).astype(kind)


def setup_inputs(seed: int = 0) -> dict:
    keys = jax.random.split(jax.random.key(seed), 19)
    return {
        "inputs": gaussian(keys[0], (2, MB_TOKENS, D), 1.0, 6.0, ((1, 16),)),
        "qkv_weight": gaussian(keys[1], (3, D, D), D ** -0.5, 0.21875, ((2, 2),)),
        "qv_bias": gaussian(keys[2], (2, D), 0.5, 3.0, ((1, 2),), jnp.float32),
        "out_weight": gaussian(keys[3], (D, D), (D // 16) ** -0.5, 0.875, ((0, 2),)),
        "out_bias": gaussian(keys[4], (D,), 0.5, 3.0, (), jnp.float32),
        "ln1_gain": jnp.clip(1.0 + 0.15 * jax.random.normal(keys[5], (D,), jnp.float32), 0.25, 1.75),
        "ln1_bias": gaussian(keys[6], (D,), 0.3, 2.0, (), jnp.float32),
        "ffn_in": gaussian(keys[7], (D, FF), D ** -0.5, 0.21875, ((1, 2),)),
        "ffn_in_bias": gaussian(keys[8], (FF,), 0.5, 3.0, ((0, 2),), jnp.float32),
        "ffn_out": gaussian(keys[9], (FF, D), (FF // 2) ** -0.5, 0.15625, ((0, 2),)),
        "ffn_out_bias": gaussian(keys[10], (D,), 0.5, 3.0, (), jnp.float32),
        "ln2_gain": jnp.clip(1.0 + 0.15 * jax.random.normal(keys[11], (D,), jnp.float32), 0.25, 1.75),
        "ln2_bias": gaussian(keys[12], (D,), 0.3, 2.0, (), jnp.float32),
        "short_lengths": draw_short_lengths(jax.random.fold_in(keys[18], 71), 0),
        "long_lengths": draw_long_lengths(jax.random.fold_in(keys[18], 71), 0),
        "short_random": draw_short_random(jax.random.fold_in(keys[18], 71), 0),
        "long_random": draw_long_random(jax.random.fold_in(keys[18], 71), 0),
        "cotangent": gaussian(keys[17], (2, MB_TOKENS, D), 1.0, 6.0, ((1, 16),)),
    }


EPSILON = 1e-06
NEGATIVE = -1000000000.0
HIGHEST = lax.Precision.HIGHEST

@jax.custom_vjp
def low(v):
    return lax.optimization_barrier(v.astype(jnp.bfloat16)).astype(jnp.float32)

@jax.custom_vjp
def low_back(v):
    return v

def low_keep(v):
    return (low(v), None)

def low_pass(kept, grad):
    return (grad,)

def back_keep(v):
    return (v, None)

def back_low(kept, grad):
    return (low(grad),)
low.defvjp(low_keep, low_pass)
low_back.defvjp(back_keep, back_low)

def layer_norm(token_rows, gain, shift):
    centre = lax.optimization_barrier(jnp.mean(token_rows, axis=-1, keepdims=True))
    centred = token_rows - centre
    spread = lax.optimization_barrier(jnp.mean(centred * centred, axis=-1, keepdims=True))
    return centred * lax.rsqrt(spread + EPSILON) * gain + shift

def attend_sequence(queries, key_rows, values, seq_length, key_table):
    seq_tokens = queries.shape[0]
    group_count = seq_tokens // (8 * BLK)
    key_block = jnp.arange(seq_tokens, dtype=jnp.int32) // BLK
    key_live = jnp.arange(seq_tokens, dtype=jnp.int32) < seq_length
    inv_root = HDIM ** (-0.5)

    def one_group(group_start):
        query_rows = lax.dynamic_slice_in_dim(queries, group_start * (8 * BLK), 8 * BLK, 0)
        row_block = group_start * 8 + jnp.arange(8 * BLK, dtype=jnp.int32) // BLK
        picked = jnp.repeat(lax.dynamic_slice_in_dim(key_table, group_start * 8, 8, 0), BLK, axis=0)
        chosen = jnp.any(picked[:, :, None] == key_block[None, None, :], axis=1)
        beside = jnp.abs(row_block[:, None] - key_block[None, :]) <= 1
        allowed = (row_block[:, None] < GLOB) | (key_block[None, :] < GLOB) | beside | chosen
        allowed = allowed & key_live[None, :]
        scores = low_back(inv_root * jnp.einsum('qhd,khd->hqk', query_rows, key_rows, precision=HIGHEST))
        scores = jnp.where(allowed[None], scores, NEGATIVE)
        row_max = lax.optimization_barrier(jnp.max(scores, axis=-1, keepdims=True))
        weights = jnp.exp(scores - row_max)
        probs = weights / lax.optimization_barrier(jnp.sum(weights, axis=-1, keepdims=True))
        return jnp.einsum('hqk,khd->qhd', low(probs), values, precision=HIGHEST)
    blocks_out = lax.map(jax.checkpoint(one_group), jnp.arange(group_count, dtype=jnp.int32))
    return blocks_out.reshape(queries.shape)

def micro_batch(token_rows, params, lengths, key_table, seq_len):
    qkv_w, qv_b, out_w, out_b, gain_one, bias_one, in_w, in_b, back_w, back_b, gain_two, bias_two = params
    rows_low = low(token_rows)
    projected = jnp.einsum('td,cde->cte', rows_low, qkv_w, precision=HIGHEST)
    queries = low(low_back(projected[0] + qv_b[0]))
    key_rows = low(low_back(projected[1]))
    values = low(low_back(projected[2] + qv_b[1]))
    seq_count = token_rows.shape[0] // seq_len
    seq_shape = (seq_count, seq_len, HEADS, HDIM)
    seq_blocks = seq_len // BLK
    mixed = lax.map(lambda item: attend_sequence(item[0], item[1], item[2], item[3], item[4]), (queries.reshape(seq_shape), key_rows.reshape(seq_shape), values.reshape(seq_shape), lengths, key_table.reshape(seq_count, seq_blocks, RAND)))
    mixed = low(low_back(mixed.reshape(token_rows.shape)))
    attention = low_back(jnp.dot(mixed, out_w, precision=HIGHEST))
    hidden = layer_norm(attention + out_b + token_rows, gain_one, bias_one)
    inner = low_back(jnp.dot(low(hidden), in_w, precision=HIGHEST) + in_b)
    activated = low(low_back(jax.nn.gelu(inner, approximate=True)))
    feed_out = low_back(jnp.dot(activated, back_w, precision=HIGHEST))
    return layer_norm(feed_out + back_b + hidden, gain_two, bias_two)

def reference(inputs, qkv_weight, qv_bias, out_weight, out_bias, ln1_gain, ln1_bias, ffn_in, ffn_in_bias, ffn_out, ffn_out_bias, ln2_gain, ln2_bias, short_lengths, long_lengths, short_random, long_random, cotangent):
    params = tuple((item.astype(jnp.float32) for item in (qkv_weight, qv_bias, out_weight, out_bias, ln1_gain, ln1_bias, ffn_in, ffn_in_bias, ffn_out, ffn_out_bias, ln2_gain, ln2_bias)))
    token_rows = inputs.astype(jnp.float32)

    def forward(all_rows, weights):
        first_out = micro_batch(all_rows[0], weights, short_lengths, short_random, SHORT_LEN)
        second_out = micro_batch(all_rows[1], weights, long_lengths, long_random, LONG_LEN)
        return jnp.stack([first_out, second_out])
    result, pullback = jax.vjp(forward, token_rows, params)
    grad_rows, grads = pullback(cotangent.astype(jnp.float32))
    g_qkv, g_qvb, g_out, g_outb, g_gone, g_bone, g_in, g_inb, g_back, g_backb, g_gtwo, g_btwo = grads
    return (result.astype(jnp.bfloat16), grad_rows.astype(jnp.bfloat16), g_qkv, g_qvb, g_out, g_outb, g_gone, g_bone, g_in, g_inb, g_back, g_backb, g_gtwo, g_btwo)
```

```python
import functools
import math

import jax
import jax.numpy as jnp
from jax import lax
from jax.experimental import pallas as pl
from jax.experimental.pallas import tpu as pltpu
from jax.sharding import PartitionSpec as P

MESH = pl.DeviceIdType.MESH
F32 = jnp.float32
BF16 = jnp.bfloat16
EPSILON = 1e-06
NEGATIVE = -1000000000.0
HDIM = 64
BLK = 64
SHORT, LONG = 0, 1
ROOT = math.sqrt(2.0 / math.pi)
CUBIC = 0.044715
COPIES = 96
VEC_ROWS = 256


def dot(a, b, ca=1, cb=0):
    return lax.dot_general(a, b, (((ca,), (cb,)), ((), ())), preferred_element_type=F32)


def aligned(start, size, step):
    return pl.ds(pl.multiple_of(start, step), size)


def loop(count, step):
    def run(index, carry):
        step(index)
        return carry

    lax.fori_loop(0, count, run, 0)


class Links:
    def __init__(self, send_sem, recv_sem, seq, head):
        self.send_sem, self.recv_sem, self.seq, self.head = send_sem, recv_sem, seq, head
        self.used = 0

    def copy(self, src, dst, seq_delta=0, head_delta=0):
        index = self.used
        self.used += 1
        item = pltpu.make_async_remote_copy(
            src_ref=src,
            dst_ref=dst,
            send_sem=self.send_sem.at[index],
            recv_sem=self.recv_sem.at[index],
            device_id=(self.seq ^ seq_delta, self.head ^ head_delta),
            device_id_type=MESH,
        )
        item.start()
        return item


def add_rows(into, into_start, more, more_start, rows, tile):
    def step(i):
        a = aligned(into_start + i * tile, tile, 16)
        b = aligned(more_start + i * tile, tile, 16)
        into[a, :] = (into[a, :].astype(F32) + more[b, :].astype(F32)).astype(BF16)

    loop(rows // tile, step)


class Reduction:
    def __init__(self, links, part, out, recv_core, recv_next, recv_far, recv_up, upper, local_sem):
        self.links, self.part, self.out = links, part, out
        self.recv_core, self.recv_next, self.recv_far = recv_core, recv_next, recv_far
        self.recv_up, self.upper, self.local_sem = recv_up, upper, local_sem
        rows = part.shape[0]
        self.half, self.quarter, self.share = rows // 2, rows // 4, rows // 16
        self.tile = min(48, self.share)
        seq = links.seq
        core, near, far = seq & 1, (seq >> 1) & 1, (seq >> 2) & 3
        self.core, self.near, self.far = core, near, far
        self.half_at = core * self.half
        self.quarter_at = self.half_at + near * self.quarter
        self.other_quarter_at = self.half_at + (1 - near) * self.quarter
        self.share_at = self.quarter_at + far * self.share
        self.sent = []

    def rows(self, ref, start, count):
        return ref.at[aligned(start, count, 16), :]

    def go(self, src, dst, delta):
        item = self.links.copy(src, dst, delta)
        self.sent.append(item)
        return item

    def start(self):
        self.first = self.go(
            self.rows(self.part, (1 - self.core) * self.half, self.half), self.recv_core, 1
        )

    def over_next(self):
        self.first.wait_recv()
        away = (1 - self.near) * self.quarter
        home = self.near * self.quarter
        add_rows(self.part, self.other_quarter_at, self.recv_core, away, self.quarter, self.tile)
        self.second = self.go(
            self.rows(self.part, self.other_quarter_at, self.quarter), self.recv_next, 2
        )
        add_rows(self.part, self.quarter_at, self.recv_core, home, self.quarter, self.tile)

    def over_far(self):
        self.second.wait_recv()
        self.third = []
        for d in (3, 1, 2):
            there = (self.far ^ d) * self.share
            add_rows(self.part, self.quarter_at + there, self.recv_next, there, self.share, self.tile)
            self.third.append(
                self.go(
                    self.rows(self.part, self.quarter_at + there, self.share),
                    self.recv_far.at[d - 1],
                    4 * d,
                )
            )
        here = self.far * self.share
        add_rows(self.part, self.share_at, self.recv_next, here, self.share, self.tile)

    def total(self):
        for item in self.third:
            item.wait_recv()

        def step(i):
            a = aligned(self.share_at + i * self.tile, self.tile, 16)
            b = aligned(i * self.tile, self.tile, 16)
            total = self.part[a, :].astype(F32)
            for d in range(3):
                total = total + self.recv_far[d, b, :].astype(F32)
            self.part[a, :] = total.astype(BF16)

        loop(self.share // self.tile, step)
        mine = self.rows(self.part, self.share_at, self.share)
        for level, delta in enumerate(self.upper):
            item = self.links.copy(mine, self.recv_up.at[level], delta)
            item.wait()
            add_rows(self.part, self.share_at, self.recv_up.at[level], 0, self.share, self.tile)
        there = self.rows(self.out, self.share_at, self.share)
        self.fourth = [self.go(mine, there, 4 * d) for d in (3, 1, 2)]
        self.kept = pltpu.make_async_copy(mine, there, self.local_sem)
        self.kept.start()

    def back_next(self):
        for item in self.fourth:
            item.wait_recv()
        self.kept.wait()
        block = self.rows(self.out, self.quarter_at, self.quarter)
        self.fifth = self.go(block, block, 2)

    def back_core(self):
        self.fifth.wait_recv()
        block = self.rows(self.out, self.half_at, self.half)
        self.sixth = self.go(block, block, 1)

    def finish(self):
        self.sixth.wait_recv()
        for item in self.sent:
            item.wait_send()


def kernel(
    seq_count,
    x_in,
    cot_in,
    qkvw_in,
    outw_in,
    win_in,
    wout_in,
    qv_bias,
    out_bias,
    gain_one,
    bias_one,
    in_bias,
    back_bias,
    gain_two,
    bias_two,
    short_len,
    long_len,
    short_table,
    long_table,
    out,
    in_grad,
    sum_back,
    sum_in,
    sum_query,
    sum_pair,
    sum_vec,
    x,
    cot,
    qkvw,
    outw,
    win,
    wout,
    kv_short,
    kv_long,
    q_rows,
    q_cols,
    live_short,
    live_long,
    mixed_cols,
    mixed,
    log_total,
    post_out,
    post_in,
    norm_one,
    root_one,
    hidden,
    act,
    slope,
    grad_rows,
    grad_feed,
    grad_inner,
    grad_attn,
    grad_mixed,
    grad_cols,
    dkv_short,
    dkv_long,
    got_short,
    got_core,
    got_far,
    grad_proj,
    part_back,
    part_in,
    part_query,
    part_pair,
    part_vec,
    vec,
    rc_back,
    rc_in,
    rc_query,
    rc_pair,
    rc_vec,
    rn_back,
    rn_in,
    rn_query,
    rn_pair,
    rn_vec,
    rf_back,
    rf_in,
    rf_query,
    rf_pair,
    rf_vec,
    *rest,
):
    upper = [16 << i for i in range(max(0, seq_count.bit_length() - 5))]
    if upper:
        ups = rest[:5]
        rest = rest[5:]
    else:
        ups = (None,) * 5
    send_sem, recv_sem, load_sem, local_sem = rest
    seq, head = lax.axis_index("seq"), lax.axis_index("head")
    links = Links(send_sem, recv_sem, seq, head)
    tok = x.shape[1]
    wide = x.shape[2]
    col = qkvw.shape[2]
    ff = win.shape[1]
    pairs = col // (2 * HDIM)
    blocks = tok // BLK
    short_span = seq_count // short_len.shape[0]
    long_span = seq_count // long_len.shape[0]
    core = seq & 1

    deltas = [1, 2, 4, 6, 8, 12] + upper
    barrier = pltpu.get_barrier_semaphore()
    for delta in deltas:
        pl.semaphore_signal(barrier, inc=1, device_id=(seq ^ delta, head), device_id_type=MESH)
    pl.semaphore_signal(barrier, inc=1, device_id=(seq, head ^ 1), device_id_type=MESH)

    loads = []
    for i, (src, dst) in enumerate(
        ((x_in, x), (qkvw_in, qkvw), (outw_in, outw), (win_in, win), (wout_in, wout), (cot_in, cot))
    ):
        item = pltpu.make_async_copy(src, dst, load_sem.at[i])
        item.start()
        loads.append(item)

    def tokens(mb):
        return pl.ds(mb * tok, tok)

    vec[...] = jnp.zeros_like(vec)
    loads[0].wait()
    loads[1].wait()

    def project(mb, c):
        return dot(x[mb], qkvw[c])

    place = seq & (long_span - 1)
    side = seq & (short_span - 1)
    kv_long[0, place] = project(LONG, 1).astype(BF16)
    kv_long[1, place] = (project(LONG, 2) + qv_bias[1:2, :]).astype(BF16)
    pl.semaphore_wait(barrier, len(deltas) + 1)
    long_direct = {
        d: links.copy(kv_long.at[:, place], kv_long.at[:, place], d) for d in (2, 4, 6)
    }
    long_core = links.copy(kv_long.at[:, place], kv_long.at[:, place], 1)
    kv_short[0, side] = project(SHORT, 1).astype(BF16)
    kv_short[1, side] = (project(SHORT, 2) + qv_bias[1:2, :]).astype(BF16)
    short_core = links.copy(kv_short.at[:, side], kv_short.at[:, side], 1)
    for mb in (SHORT, LONG):
        query = (project(mb, 0) + qv_bias[0:1, :]).astype(BF16).astype(F32) * (HDIM**-0.5)
        q_rows[mb] = query.astype(BF16)
        for g in range(pairs):
            lanes = slice(g * 128, g * 128 + 128)
            q_cols[mb, lanes, :] = query[:, lanes].T.astype(BF16)

    def make_live(live, count, spot, table, length):
        lane_block = lax.broadcasted_iota(jnp.int32, (1, tok), 1) >> 6
        row_block = spot * blocks + lane_block
        picks = []
        for k in range(table.shape[1]):
            pick = jnp.full((1, tok), table[0, k], jnp.int32)
            for b in range(1, blocks):
                pick = jnp.where(lane_block == b, table[b, k], pick)
            picks.append(pick)

        def step(t):
            key = t * tok + lax.broadcasted_iota(jnp.int32, (tok, tok), 0)
            block = key >> 6
            allowed = (block < 2) | (row_block < 2) | (jnp.abs(row_block - block) <= 1)
            for pick in picks:
                allowed = allowed | (block == pick)
            live[t] = jnp.where(allowed & (key < length), 0.0, NEGATIVE)

        loop(count, step)

    make_live(live_short, short_span, side, short_table, short_len[seq // short_span])
    make_live(live_long, long_span, place, long_table, long_len[seq // long_span])

    def spread_cols(pair):
        zero = jnp.zeros((HDIM, tok), BF16)
        return jnp.concatenate(
            [
                jnp.concatenate([pair[:HDIM], zero], 0),
                jnp.concatenate([zero, pair[HDIM:]], 0),
            ],
            1,
        )

    def spread_rows(pair):
        lane = lax.broadcasted_iota(jnp.int32, (tok, 128), 1)
        full = pair.astype(F32)
        return jnp.concatenate(
            [jnp.where(lane < HDIM, full, 0.0), jnp.where(lane < HDIM, 0.0, full)], 0
        ).astype(BF16)

    def attend(mb, kv, live, count):
        def pair_step(g):
            lanes = aligned(g * 128, 128, 128)
            q2 = spread_cols(q_cols[mb, lanes, :])

            def tile_step(t, carry):
                top, total, acc_a, acc_b = carry
                keys = kv[0, t, :, lanes]
                values = kv[1, t, :, lanes]
                mask = live[t]
                scores = dot(keys, q2) + jnp.concatenate([mask, mask], 1)
                new_top = jnp.maximum(top, jnp.max(scores, axis=0, keepdims=True))
                scale = jnp.exp(top - new_top)
                weights = jnp.exp(scores - new_top)
                total = total * scale + jnp.sum(weights, axis=0, keepdims=True)
                low = weights.astype(BF16)
                turned = values.T
                acc_a = acc_a * scale[:, :tok] + dot(turned[:HDIM], low[:, :tok])
                acc_b = acc_b * scale[:, tok:] + dot(turned[HDIM:], low[:, tok:])
                return new_top, total, acc_a, acc_b

            top, total, acc_a, acc_b = lax.fori_loop(
                0,
                count,
                tile_step,
                (
                    jnp.full((1, 2 * tok), -3.0e38, F32),
                    jnp.zeros((1, 2 * tok), F32),
                    jnp.zeros((HDIM, tok), F32),
                    jnp.zeros((HDIM, tok), F32),
                ),
            )
            inverse = 1.0 / total
            pair = jnp.concatenate([acc_a * inverse[:, :tok], acc_b * inverse[:, tok:]], 0)
            mixed_cols[mb, lanes, :] = pair
            mixed[tokens(mb), lanes] = pair.T.astype(BF16)
            log_total[mb * pairs + g] = top + jnp.log(total)

        loop(pairs, pair_step)

    def post(stage, mb):
        buf = stage % 2
        return links.copy(post_out.at[buf, mb], post_in.at[buf, mb], 0, 1)

    def received(stage, mb, rows):
        buf = stage % 2
        return post_out[buf, mb, rows, :].astype(F32) + post_in[buf, mb, rows, :].astype(F32)

    def attention_out(mb):
        post_out[0, mb] = dot(mixed[tokens(mb), :], outw[...]).astype(BF16)
        return post(0, mb)

    short_core.wait()
    attend(SHORT, kv_short, live_short, short_span)
    loads[2].wait()
    posts = {(0, SHORT): attention_out(SHORT)}

    forwards = []
    for d in (2, 4, 6):
        long_direct[d].wait_recv()
        spot = place ^ d
        forwards.append(links.copy(kv_long.at[:, spot], kv_long.at[:, spot], 1))
    long_core.wait()
    for item in forwards:
        item.wait()
    attend(LONG, kv_long, live_long, long_span)
    posts[0, LONG] = attention_out(LONG)
    for d in (2, 4, 6):
        long_direct[d].wait_send()

    def mean(value):
        return jnp.sum(value, axis=-1, keepdims=True) * (1.0 / wide)

    def vec_add(index, value):
        vec[index : index + 1, :wide] += jnp.sum(value, axis=0, keepdims=True)

    OUTB, GAIN1, BIAS1, BACKB, GAIN2, BIAS2 = range(6)

    tile_rows = 64

    def feed_forward(mb):
        posts[0, mb].wait()

        def norm_step(r):
            rows = aligned(r * tile_rows, tile_rows, tile_rows)
            joined = received(0, mb, rows) + out_bias[...] + x[mb, rows, :].astype(F32)
            centred = joined - mean(joined)
            root = lax.rsqrt(mean(centred * centred) + EPSILON)
            normed = centred * root
            norm_one[mb, rows, :] = normed
            root_one[mb, rows, :] = jnp.broadcast_to(root, (tile_rows, 128))
            all_rows = aligned(mb * tok + r * tile_rows, tile_rows, tile_rows)
            hidden[all_rows, :] = (normed * gain_one[...] + bias_one[...]).astype(BF16)

        loop(tok // tile_rows, norm_step)

        def col_step(j):
            lanes = aligned(j * 512, 512, 512)
            u = dot(hidden[tokens(mb), :], win[:, lanes]) + in_bias[:, lanes]
            square = u * u
            t = jnp.tanh(ROOT * u * (1.0 + CUBIC * square))
            half = 0.5 * (1.0 + t)
            act[tokens(mb), lanes] = (u * half).astype(BF16)
            slope[mb, :, lanes] = half + (0.5 * ROOT) * u * (1.0 - t * t) * (
                1.0 + (3.0 * CUBIC) * square
            )

        loop(ff // 512, col_step)
        post_out[1, mb] = dot(act[tokens(mb), :], wout[...]).astype(BF16)
        posts[1, mb] = post(1, mb)

    loads[3].wait()
    loads[4].wait()
    loads[5].wait()
    feed_forward(SHORT)
    feed_forward(LONG)

    def norm_back(grad, normed, root):
        return root * (grad - mean(grad) - normed * mean(grad * normed))

    def feed_back(mb):
        posts[1, mb].wait()

        def norm_step(r):
            rows = aligned(r * tile_rows, tile_rows, tile_rows)
            all_rows = aligned(mb * tok + r * tile_rows, tile_rows, tile_rows)
            hid = norm_one[mb, rows, :] * gain_one[...] + bias_one[...]
            second = received(1, mb, rows) + back_bias[...] + hid
            centred = second - mean(second)
            root = lax.rsqrt(mean(centred * centred) + EPSILON)
            normed = centred * root
            out[mb, rows, :] = (normed * gain_two[...] + bias_two[...]).astype(BF16)
            g = cot[mb, rows, :].astype(F32)
            vec_add(GAIN2, g * normed)
            vec_add(BIAS2, g)
            grad = norm_back(g * gain_two[...], normed, root)
            vec_add(BACKB, grad)
            grad_rows[mb, rows, :] = grad
            grad_feed[all_rows, :] = grad.astype(BF16)

        loop(tok // tile_rows, norm_step)

        def col_step(j):
            lanes = aligned(j * 512, 512, 512)
            grad_act = dot(grad_feed[tokens(mb), :], wout[lanes, :], 1, 1).astype(BF16)
            low = (grad_act.astype(F32) * slope[mb, :, lanes]).astype(BF16)
            grad_inner[tokens(mb), lanes] = low
            vec[6:7, lanes] += jnp.sum(low.astype(F32), axis=0, keepdims=True)

        loop(ff // 512, col_step)
        post_out[0, mb] = dot(grad_inner[tokens(mb), :], win[...], 1, 1).astype(BF16)
        posts[2, mb] = post(2, mb)

    feed_back(SHORT)
    feed_back(LONG)

    def reduction(index, part, total, first, second, third):
        return Reduction(
            links, part, total, first, second, third, ups[index], upper, local_sem.at[index]
        )

    red_back = reduction(0, part_back, sum_back, rc_back, rn_back, rf_back)
    red_in = reduction(1, part_in, sum_in, rc_in, rn_in, rf_in)
    red_query = reduction(2, part_query, sum_query, rc_query, rn_query, rf_query)
    red_pair = reduction(3, part_pair, sum_pair, rc_pair, rn_pair, rf_pair)
    red_vec = reduction(4, part_vec, sum_vec, rc_vec, rn_vec, rf_vec)

    def back_step(j):
        rows = aligned(j * 256, 256, 256)
        part_back[rows, :] = dot(act[:, rows], grad_feed[...], 0, 0).astype(BF16)

    loop(ff // 256, back_step)
    red_back.start()

    def in_step(j):
        rows = aligned(j * 256, 256, 256)
        part_in[rows, :] = dot(hidden[:, rows], grad_inner[...], 0, 0).astype(BF16)

    loop(wide // 256, in_step)
    red_in.start()

    def norm_one_back(mb):
        posts[2, mb].wait()

        def norm_step(r):
            rows = aligned(r * tile_rows, tile_rows, tile_rows)
            all_rows = aligned(mb * tok + r * tile_rows, tile_rows, tile_rows)
            grad = grad_rows[mb, rows, :] + received(2, mb, rows)
            normed = norm_one[mb, rows, :]
            vec_add(GAIN1, grad * normed)
            vec_add(BIAS1, grad)
            joined = norm_back(grad * gain_one[...], normed, root_one[mb, rows, :1])
            vec_add(OUTB, joined)
            grad_rows[mb, rows, :] = joined
            grad_attn[all_rows, :] = joined.astype(BF16)

        loop(tok // tile_rows, norm_step)
        low = dot(grad_attn[tokens(mb), :], outw[...], 1, 1).astype(BF16)
        grad_mixed[...] = low
        for g in range(pairs):
            lanes = slice(g * 128, g * 128 + 128)
            grad_cols[lanes, :] = low[:, lanes].astype(F32).T

    def attend_back(mb, kv, live, count, store):
        def pair_step(g):
            lanes = aligned(g * 128, 128, 128)
            q2 = spread_cols(q_cols[mb, lanes, :])
            cols = grad_cols[lanes, :]
            g2 = spread_cols(cols.astype(BF16))
            q2_rows = spread_rows(q_rows[mb, :, lanes])
            g2_rows = spread_rows(grad_mixed[:, lanes])
            product = cols * mixed_cols[mb, lanes, :]
            delta = jnp.concatenate(
                [
                    jnp.sum(product[:HDIM], axis=0, keepdims=True),
                    jnp.sum(product[HDIM:], axis=0, keepdims=True),
                ],
                1,
            )
            logs = log_total[mb * pairs + g]

            def tile_step(t, carry):
                acc_a, acc_b = carry
                keys = kv[0, t, :, lanes]
                values = kv[1, t, :, lanes]
                mask = live[t]
                scores = dot(keys, q2) + jnp.concatenate([mask, mask], 1)
                probs = jnp.exp(scores - logs)
                grad_probs = dot(values, g2)
                low = (probs * (grad_probs - delta)).astype(BF16)
                store(0, t, lanes, dot(low, q2_rows).astype(BF16))
                store(1, t, lanes, dot(probs.astype(BF16), g2_rows).astype(BF16))
                turned = keys.T
                acc_a = acc_a + dot(turned[:HDIM], low[:, :tok])
                acc_b = acc_b + dot(turned[HDIM:], low[:, tok:])
                return acc_a, acc_b

            acc_a, acc_b = lax.fori_loop(
                0,
                count,
                tile_step,
                (jnp.zeros((HDIM, tok), F32), jnp.zeros((HDIM, tok), F32)),
            )
            pair = jnp.concatenate([acc_a, acc_b], 0) * (HDIM**-0.5)
            grad_proj[tokens(mb), lanes] = pair.T.astype(BF16)

        loop(pairs, pair_step)

    def store_short(which, t, lanes, value):
        dkv_short[which, t, :, lanes] = value

    def store_long(which, t, lanes, value):
        dkv_long[which, t >> 1, t & 1, :, lanes] = value

    norm_one_back(SHORT)
    attend_back(SHORT, kv_short, live_short, short_span, store_short)
    short_grads = links.copy(dkv_short.at[:, 1 - side], got_short, 1)
    red_back.over_next()
    red_in.over_next()
    norm_one_back(LONG)
    attend_back(LONG, kv_long, live_long, long_span, store_long)
    long_grads = links.copy(dkv_long.at[:, :, 1 - core], got_core, 1)

    half_wide = wide // 2

    def out_step(j):
        lanes = aligned(j * half_wide, half_wide, half_wide)
        rows = aligned(j * col, col, col)
        part_query[rows, 0:col] = dot(mixed[...], grad_attn[:, lanes], 0, 0).astype(BF16)

    loop(2, out_step)

    short_grads.wait()
    for which in range(2):
        lanes = slice((1 + which) * col, (2 + which) * col)
        total = dkv_short[which, side].astype(F32) + got_short[which].astype(F32)
        grad_proj[tokens(SHORT), lanes] = total.astype(BF16)

    long_grads.wait()
    mine = (seq >> 1) & 3
    far_grads = []

    def add_far(j):
        for which in range(2):
            dkv_long[which, j, core] = (
                dkv_long[which, j, core].astype(F32) + got_core[which, j].astype(F32)
            ).astype(BF16)

    for d in (3, 1, 2):
        add_far(mine ^ d)
        far_grads.append(
            links.copy(dkv_long.at[:, mine ^ d, core], got_far.at[d - 1], 2 * d)
        )
    add_far(mine)

    def x_grad(part, lanes):
        def step(j):
            rows = aligned(j * 256, 256, 256)
            for mb_part, lanes_here, proj_here in part:
                mb_part[rows, lanes_here] = dot(xs_cols(rows), grad_proj[:, proj_here], 0, 0).astype(
                    BF16
                )

        loop(wide // 256, step)

    def xs_cols(rows):
        return jnp.concatenate([x[0, :, rows], x[1, :, rows]], 0)

    x_grad(((part_query, slice(col, 2 * col), slice(0, col)),), None)
    red_query.start()

    def input_part(mb):
        rows = tokens(mb)
        total = dot(grad_proj[rows, 0:col], qkvw[0], 1, 1)
        total = total + dot(grad_proj[rows, col : 2 * col], qkvw[1], 1, 1)
        total = total + dot(grad_proj[rows, 2 * col : 3 * col], qkvw[2], 1, 1)
        post_out[1, mb] = total.astype(BF16)
        posts[3, mb] = post(3, mb)

    def input_done(mb):
        posts[3, mb].wait()

        def step(r):
            rows = aligned(r * tile_rows, tile_rows, tile_rows)
            in_grad[mb, rows, :] = (grad_rows[mb, rows, :] + received(3, mb, rows)).astype(BF16)

        loop(tok // tile_rows, step)

    input_part(SHORT)
    red_back.over_far()
    red_in.over_far()
    red_query.over_next()

    for item in far_grads:
        item.wait()
    for which in range(2):
        lanes = slice((1 + which) * col, (2 + which) * col)
        total = dkv_long[which, mine, core].astype(F32)
        for d in range(3):
            total = total + got_far[d, which].astype(F32)
        grad_proj[tokens(LONG), lanes] = total.astype(BF16)
    x_grad(
        (
            (part_pair, slice(0, col), slice(col, 2 * col)),
            (part_pair, slice(col, 2 * col), slice(2 * col, 3 * col)),
        ),
        None,
    )
    red_pair.start()

    vec[7:8, 0:col] = jnp.sum(grad_proj[:, 0:col].astype(F32), axis=0, keepdims=True)
    vec[7:8, col : 2 * col] = jnp.sum(
        grad_proj[:, 2 * col : 3 * col].astype(F32), axis=0, keepdims=True
    )
    part_vec[...] = jnp.zeros_like(part_vec)
    row = 0
    lines = []
    for index, width in [(i, wide) for i in range(6)] + [(7, 2 * col), (6, ff)]:
        for k in range(width // 128):
            lines.append(vec[index : index + 1, k * 128 : k * 128 + 128])
    while len(lines) % 16:
        lines.append(jnp.zeros((1, 128), F32))
    part_vec[0 : len(lines), :] = jnp.concatenate(lines, 0).astype(BF16)
    red_vec.start()

    input_part(LONG)
    red_pair.over_next()
    red_vec.over_next()
    red_query.over_far()
    red_back.total()
    red_in.total()
    red_pair.over_far()
    red_vec.over_far()
    input_done(SHORT)
    input_done(LONG)
    red_query.total()
    red_back.back_next()
    red_in.back_next()
    red_pair.total()
    red_vec.total()
    red_query.back_next()
    red_back.back_core()
    red_in.back_core()
    red_pair.back_next()
    red_vec.back_next()
    red_query.back_core()
    red_pair.back_core()
    red_vec.back_core()
    for item in (red_back, red_in, red_query, red_pair, red_vec):
        item.finish()


def body(
    seq_count,
    inputs,
    qkv_weight,
    qv_bias,
    out_weight,
    out_bias,
    ln1_gain,
    ln1_bias,
    ffn_in,
    ffn_in_bias,
    ffn_out,
    ffn_out_bias,
    ln2_gain,
    ln2_bias,
    short_lengths,
    long_lengths,
    short_random,
    long_random,
    cotangent,
):
    tok, wide = inputs.shape[1:]
    col = qkv_weight.shape[2]
    ff = ffn_in.shape[1]
    pairs = col // (2 * HDIM)
    short_span = seq_count // short_lengths.shape[0]
    long_span = seq_count // long_lengths.shape[0]
    upper = max(0, seq_count.bit_length() - 5)

    def row(vector):
        return vector.reshape(1, -1)

    parts = [(ff, wide), (wide, ff), (wide, 2 * col), (wide, 2 * col), (VEC_ROWS, 128)]
    vmem = pltpu.VMEM
    scratch = [
        vmem((2, tok, wide), BF16),
        vmem((2, tok, wide), BF16),
        vmem((3, wide, col), BF16),
        vmem((col, wide), BF16),
        vmem((wide, ff), BF16),
        vmem((ff, wide), BF16),
        vmem((2, short_span, tok, col), BF16),
        vmem((2, long_span, tok, col), BF16),
        vmem((2, tok, col), BF16),
        vmem((2, col, tok), BF16),
        vmem((short_span, tok, tok), F32),
        vmem((long_span, tok, tok), F32),
        vmem((2, col, tok), F32),
        vmem((2 * tok, col), BF16),
        vmem((2 * pairs, 1, 2 * tok), F32),
        vmem((2, 2, tok, wide), BF16),
        vmem((2, 2, tok, wide), BF16),
        vmem((2, tok, wide), F32),
        vmem((2, tok, 128), F32),
        vmem((2 * tok, wide), BF16),
        vmem((2 * tok, ff), BF16),
        vmem((2, tok, ff), F32),
        vmem((2, tok, wide), F32),
        vmem((2 * tok, wide), BF16),
        vmem((2 * tok, ff), BF16),
        vmem((2 * tok, wide), BF16),
        vmem((tok, col), BF16),
        vmem((col, tok), F32),
        vmem((2, short_span, tok, col), BF16),
        vmem((2, long_span // 2, 2, tok, col), BF16),
        vmem((2, tok, col), BF16),
        vmem((2, long_span // 2, tok, col), BF16),
        vmem((long_span // 2 - 1, 2, tok, col), BF16),
        vmem((2 * tok, 3 * col), BF16),
    ]
    scratch += [vmem(shape, BF16) for shape in parts]
    scratch += [vmem((8, ff), F32)]
    scratch += [vmem((r // 2, w), BF16) for r, w in parts]
    scratch += [vmem((r // 4, w), BF16) for r, w in parts]
    scratch += [vmem((3, r // 16, w), BF16) for r, w in parts]
    if upper:
        scratch += [vmem((upper, r // 16, w), BF16) for r, w in parts]
    scratch += [
        pltpu.SemaphoreType.DMA((COPIES,)),
        pltpu.SemaphoreType.DMA((COPIES,)),
        pltpu.SemaphoreType.DMA((8,)),
        pltpu.SemaphoreType.DMA((8,)),
    ]
    any_spec = pl.BlockSpec(memory_space=pl.ANY)
    vmem_spec = pl.BlockSpec(memory_space=pltpu.VMEM)
    smem_spec = pl.BlockSpec(memory_space=pltpu.SMEM)
    out, in_grad, s_back, s_in, s_query, s_pair, s_vec = pl.pallas_call(
        functools.partial(kernel, seq_count),
        out_shape=[
            jax.ShapeDtypeStruct(inputs.shape, BF16),
            jax.ShapeDtypeStruct(inputs.shape, BF16),
        ]
        + [jax.ShapeDtypeStruct(shape, BF16) for shape in parts],
        in_specs=[any_spec] * 6 + [vmem_spec] * 8 + [smem_spec] * 4,
        out_specs=[vmem_spec] * 2 + [any_spec] * 5,
        scratch_shapes=scratch,
        compiler_params=pltpu.CompilerParams(
            collective_id=0, has_side_effects=True, vmem_limit_bytes=63 * 1024 * 1024
        ),
        cost_estimate=pl.CostEstimate(
            flops=12_000_000_000, bytes_accessed=40_000_000, transcendentals=8_000_000
        ),
        name="layer",
    )(
        inputs,
        cotangent,
        qkv_weight,
        out_weight,
        ffn_in,
        ffn_out,
        qv_bias,
        row(out_bias),
        row(ln1_gain),
        row(ln1_bias),
        row(ffn_in_bias),
        row(ffn_out_bias),
        row(ln2_gain),
        row(ln2_bias),
        short_lengths,
        long_lengths,
        short_random,
        long_random,
    )
    qkv_grad = jnp.stack([s_query[:, col:], s_pair[:, :col], s_pair[:, col:]]).astype(F32)
    out_grad = jnp.concatenate([s_query[:col, :col], s_query[col:, :col]], 1).astype(F32)
    flat = s_vec.astype(F32).reshape(-1)
    pieces = [flat[i * wide : (i + 1) * wide] for i in range(6)]
    qv_grad = flat[6 * wide : 6 * wide + 2 * col].reshape(2, col)
    inner_grad = flat[6 * wide + 2 * col : 6 * wide + 2 * col + ff]
    return (
        out,
        in_grad,
        qkv_grad,
        qv_grad,
        out_grad,
        pieces[0],
        pieces[1],
        pieces[2],
        s_in.astype(F32),
        inner_grad,
        s_back.astype(F32),
        pieces[3],
        pieces[4],
        pieces[5],
    )


def solution(mesh):
    return jax.shard_map(
        functools.partial(body, mesh.shape["seq"]),
        mesh=mesh,
        in_specs=(
            P(None, "seq", None),
            P(None, None, "head"),
            P(None, "head"),
            P("head", None),
            P(),
            P(),
            P(),
            P(None, "head"),
            P("head"),
            P("head", None),
            P(),
            P(),
            P(),
            P(),
            P(),
            P("seq", None),
            P("seq", None),
            P(None, "seq", None),
        ),
        out_specs=(
            P(None, "seq", None),
            P(None, "seq", None),
            P(None, None, "head"),
            P(None, "head"),
            P("head", None),
            P(),
            P(),
            P(),
            P(None, "head"),
            P("head"),
            P("head", None),
            P(),
            P(),
            P(),
        ),
        check_vma=False,
    )
```

```python
import functools
import math

import jax
import jax.numpy as jnp
from jax import lax
from jax.experimental import pallas as pl
from jax.experimental.pallas import tpu as pltpu
from jax.sharding import PartitionSpec as P

MESH = pl.DeviceIdType.MESH
F32 = jnp.float32
BF16 = jnp.bfloat16
EPSILON = 1e-06
NEGATIVE = -1000000000.0
HDIM = 64
BLK = 64
SHORT, LONG = 0, 1
ROOT = math.sqrt(2.0 / math.pi)
CUBIC = 0.044715
COPIES = 96
VEC_ROWS = 256


def dot(a, b, ca=1, cb=0):
    return lax.dot_general(a, b, (((ca,), (cb,)), ((), ())), preferred_element_type=F32)


def aligned(start, size, step):
    return pl.ds(pl.multiple_of(start, step), size)


def loop(count, step):
    def run(index, carry):
        step(index)
        return carry

    lax.fori_loop(0, count, run, 0)


class Links:
    def __init__(self, send_sem, recv_sem, seq, head):
        self.send_sem, self.recv_sem, self.seq, self.head = send_sem, recv_sem, seq, head
        self.used = 0

    def copy(self, src, dst, seq_delta=0, head_delta=0):
        index = self.used
        self.used += 1
        item = pltpu.make_async_remote_copy(
            src_ref=src,
            dst_ref=dst,
            send_sem=self.send_sem.at[index],
            recv_sem=self.recv_sem.at[index],
            device_id=(self.seq ^ seq_delta, self.head ^ head_delta),
            device_id_type=MESH,
        )
        item.start()
        return item


def add_rows(into, into_start, more, more_start, rows, tile):
    def step(i):
        a = aligned(into_start + i * tile, tile, 16)
        b = aligned(more_start + i * tile, tile, 16)
        into[a, :] = (into[a, :].astype(F32) + more[b, :].astype(F32)).astype(BF16)

    loop(rows // tile, step)


class Reduction:
    def __init__(self, links, part, out, got, deltas, up, upper, local_sem):
        self.links, self.part, self.out, self.got = links, part, out, got
        self.up, self.upper, self.local_sem = up, upper, local_sem
        self.deltas = deltas
        size = part.shape[0]
        self.tile = min(48, size // 16)
        start = 0
        self.levels = []
        got_at = 0
        for delta in deltas:
            size = size // 2
            upper_half = (links.seq >> (delta.bit_length() - 1)) & 1
            kept, away = start + upper_half * size, start + (1 - upper_half) * size
            self.levels.append((delta, size, start, kept, away, got_at))
            start = kept
            got_at += size
        self.share, self.share_at = size, start
        self.sent = []
        self.last = None

    def rows(self, ref, start, count):
        return ref.at[aligned(start, count, 16), :]

    def go(self, src, dst, delta):
        self.last = self.links.copy(src, dst, delta)
        self.sent.append(self.last)

    def add(self, start, got_start, rows):
        add_rows(self.part, start, self.got, got_start, rows, self.tile)

    def step(self, index):
        delta, size, start, kept, away, got_at = self.levels[index]
        if index:
            self.last.wait_recv()
            got_start = self.levels[index - 1][5]
            self.add(away, got_start + (away - start), size)
        self.go(self.rows(self.part, away, size), self.rows(self.got, got_at, size), delta)
        if index:
            self.add(kept, got_start + (kept - start), size)

    def total(self):
        self.last.wait_recv()
        self.add(self.share_at, self.levels[-1][5], self.share)
        mine = self.rows(self.part, self.share_at, self.share)
        for level, delta in enumerate(self.upper):
            item = self.links.copy(mine, self.up.at[level], delta)
            item.wait()
            add_rows(self.part, self.share_at, self.up.at[level], 0, self.share, self.tile)
        there = self.rows(self.out, self.share_at, self.share)
        self.go(mine, there, self.deltas[-1])
        self.kept = pltpu.make_async_copy(mine, there, self.local_sem)
        self.kept.start()

    def back(self, index):
        self.last.wait_recv()
        if index == len(self.levels) - 2:
            self.kept.wait()
        delta, size, start, kept, away, got_at = self.levels[index]
        block = self.rows(self.out, kept, size)
        self.go(block, block, delta)

    def finish(self):
        self.last.wait_recv()
        for item in self.sent:
            item.wait_send()


def kernel(
    seq_count,
    x_in,
    cot_in,
    qkvw_in,
    outw_in,
    win_in,
    wout_in,
    qv_bias,
    out_bias_in,
    gain_one_in,
    bias_one_in,
    back_bias_in,
    gain_two_in,
    bias_two_in,
    in_bias_in,
    short_len,
    long_len,
    short_table,
    long_table,
    out,
    in_grad,
    sum_back,
    sum_in,
    sum_query,
    sum_pair,
    sum_vec,
    x,
    cot,
    qkvw,
    outw,
    win,
    wout,
    params,
    kv_short,
    kv_long,
    q_cols,
    q_rows,
    live_short,
    live_long,
    mixed_cols,
    mixed,
    tops,
    totals,
    post_out,
    post_in,
    norm_one,
    root_one,
    hidden,
    act,
    slope,
    grad_rows,
    grad_feed,
    grad_inner,
    grad_attn,
    g_cols,
    g_rows,
    deltas,
    query_cols,
    dkv_short,
    dkv_long,
    got_short,
    got_core,
    got_far,
    grad_proj,
    part_back,
    part_in,
    part_query,
    part_pair,
    part_vec,
    vec,
    got_back,
    got_in,
    got_query,
    got_pair,
    got_vec,
    *rest,
):
    upper = [16 << i for i in range(max(0, seq_count.bit_length() - 5))]
    if upper:
        ups = rest[:5]
        rest = rest[5:]
    else:
        ups = (None,) * 5
    send_sem, recv_sem, load_sem, local_sem = rest
    seq, head = lax.axis_index("seq"), lax.axis_index("head")
    links = Links(send_sem, recv_sem, seq, head)
    tok = x.shape[1]
    wide = x.shape[2]
    col = qkvw.shape[2]
    ff = win.shape[1]
    pairs = col // (2 * HDIM)
    blocks = tok // BLK
    short_span = seq_count // short_len.shape[0]
    long_span = seq_count // long_len.shape[0]
    core = seq & 1

    peers = [1, 2, 4, 8] + upper
    barrier = pltpu.get_barrier_semaphore()
    for delta in peers:
        pl.semaphore_signal(barrier, inc=1, device_id=(seq ^ delta, head), device_id_type=MESH)
    pl.semaphore_signal(barrier, inc=1, device_id=(seq, head ^ 1), device_id_type=MESH)

    loads = []
    for i, (src, dst) in enumerate(
        ((x_in, x), (qkvw_in, qkvw), (outw_in, outw), (win_in, win), (wout_in, wout), (cot_in, cot))
    ):
        item = pltpu.make_async_copy(src, dst, load_sem.at[i])
        item.start()
        loads.append(item)

    vectors = (out_bias_in, gain_one_in, bias_one_in, back_bias_in, gain_two_in, bias_two_in)
    for i, vector in enumerate(vectors):
        params[i : i + 1, :wide] = vector[...].reshape(1, wide)
    params[6:7, :] = in_bias_in[...].reshape(1, ff)

    def param(index):
        return params[index : index + 1, :wide]

    OUTB, GAIN1, BIAS1, BACKB, GAIN2, BIAS2 = range(6)

    def tokens(mb):
        return pl.ds(mb * tok, tok)

    vec[...] = jnp.zeros_like(vec)
    loads[0].wait()
    loads[1].wait()

    def project(mb, c):
        return dot(x[mb], qkvw[c])

    place = seq & (long_span - 1)
    side = seq & (short_span - 1)
    kv_long[0, place] = project(LONG, 1).astype(BF16)
    kv_long[1, place] = (project(LONG, 2) + qv_bias[1:2, :]).astype(BF16)
    pl.semaphore_wait(barrier, len(peers) + 1)

    def block(which, spot):
        return kv_long.at[which, spot]

    key_next = links.copy(block(0, place), block(0, place), 2)
    value_far = links.copy(block(1, place), block(1, place), 4)
    value_next = links.copy(block(1, place), block(1, place), 2)
    key_far = links.copy(block(0, place), block(0, place), 4)
    long_core = links.copy(kv_long.at[:, place], kv_long.at[:, place], 1)
    kv_short[0, side] = project(SHORT, 1).astype(BF16)
    kv_short[1, side] = (project(SHORT, 2) + qv_bias[1:2, :]).astype(BF16)
    short_core = links.copy(kv_short.at[:, side], kv_short.at[:, side], 1)

    def spread_cols(pair):
        zero = jnp.zeros((HDIM, tok), BF16)
        return jnp.concatenate(
            [
                jnp.concatenate([pair[:HDIM], zero], 0),
                jnp.concatenate([zero, pair[HDIM:]], 0),
            ],
            1,
        )

    def spread_rows(pair):
        lane = lax.broadcasted_iota(jnp.int32, (tok, 128), 1)
        return jnp.concatenate(
            [jnp.where(lane < HDIM, pair, 0.0), jnp.where(lane < HDIM, 0.0, pair)], 0
        ).astype(BF16)

    for mb in (SHORT, LONG):
        query = (project(mb, 0) + qv_bias[0:1, :]).astype(BF16).astype(F32) * (HDIM**-0.5)
        for g in range(pairs):
            pair = query[:, g * 128 : g * 128 + 128]
            q_rows[mb, g] = spread_rows(pair)
            q_cols[mb, g] = spread_cols(pair.T.astype(BF16))

    def make_live(live, count, spot, table, length):
        lane_block = lax.broadcasted_iota(jnp.int32, (1, tok), 1) >> 6
        row_block = spot * blocks + lane_block
        picks = []
        for k in range(table.shape[1]):
            pick = jnp.full((1, tok), table[0, k], jnp.int32)
            for b in range(1, blocks):
                pick = jnp.where(lane_block == b, table[b, k], pick)
            picks.append(pick)

        def step(t):
            key = t * tok + lax.broadcasted_iota(jnp.int32, (tok, tok), 0)
            key_block = key >> 6
            allowed = (key_block < 2) | (row_block < 2) | (jnp.abs(row_block - key_block) <= 1)
            for pick in picks:
                allowed = allowed | (key_block == pick)
            live[t] = jnp.where(allowed & (key < length), 0.0, NEGATIVE)

        loop(count, step)

    make_live(live_short, short_span, side, short_table, short_len[seq // short_span])
    make_live(live_long, long_span, place, long_table, long_len[seq // long_span])

    def attend(mb, kv, live, spots, first=False):
        def pair_step(g):
            lanes = aligned(g * 128, 128, 128)
            q2 = q_cols[mb, g]
            index = mb * pairs + g
            scores = []
            for t in spots:
                mask = live[t]
                scores.append(dot(kv[0, t, :, lanes], q2) + jnp.concatenate([mask, mask], 1))
            top = functools.reduce(jnp.maximum, [jnp.max(s, axis=0, keepdims=True) for s in scores])
            if not first:
                old = tops[index]
                top = jnp.maximum(old, top)
            tops[index] = top
            total = 0.0
            acc_a = 0.0
            acc_b = 0.0
            for t, s in zip(spots, scores):
                weights = jnp.exp(s - top)
                total = total + jnp.sum(weights, axis=0, keepdims=True)
                low = weights.astype(BF16)
                turned = kv[1, t, :, lanes].T
                acc_a = acc_a + dot(turned[:HDIM], low[:, :tok])
                acc_b = acc_b + dot(turned[HDIM:], low[:, tok:])
            rows_a = aligned(g * 128, HDIM, HDIM)
            rows_b = aligned(g * 128 + HDIM, HDIM, HDIM)
            if not first:
                scale = jnp.exp(old - top)
                total = total + totals[index] * scale
                acc_a = acc_a + mixed_cols[mb, rows_a, :] * scale[:, :tok]
                acc_b = acc_b + mixed_cols[mb, rows_b, :] * scale[:, tok:]
            totals[index] = total
            mixed_cols[mb, rows_a, :] = acc_a
            mixed_cols[mb, rows_b, :] = acc_b

        loop(pairs, pair_step)

    def post(stage, mb):
        buf = stage % 2
        return links.copy(post_out.at[buf, mb], post_in.at[buf, mb], 0, 1)

    def received(stage, mb, rows):
        buf = stage % 2
        return post_out[buf, mb, rows, :].astype(F32) + post_in[buf, mb, rows, :].astype(F32)

    posts = {}

    def attention_out(mb):
        for g in range(pairs):
            index = mb * pairs + g
            lanes = slice(g * 128, g * 128 + 128)
            total = totals[index]
            inverse = 1.0 / total
            pair = jnp.concatenate(
                [
                    mixed_cols[mb, g * 128 : g * 128 + HDIM, :] * inverse[:, :tok],
                    mixed_cols[mb, g * 128 + HDIM : g * 128 + 128, :] * inverse[:, tok:],
                ],
                0,
            )
            mixed_cols[mb, lanes, :] = pair
            mixed[tokens(mb), lanes] = pair.T.astype(BF16)
            tops[index] = tops[index] + jnp.log(total)
        post_out[0, mb] = dot(mixed[tokens(mb), :], outw[...]).astype(BF16)
        posts[0, mb] = post(0, mb)

    short_core.wait()
    attend(SHORT, kv_short, live_short, tuple(range(short_span)), True)
    loads[2].wait()
    attention_out(SHORT)

    key_next.wait_recv()
    key_corner = links.copy(block(0, place ^ 2), block(0, place ^ 2), 4)
    value_far.wait_recv()
    value_corner = links.copy(block(1, place ^ 4), block(1, place ^ 4), 2)
    long_core.wait()
    attend(LONG, kv_long, live_long, (place, place ^ 1), True)
    value_next.wait_recv()
    pass_next = links.copy(kv_long.at[:, place ^ 2], kv_long.at[:, place ^ 2], 1)
    key_far.wait_recv()
    pass_far = links.copy(kv_long.at[:, place ^ 4], kv_long.at[:, place ^ 4], 1)
    attend(LONG, kv_long, live_long, (place ^ 2, place ^ 4))
    pass_next.wait_recv()
    pass_far.wait_recv()
    attend(LONG, kv_long, live_long, (place ^ 3, place ^ 5))
    key_corner.wait_recv()
    value_corner.wait_recv()
    pass_corner = links.copy(kv_long.at[:, place ^ 6], kv_long.at[:, place ^ 6], 1)
    attend(LONG, kv_long, live_long, (place ^ 6,))
    pass_corner.wait_recv()
    attend(LONG, kv_long, live_long, (place ^ 7,))
    attention_out(LONG)
    for item in (
        key_next, value_far, value_next, key_far, key_corner, value_corner,
        pass_next, pass_far, pass_corner,
    ):
        item.wait_send()

    def mean(value):
        return jnp.sum(value, axis=-1, keepdims=True) * (1.0 / wide)

    def vec_add(index, value):
        vec[index : index + 1, :wide] += jnp.sum(value, axis=0, keepdims=True)

    tile_rows = 64

    def feed_forward(mb):
        posts[0, mb].wait()

        def norm_step(r):
            rows = aligned(r * tile_rows, tile_rows, tile_rows)
            joined = received(0, mb, rows) + param(OUTB) + x[mb, rows, :].astype(F32)
            centred = joined - mean(joined)
            root = lax.rsqrt(mean(centred * centred) + EPSILON)
            normed = centred * root
            norm_one[mb, rows, :] = normed
            root_one[mb, rows, :] = jnp.broadcast_to(root, (tile_rows, 128))
            all_rows = aligned(mb * tok + r * tile_rows, tile_rows, tile_rows)
            hidden[all_rows, :] = (normed * param(GAIN1) + param(BIAS1)).astype(BF16)

        loop(tok // tile_rows, norm_step)

        def col_step(j):
            lanes = aligned(j * 512, 512, 512)
            u = dot(hidden[tokens(mb), :], win[:, lanes]) + params[6:7, lanes]
            square = u * u
            t = jnp.tanh(ROOT * u * (1.0 + CUBIC * square))
            half = 0.5 * (1.0 + t)
            act[tokens(mb), lanes] = (u * half).astype(BF16)
            slope[mb, :, lanes] = half + (0.5 * ROOT) * u * (1.0 - t * t) * (
                1.0 + (3.0 * CUBIC) * square
            )

        loop(ff // 512, col_step)
        post_out[1, mb] = dot(act[tokens(mb), :], wout[...]).astype(BF16)
        posts[1, mb] = post(1, mb)

    loads[3].wait()
    loads[4].wait()
    loads[5].wait()
    feed_forward(SHORT)
    feed_forward(LONG)

    def norm_back(grad, normed, root):
        return root * (grad - mean(grad) - normed * mean(grad * normed))

    def feed_norm(mb):
        posts[1, mb].wait()

        def norm_step(r):
            rows = aligned(r * tile_rows, tile_rows, tile_rows)
            all_rows = aligned(mb * tok + r * tile_rows, tile_rows, tile_rows)
            hid = norm_one[mb, rows, :] * param(GAIN1) + param(BIAS1)
            second = received(1, mb, rows) + param(BACKB) + hid
            centred = second - mean(second)
            root = lax.rsqrt(mean(centred * centred) + EPSILON)
            normed = centred * root
            out[mb, rows, :] = (normed * param(GAIN2) + param(BIAS2)).astype(BF16)
            g = cot[mb, rows, :].astype(F32)
            vec_add(GAIN2, g * normed)
            vec_add(BIAS2, g)
            grad = norm_back(g * param(GAIN2), normed, root)
            vec_add(BACKB, grad)
            grad_rows[mb, rows, :] = grad
            grad_feed[all_rows, :] = grad.astype(BF16)

        loop(tok // tile_rows, norm_step)

    def feed_back(mb):
        def col_step(j):
            lanes = aligned(j * 512, 512, 512)
            grad_act = dot(grad_feed[tokens(mb), :], wout[lanes, :], 1, 1).astype(BF16)
            low = (grad_act.astype(F32) * slope[mb, :, lanes]).astype(BF16)
            grad_inner[tokens(mb), lanes] = low
            vec[6:7, lanes] += jnp.sum(low.astype(F32), axis=0, keepdims=True)

        loop(ff // 512, col_step)
        post_out[0, mb] = dot(grad_inner[tokens(mb), :], win[...], 1, 1).astype(BF16)
        posts[2, mb] = post(2, mb)

    feed_norm(SHORT)
    feed_back(SHORT)

    def reduction(index, part, total, got, order):
        return Reduction(links, part, total, got, order, ups[index], upper, local_sem.at[index])

    near_first, far_first = (1, 2, 4, 8), (1, 4, 8, 2)
    red_back = reduction(0, part_back, sum_back, got_back, near_first)
    red_in = reduction(1, part_in, sum_in, got_in, near_first)
    red_query = reduction(2, part_query, sum_query, got_query, far_first)
    red_pair = reduction(3, part_pair, sum_pair, got_pair, near_first)
    red_vec = reduction(4, part_vec, sum_vec, got_vec, near_first)

    feed_norm(LONG)

    def back_step(j):
        rows = aligned(j * 256, 256, 256)
        part_back[rows, :] = dot(act[:, rows], grad_feed[...], 0, 0).astype(BF16)

    loop(ff // 256, back_step)
    red_back.step(0)
    feed_back(LONG)

    def in_step(j):
        rows = aligned(j * 256, 256, 256)
        part_in[rows, :] = dot(hidden[:, rows], grad_inner[...], 0, 0).astype(BF16)

    red_back.step(1)
    loop(wide // 256, in_step)
    red_in.step(0)

    def norm_one_back(mb):
        posts[2, mb].wait()

        def norm_step(r):
            rows = aligned(r * tile_rows, tile_rows, tile_rows)
            all_rows = aligned(mb * tok + r * tile_rows, tile_rows, tile_rows)
            grad = grad_rows[mb, rows, :] + received(2, mb, rows)
            normed = norm_one[mb, rows, :]
            vec_add(GAIN1, grad * normed)
            vec_add(BIAS1, grad)
            joined = norm_back(grad * param(GAIN1), normed, root_one[mb, rows, :1])
            vec_add(OUTB, joined)
            grad_rows[mb, rows, :] = joined
            grad_attn[all_rows, :] = joined.astype(BF16)

        loop(tok // tile_rows, norm_step)
        low = dot(grad_attn[tokens(mb), :], outw[...], 1, 1).astype(BF16).astype(F32)
        for g in range(pairs):
            pair = low[:, g * 128 : g * 128 + 128]
            turned = pair.T
            g_rows[g] = spread_rows(pair)
            g_cols[g] = spread_cols(turned.astype(BF16))
            product = turned * mixed_cols[mb, g * 128 : g * 128 + 128, :]
            deltas[g] = jnp.concatenate(
                [
                    jnp.sum(product[:HDIM], axis=0, keepdims=True),
                    jnp.sum(product[HDIM:], axis=0, keepdims=True),
                ],
                1,
            )

    def attend_back(mb, kv, live, t, store, first=False):
        def pair_step(g):
            lanes = aligned(g * 128, 128, 128)
            keys = kv[0, t, :, lanes]
            values = kv[1, t, :, lanes]
            mask = live[t]
            scores = dot(keys, q_cols[mb, g]) + jnp.concatenate([mask, mask], 1)
            probs = jnp.exp(scores - tops[mb * pairs + g])
            grad_probs = dot(values, g_cols[g])
            low = (probs * (grad_probs - deltas[g])).astype(BF16)
            store(0, lanes, dot(low, q_rows[mb, g]).astype(BF16))
            store(1, lanes, dot(probs.astype(BF16), g_rows[g]).astype(BF16))
            turned = keys.T
            rows_a = aligned(g * 128, HDIM, HDIM)
            rows_b = aligned(g * 128 + HDIM, HDIM, HDIM)
            acc_a = dot(turned[:HDIM], low[:, :tok])
            acc_b = dot(turned[HDIM:], low[:, tok:])
            if not first:
                acc_a = acc_a + query_cols[rows_a, :]
                acc_b = acc_b + query_cols[rows_b, :]
            query_cols[rows_a, :] = acc_a
            query_cols[rows_b, :] = acc_b

        loop(pairs, pair_step)

    def query_done(mb):
        for g in range(pairs):
            lanes = slice(g * 128, g * 128 + 128)
            grad_proj[tokens(mb), lanes] = (query_cols[lanes, :] * (HDIM**-0.5)).T.astype(BF16)

    def store_short(t):
        def store(which, lanes, value):
            dkv_short[which, t, :, lanes] = value

        return store

    def store_long(j, c):
        def store(which, lanes, value):
            dkv_long[which, j, c, :, lanes] = value

        return store

    norm_one_back(SHORT)
    attend_back(SHORT, kv_short, live_short, 1 - side, store_short(1 - side), True)
    short_grads = links.copy(dkv_short.at[:, 1 - side], got_short, 1)
    attend_back(SHORT, kv_short, live_short, side, store_short(side))
    query_done(SHORT)
    red_in.step(1)
    red_back.step(2)
    norm_one_back(LONG)
    mine = (seq >> 1) & 3

    def add_block(which, j, more):
        dkv_long[which, j, core] = (
            dkv_long[which, j, core].astype(F32) + more[...].astype(F32)
        ).astype(BF16)

    def go_far(which, j, slot, delta):
        return links.copy(dkv_long.at[which, j, core], got_far.at[slot], delta)

    core_grads = []
    key_hop = []
    value_hop = []
    for order, d in enumerate((3, 1, 2, 0)):
        j = mine ^ d
        attend_back(LONG, kv_long, live_long, 2 * j + 1 - core, store_long(j, 1 - core), order == 0)
        item = links.copy(dkv_long.at[:, j, 1 - core], got_core.at[:, j], 1)
        core_grads.append(item)
        attend_back(LONG, kv_long, live_long, 2 * j + core, store_long(j, core))
        item.wait_recv()
        for which in range(2):
            add_block(which, j, got_core.at[which, j])
        if d == 1:
            key_hop = [go_far(0, mine ^ 3, 0, 2), go_far(0, mine ^ 1, 1, 2)]
        if d == 2:
            value_hop = [go_far(1, mine ^ 3, 2, 4), go_far(1, mine ^ 2, 3, 4)]
    query_done(LONG)
    key_hop[0].wait_recv()
    add_block(0, mine ^ 2, got_far.at[0])
    key_hop.append(go_far(0, mine ^ 2, 4, 4))
    value_hop[0].wait_recv()
    add_block(1, mine ^ 1, got_far.at[2])
    value_hop.append(go_far(1, mine ^ 1, 5, 2))

    half_wide = wide // 2

    def out_step(j):
        lanes = aligned(j * half_wide, half_wide, half_wide)
        rows = aligned(j * col, col, col)
        part_query[rows, 0:col] = dot(mixed[...], grad_attn[:, lanes], 0, 0).astype(BF16)

    loop(2, out_step)

    def x_grad(items):
        def step(j):
            rows = aligned(j * 256, 256, 256)
            columns = jnp.concatenate([x[0, :, rows], x[1, :, rows]], 0)
            for part, lanes, source in items:
                part[rows, lanes] = dot(columns, grad_proj[:, source], 0, 0).astype(BF16)

        loop(wide // 256, step)

    x_grad([(part_query, slice(col, 2 * col), slice(0, col))])
    red_query.step(0)

    short_grads.wait()
    for which in range(2):
        lanes = slice((1 + which) * col, (2 + which) * col)
        total = dkv_short[which, side].astype(F32) + got_short[which].astype(F32)
        grad_proj[tokens(SHORT), lanes] = total.astype(BF16)

    def input_part(mb):
        rows = tokens(mb)
        total = dot(grad_proj[rows, 0:col], qkvw[0], 1, 1)
        total = total + dot(grad_proj[rows, col : 2 * col], qkvw[1], 1, 1)
        total = total + dot(grad_proj[rows, 2 * col : 3 * col], qkvw[2], 1, 1)
        post_out[1, mb] = total.astype(BF16)
        posts[3, mb] = post(3, mb)

    def input_done(mb):
        posts[3, mb].wait()

        def step(r):
            rows = aligned(r * tile_rows, tile_rows, tile_rows)
            in_grad[mb, rows, :] = (grad_rows[mb, rows, :] + received(3, mb, rows)).astype(BF16)

        loop(tok // tile_rows, step)

    input_part(SHORT)
    red_in.step(2)
    red_back.step(3)
    red_query.step(1)

    for hop, which in ((key_hop, 0), (value_hop, 1)):
        lanes = slice((1 + which) * col, (2 + which) * col)
        hop[1].wait_recv()
        hop[2].wait_recv()
        total = dkv_long[which, mine, core].astype(F32) + got_far[2 * which + 1].astype(F32)
        total = total + got_far[4 + which].astype(F32)
        grad_proj[tokens(LONG), lanes] = total.astype(BF16)
    x_grad(
        [
            (part_pair, slice(0, col), slice(col, 2 * col)),
            (part_pair, slice(col, 2 * col), slice(2 * col, 3 * col)),
        ]
    )
    red_pair.step(0)

    vec[7:8, 0:col] = jnp.sum(grad_proj[:, 0:col].astype(F32), axis=0, keepdims=True)
    vec[7:8, col : 2 * col] = jnp.sum(
        grad_proj[:, 2 * col : 3 * col].astype(F32), axis=0, keepdims=True
    )
    part_vec[...] = jnp.zeros_like(part_vec)
    lines = []
    for index, width in [(i, wide) for i in range(6)] + [(7, 2 * col), (6, ff)]:
        for k in range(width // 128):
            lines.append(vec[index : index + 1, k * 128 : k * 128 + 128])
    while len(lines) % 16:
        lines.append(jnp.zeros((1, 128), F32))
    part_vec[0 : len(lines), :] = jnp.concatenate(lines, 0).astype(BF16)
    red_vec.step(0)
    input_part(LONG)

    red_back.total()
    red_pair.step(1)
    red_vec.step(1)
    red_in.step(3)
    red_query.step(2)
    red_back.back(2)
    input_done(SHORT)
    red_in.total()
    red_pair.step(2)
    red_vec.step(2)
    red_query.step(3)
    red_back.back(1)
    red_in.back(2)
    red_pair.step(3)
    red_vec.step(3)
    red_query.total()
    red_in.back(1)
    red_pair.total()
    red_vec.total()
    red_query.back(2)
    input_done(LONG)
    red_pair.back(2)
    red_vec.back(2)
    red_back.back(0)
    red_query.back(1)
    red_pair.back(1)
    red_vec.back(1)
    red_in.back(0)
    red_query.back(0)
    red_pair.back(0)
    red_vec.back(0)
    for item in (red_back, red_in, red_query, red_pair, red_vec):
        item.finish()
    for item in core_grads + key_hop + value_hop:
        item.wait_send()


def widen(back, inner, query, out_low, out_high, pair, vec, out_in, grad_in, *outs):
    out, in_grad, g_back, g_inner, g_qkv, g_out, g_qv, g_in_bias, *vectors = outs
    col = query.shape[1]
    wide = vectors[0].shape[0]
    out[...] = out_in[...]
    in_grad[...] = grad_in[...]
    g_back[...] = back[...].astype(F32)
    g_inner[...] = inner[...].astype(F32)
    g_qkv[0] = query[...].astype(F32)
    g_qkv[1] = pair[:, :col].astype(F32)
    g_qkv[2] = pair[:, col:].astype(F32)
    g_out[:, :col] = out_low[...].astype(F32)
    g_out[:, col:] = out_high[...].astype(F32)

    @pl.when(pl.program_id(0) == 0)
    def _():
        full = vec[...].astype(F32)

        def line(row, count):
            return jnp.concatenate([full[r : r + 1, :] for r in range(row, row + count)], 1)

        per = wide // 128
        for i, vector in enumerate(vectors):
            vector[...] = line(i * per, per).reshape(wide)
        row = len(vectors) * per
        g_qv[...] = jnp.concatenate(
            [line(row, col // 128), line(row + col // 128, col // 128)], 0
        )
        g_in_bias[...] = line(row + 2 * col // 128, g_in_bias.shape[0] // 128).reshape(
            g_in_bias.shape[0]
        )


def body(
    seq_count,
    inputs,
    qkv_weight,
    qv_bias,
    out_weight,
    out_bias,
    ln1_gain,
    ln1_bias,
    ffn_in,
    ffn_in_bias,
    ffn_out,
    ffn_out_bias,
    ln2_gain,
    ln2_bias,
    short_lengths,
    long_lengths,
    short_random,
    long_random,
    cotangent,
):
    tok, wide = inputs.shape[1:]
    col = qkv_weight.shape[2]
    ff = ffn_in.shape[1]
    pairs = col // (2 * HDIM)
    short_span = seq_count // short_lengths.shape[0]
    long_span = seq_count // long_lengths.shape[0]
    upper = max(0, seq_count.bit_length() - 5)

    parts = [(ff, wide), (wide, ff), (wide, 2 * col), (wide, 2 * col), (VEC_ROWS, 128)]
    vmem = pltpu.VMEM
    scratch = [
        vmem((2, tok, wide), BF16),
        vmem((2, tok, wide), BF16),
        vmem((3, wide, col), BF16),
        vmem((col, wide), BF16),
        vmem((wide, ff), BF16),
        vmem((ff, wide), BF16),
        vmem((8, ff), F32),
        vmem((2, short_span, tok, col), BF16),
        vmem((2, long_span, tok, col), BF16),
        vmem((2, pairs, 128, 2 * tok), BF16),
        vmem((2, pairs, 2 * tok, 128), BF16),
        vmem((short_span, tok, tok), F32),
        vmem((long_span, tok, tok), F32),
        vmem((2, col, tok), F32),
        vmem((2 * tok, col), BF16),
        vmem((2 * pairs, 1, 2 * tok), F32),
        vmem((2 * pairs, 1, 2 * tok), F32),
        vmem((2, 2, tok, wide), BF16),
        vmem((2, 2, tok, wide), BF16),
        vmem((2, tok, wide), F32),
        vmem((2, tok, 128), F32),
        vmem((2 * tok, wide), BF16),
        vmem((2 * tok, ff), BF16),
        vmem((2, tok, ff), F32),
        vmem((2, tok, wide), F32),
        vmem((2 * tok, wide), BF16),
        vmem((2 * tok, ff), BF16),
        vmem((2 * tok, wide), BF16),
        vmem((pairs, 128, 2 * tok), BF16),
        vmem((pairs, 2 * tok, 128), BF16),
        vmem((pairs, 1, 2 * tok), F32),
        vmem((col, tok), F32),
        vmem((2, short_span, tok, col), BF16),
        vmem((2, long_span // 2, 2, tok, col), BF16),
        vmem((2, tok, col), BF16),
        vmem((2, long_span // 2, tok, col), BF16),
        vmem((6, tok, col), BF16),
        vmem((2 * tok, 3 * col), BF16),
    ]
    scratch += [vmem(shape, BF16) for shape in parts]
    scratch += [vmem((8, ff), F32)]
    scratch += [vmem((r - r // 16, w), BF16) for r, w in parts]
    if upper:
        scratch += [vmem((upper, r // 16, w), BF16) for r, w in parts]
    scratch += [
        pltpu.SemaphoreType.DMA((COPIES,)),
        pltpu.SemaphoreType.DMA((COPIES,)),
        pltpu.SemaphoreType.DMA((8,)),
        pltpu.SemaphoreType.DMA((8,)),
    ]
    any_spec = pl.BlockSpec(memory_space=pl.ANY)
    vmem_spec = pl.BlockSpec(memory_space=pltpu.VMEM)
    smem_spec = pl.BlockSpec(memory_space=pltpu.SMEM)
    out, in_grad, s_back, s_in, s_query, s_pair, s_vec = pl.pallas_call(
        functools.partial(kernel, seq_count),
        out_shape=[
            jax.ShapeDtypeStruct(inputs.shape, BF16),
            jax.ShapeDtypeStruct(inputs.shape, BF16),
        ]
        + [jax.ShapeDtypeStruct(shape, BF16) for shape in parts],
        in_specs=[any_spec] * 6 + [vmem_spec] * 8 + [smem_spec] * 4,
        out_specs=[vmem_spec] * 2 + [any_spec] * 5,
        scratch_shapes=scratch,
        compiler_params=pltpu.CompilerParams(
            collective_id=0, has_side_effects=True, vmem_limit_bytes=63 * 1024 * 1024
        ),
        cost_estimate=pl.CostEstimate(
            flops=12_000_000_000, bytes_accessed=40_000_000, transcendentals=8_000_000
        ),
        name="layer",
    )(
        inputs,
        cotangent,
        qkv_weight,
        out_weight,
        ffn_in,
        ffn_out,
        qv_bias,
        out_bias,
        ln1_gain,
        ln1_bias,
        ffn_out_bias,
        ln2_gain,
        ln2_bias,
        ffn_in_bias,
        short_lengths,
        long_lengths,
        short_random,
        long_random,
    )
    steps = 8
    vector = jax.ShapeDtypeStruct((wide,), F32)
    whole = pl.BlockSpec(memory_space=pltpu.VMEM)
    rows_spec = pl.BlockSpec((2, tok // steps, wide), lambda i: (0, i, 0))
    out, in_grad, g_back, g_inner, g_qkv, g_out, g_qv, g_in_bias, *vectors = pl.pallas_call(
        widen,
        grid=(steps,),
        out_shape=[
            jax.ShapeDtypeStruct(inputs.shape, BF16),
            jax.ShapeDtypeStruct(inputs.shape, BF16),
            jax.ShapeDtypeStruct((ff, wide), F32),
            jax.ShapeDtypeStruct((wide, ff), F32),
            jax.ShapeDtypeStruct((3, wide, col), F32),
            jax.ShapeDtypeStruct((col, wide), F32),
            jax.ShapeDtypeStruct((2, col), F32),
            jax.ShapeDtypeStruct((ff,), F32),
        ]
        + [vector] * 6,
        in_specs=[
            pl.BlockSpec((ff // steps, wide), lambda i: (i, 0)),
            pl.BlockSpec((wide // steps, ff), lambda i: (i, 0)),
            pl.BlockSpec((wide // steps, col), lambda i: (i, 1)),
            pl.BlockSpec((col // steps, col), lambda i: (i, 0)),
            pl.BlockSpec((col // steps, col), lambda i: (i + steps, 0)),
            pl.BlockSpec((wide // steps, 2 * col), lambda i: (i, 0)),
            whole,
            rows_spec,
            rows_spec,
        ],
        out_specs=[
            rows_spec,
            rows_spec,
            pl.BlockSpec((ff // steps, wide), lambda i: (i, 0)),
            pl.BlockSpec((wide // steps, ff), lambda i: (i, 0)),
            pl.BlockSpec((3, wide // steps, col), lambda i: (0, i, 0)),
            pl.BlockSpec((col // steps, wide), lambda i: (i, 0)),
        ]
        + [whole] * 8,
        compiler_params=pltpu.CompilerParams(vmem_limit_bytes=63 * 1024 * 1024),
        name="widen",
    )(s_back, s_in, s_query, s_query, s_query, s_pair, s_vec, out, in_grad)
    return (
        out,
        in_grad,
        g_qkv,
        g_qv,
        g_out,
        vectors[0],
        vectors[1],
        vectors[2],
        g_inner,
        g_in_bias,
        g_back,
        vectors[3],
        vectors[4],
        vectors[5],
    )


def solution(mesh):
    return jax.shard_map(
        functools.partial(body, mesh.shape["seq"]),
        mesh=mesh,
        in_specs=(
            P(None, "seq", None),
            P(None, None, "head"),
            P(None, "head"),
            P("head", None),
            P(),
            P(),
            P(),
            P(None, "head"),
            P("head"),
            P("head", None),
            P(),
            P(),
            P(),
            P(),
            P(),
            P("seq", None),
            P("seq", None),
            P(None, "seq", None),
        ),
        out_specs=(
            P(None, "seq", None),
            P(None, "seq", None),
            P(None, None, "head"),
            P(None, "head"),
            P("head", None),
            P(),
            P(),
            P(),
            P(None, "head"),
            P("head"),
            P("head", None),
            P(),
            P(),
            P(),
        ),
        check_vma=False,
    )
```

```python
import functools
import math

import jax
import jax.numpy as jnp
from jax import lax
from jax.experimental import pallas as pl
from jax.experimental.pallas import tpu as pltpu
from jax.sharding import PartitionSpec as P

MESH = pl.DeviceIdType.MESH
F32 = jnp.float32
BF16 = jnp.bfloat16
EPSILON = 1e-06
NEGATIVE = -1000000000.0
HDIM = 64
BLK = 64
SHORT, LONG = 0, 1
ROOT = math.sqrt(2.0 / math.pi)
CUBIC = 0.044715
COPIES = 112
TAIL = (
    *("feed_long", "post_long", "back_b", "b0", "in_d", "d0", "in_c", "b1", "back_a", "d1"),
    *("c0", "c1", "post_short", "norm_long", "a0", "long3", "d2", "b2", "long1", "long2"),
    *("long0", "b3", "a1", "norm_short", "short_back", "c2", "d3", "query_e", "bt", "hop"),
    *("e0", "e1", "c3", "a2", "short_done", "long_done", "part_short", "br2", "pair_f", "part_long"),
    *("ct", "f0", "vec_v", "a3", "v0", "e2", "v1", "f1", "cr2", "v2"),
    *("e3", "br1", "v3", "f2", "cr1", "vt", "at", "done_long", "et", "vr2"),
    *("f3", "ar2", "cr0", "er2", "vr1", "dt", "ft", "ar1", "done_short", "dr2"),
    *("er1", "fr2", "dr1", "fr1", "br0", "er0", "ar0", "dr0", "fr0", "vr0"),
)
VEC_ROWS = 256


def dot(a, b, ca=1, cb=0):
    return lax.dot_general(a, b, (((ca,), (cb,)), ((), ())), preferred_element_type=F32)


def aligned(start, size, step):
    return pl.ds(pl.multiple_of(start, step), size)


def loop(count, step):
    def run(index, carry):
        step(index)
        return carry

    lax.fori_loop(0, count, run, 0)


class Links:
    def __init__(self, send_sem, recv_sem, seq, head):
        self.send_sem, self.recv_sem, self.seq, self.head = send_sem, recv_sem, seq, head
        self.used = 0

    def copy(self, src, dst, seq_delta=0, head_delta=0):
        index = self.used
        self.used += 1
        item = pltpu.make_async_remote_copy(
            src_ref=src,
            dst_ref=dst,
            send_sem=self.send_sem.at[index],
            recv_sem=self.recv_sem.at[index],
            device_id=(self.seq ^ seq_delta, self.head ^ head_delta),
            device_id_type=MESH,
        )
        item.start()
        return item


def add_rows(into, into_start, more, more_start, rows, tile):
    def step(i):
        a = aligned(into_start + i * tile, tile, 16)
        b = aligned(more_start + i * tile, tile, 16)
        into[a, :] = (into[a, :].astype(F32) + more[b, :].astype(F32)).astype(BF16)

    loop(rows // tile, step)


class Reduction:
    def __init__(self, links, part, out, got, deltas, up, upper, local_sem):
        self.links, self.part, self.out, self.got = links, part, out, got
        self.up, self.upper, self.local_sem = up, upper, local_sem
        self.deltas = deltas
        size = part.shape[0]
        self.tile = min(48, size // 16)
        start = 0
        self.levels = []
        got_at = 0
        for delta in deltas:
            size = size // 2
            upper_half = (links.seq >> (delta.bit_length() - 1)) & 1
            kept, away = start + upper_half * size, start + (1 - upper_half) * size
            self.levels.append((delta, size, start, kept, away, got_at))
            start = kept
            got_at += size
        self.share, self.share_at = size, start
        self.sent = []
        self.last = None

    def rows(self, ref, start, count):
        return ref.at[aligned(start, count, 16), :]

    def go(self, src, dst, delta):
        self.last = self.links.copy(src, dst, delta)
        self.sent.append(self.last)

    def add(self, start, got_start, rows):
        add_rows(self.part, start, self.got, got_start, rows, self.tile)

    def step(self, index):
        delta, size, start, kept, away, got_at = self.levels[index]
        if index:
            self.last.wait_recv()
            got_start = self.levels[index - 1][5]
            self.add(away, got_start + (away - start), size)
        self.go(self.rows(self.part, away, size), self.rows(self.got, got_at, size), delta)
        if index:
            self.add(kept, got_start + (kept - start), size)

    def total(self):
        self.last.wait_recv()
        self.add(self.share_at, self.levels[-1][5], self.share)
        mine = self.rows(self.part, self.share_at, self.share)
        for level, delta in enumerate(self.upper):
            item = self.links.copy(mine, self.up.at[level], delta)
            item.wait()
            add_rows(self.part, self.share_at, self.up.at[level], 0, self.share, self.tile)
        there = self.rows(self.out, self.share_at, self.share)
        self.go(mine, there, self.deltas[-1])
        self.kept = pltpu.make_async_copy(mine, there, self.local_sem)
        self.kept.start()

    def back(self, index):
        self.last.wait_recv()
        if index == len(self.levels) - 2:
            self.kept.wait()
        delta, size, start, kept, away, got_at = self.levels[index]
        block = self.rows(self.out, kept, size)
        self.go(block, block, delta)

    def finish(self):
        self.last.wait_recv()
        for item in self.sent:
            item.wait_send()


def kernel(
    seq_count,
    x_in,
    cot_in,
    qkvw_in,
    outw_in,
    win_in,
    wout_in,
    qv_bias,
    out_bias_in,
    gain_one_in,
    bias_one_in,
    back_bias_in,
    gain_two_in,
    bias_two_in,
    in_bias_in,
    short_len_in,
    long_len_in,
    short_table_in,
    long_table_in,
    out_in,
    in_grad_in,
    sum_back_a,
    sum_back_b,
    sum_in_a,
    sum_in_b,
    sum_query,
    sum_pair,
    sum_vec,
    short_len,
    long_len,
    short_table,
    long_table,
    out,
    in_grad,
    x,
    cot,
    qkvw,
    outw,
    win,
    wout,
    params,
    kv_short,
    kv_long,
    q_cols,
    q_rows,
    live_short,
    live_long,
    mixed_cols,
    mixed,
    tops,
    totals,
    post_out,
    post_in,
    norm_one,
    root_one,
    hidden,
    act,
    slope,
    grad_rows,
    grad_feed,
    grad_inner,
    grad_attn,
    g_cols,
    g_rows,
    deltas,
    query_cols,
    dkv_short,
    dkv_long,
    got_short,
    got_core,
    got_far,
    grad_proj,
    part_back_a,
    part_back_b,
    part_in_a,
    part_in_b,
    part_query,
    part_pair,
    part_vec,
    vec,
    got_back_a,
    got_back_b,
    got_in_a,
    got_in_b,
    got_query,
    got_pair,
    got_vec,
    *rest,
):
    upper = [16 << i for i in range(max(0, seq_count.bit_length() - 5))]
    if upper:
        ups = rest[:7]
        rest = rest[7:]
    else:
        ups = (None,) * 7
    send_sem, recv_sem, load_sem, local_sem = rest
    seq, head = lax.axis_index("seq"), lax.axis_index("head")
    links = Links(send_sem, recv_sem, seq, head)
    tok = x.shape[1]
    wide = x.shape[2]
    col = qkvw.shape[2]
    ff = win.shape[1]
    pairs = col // (2 * HDIM)
    blocks = tok // BLK
    short_span = seq_count // short_len.shape[0]
    long_span = seq_count // long_len.shape[0]
    core = seq & 1

    peers = [1, 2, 4, 8] + upper
    barrier = pltpu.get_barrier_semaphore()
    for delta in peers:
        pl.semaphore_signal(barrier, inc=1, device_id=(seq ^ delta, head), device_id_type=MESH)
    pl.semaphore_signal(barrier, inc=1, device_id=(seq, head ^ 1), device_id_type=MESH)

    loads = []
    for i, (src, dst) in enumerate(
        (
            (x_in, x),
            (qkvw_in, qkvw),
            (short_len_in, short_len),
            (long_len_in, long_len),
            (short_table_in, short_table),
            (long_table_in, long_table),
            (outw_in, outw),
            (win_in, win),
            (wout_in, wout),
            (cot_in, cot),
        )
    ):
        loads.append(pltpu.make_async_copy(src, dst, load_sem.at[i]))
    for item in loads[:6]:
        item.start()

    def param(index):
        return params[index : index + 1, :wide]

    OUTB, GAIN1, BIAS1, BACKB, GAIN2, BIAS2 = range(6)

    def tokens(mb):
        return pl.ds(mb * tok, tok)

    loads[0].wait()
    loads[1].wait()

    def project(mb, c):
        return dot(x[mb], qkvw[c])

    place = seq & (long_span - 1)
    side = seq & (short_span - 1)
    def spread_cols(pair):
        zero = jnp.zeros((HDIM, tok), BF16)
        return jnp.concatenate(
            [
                jnp.concatenate([pair[:HDIM], zero], 0),
                jnp.concatenate([zero, pair[HDIM:]], 0),
            ],
            1,
        )

    def spread_rows(pair):
        lane = lax.broadcasted_iota(jnp.int32, (tok, 128), 1)
        return jnp.concatenate(
            [jnp.where(lane < HDIM, pair, 0.0), jnp.where(lane < HDIM, 0.0, pair)], 0
        ).astype(BF16)

    def queries(mb):
        query = (project(mb, 0) + qv_bias[0:1, :]).astype(BF16).astype(F32) * (HDIM**-0.5)
        for g in range(pairs):
            pair = query[:, g * 128 : g * 128 + 128]
            q_rows[mb, g] = spread_rows(pair)
            q_cols[mb, g] = spread_cols(pair.T.astype(BF16))

    def make_live(live, count, spot, table, length):
        lane_block = lax.broadcasted_iota(jnp.int32, (1, tok), 1) >> 6
        row_block = spot * blocks + lane_block
        picks = []
        for k in range(table.shape[1]):
            pick = jnp.full((1, tok), table[0, k], jnp.int32)
            for b in range(1, blocks):
                pick = jnp.where(lane_block == b, table[b, k], pick)
            picks.append(pick)

        def step(t):
            key = t * tok + lax.broadcasted_iota(jnp.int32, (tok, tok), 0)
            key_block = key >> 6
            allowed = (key_block < 2) | (row_block < 2) | (jnp.abs(row_block - key_block) <= 1)
            for pick in picks:
                allowed = allowed | (key_block == pick)
            live[t] = jnp.where(allowed & (key < length), 0.0, NEGATIVE)

        loop(count, step)

    kv_long[0, place] = project(LONG, 1).astype(BF16)
    kv_long[1, place] = (project(LONG, 2) + qv_bias[1:2, :]).astype(BF16)
    kv_short[0, side] = project(SHORT, 1).astype(BF16)
    kv_short[1, side] = (project(SHORT, 2) + qv_bias[1:2, :]).astype(BF16)
    queries(SHORT)
    for item in loads[2:6]:
        item.wait()
    make_live(live_short, short_span, side, short_table, short_len[seq // short_span])
    queries(LONG)

    def block(which, spot):
        return kv_long.at[which, spot]

    pl.semaphore_wait(barrier, len(peers) + 1)
    key_next = links.copy(block(0, place), block(0, place), 2)
    value_far = links.copy(block(1, place), block(1, place), 4)
    short_core = links.copy(kv_short.at[:, side], kv_short.at[:, side], 1)
    long_core = links.copy(kv_long.at[:, place], kv_long.at[:, place], 1)
    value_next = links.copy(block(1, place), block(1, place), 2)
    key_far = links.copy(block(0, place), block(0, place), 4)
    for item in loads[6:]:
        item.start()

    def attend(mb, kv, live, spots, first=False):
        def pair_step(g):
            lanes = aligned(g * 128, 128, 128)
            q2 = q_cols[mb, g]
            index = mb * pairs + g
            scores = []
            for t in spots:
                mask = live[t]
                scores.append(dot(kv[0, t, :, lanes], q2) + jnp.concatenate([mask, mask], 1))
            top = functools.reduce(jnp.maximum, [jnp.max(s, axis=0, keepdims=True) for s in scores])
            if not first:
                old = tops[index]
                top = jnp.maximum(old, top)
            tops[index] = top
            total = 0.0
            acc_a = 0.0
            acc_b = 0.0
            for t, s in zip(spots, scores):
                weights = jnp.exp(s - top)
                total = total + jnp.sum(weights, axis=0, keepdims=True)
                low = weights.astype(BF16)
                turned = kv[1, t, :, lanes].T
                acc_a = acc_a + dot(turned[:HDIM], low[:, :tok])
                acc_b = acc_b + dot(turned[HDIM:], low[:, tok:])
            rows_a = aligned(g * 128, HDIM, HDIM)
            rows_b = aligned(g * 128 + HDIM, HDIM, HDIM)
            if not first:
                scale = jnp.exp(old - top)
                total = total + totals[index] * scale
                acc_a = acc_a + mixed_cols[mb, rows_a, :] * scale[:, :tok]
                acc_b = acc_b + mixed_cols[mb, rows_b, :] * scale[:, tok:]
            totals[index] = total
            mixed_cols[mb, rows_a, :] = acc_a
            mixed_cols[mb, rows_b, :] = acc_b

        loop(pairs, pair_step)

    def post(stage, mb):
        buf = stage % 2
        return links.copy(post_out.at[buf, mb], post_in.at[buf, mb], 0, 1)

    def received(stage, mb, rows):
        buf = stage % 2
        return post_out[buf, mb, rows, :].astype(F32) + post_in[buf, mb, rows, :].astype(F32)

    posts = {}
    stores = []

    def store(src, dst):
        item = pltpu.make_async_copy(src, dst, load_sem.at[len(loads) + len(stores)])
        item.start()
        stores.append(item)

    def attention_out(mb):
        for g in range(pairs):
            index = mb * pairs + g
            lanes = slice(g * 128, g * 128 + 128)
            total = totals[index]
            inverse = 1.0 / total
            pair = jnp.concatenate(
                [
                    mixed_cols[mb, g * 128 : g * 128 + HDIM, :] * inverse[:, :tok],
                    mixed_cols[mb, g * 128 + HDIM : g * 128 + 128, :] * inverse[:, tok:],
                ],
                0,
            )
            mixed_cols[mb, lanes, :] = pair
            mixed[tokens(mb), lanes] = pair.T.astype(BF16)
            tops[index] = tops[index] + jnp.log(total)
        post_out[0, mb] = dot(mixed[tokens(mb), :], outw[...]).astype(BF16)
        posts[0, mb] = post(0, mb)

    short_core.wait()
    attend(SHORT, kv_short, live_short, tuple(range(short_span)), True)
    loads[6].wait()
    attention_out(SHORT)

    make_live(live_long, long_span, place, long_table, long_len[seq // long_span])
    vec[...] = jnp.zeros_like(vec)
    vectors = (out_bias_in, gain_one_in, bias_one_in, back_bias_in, gain_two_in, bias_two_in)
    for i, vector in enumerate(vectors):
        params[i : i + 1, :wide] = vector[...].reshape(1, wide)
    params[6:7, :] = in_bias_in[...].reshape(1, ff)

    key_next.wait_recv()
    key_corner = links.copy(block(0, place ^ 2), block(0, place ^ 2), 4)
    value_far.wait_recv()
    value_corner = links.copy(block(1, place ^ 4), block(1, place ^ 4), 2)
    long_core.wait()
    attend(LONG, kv_long, live_long, (place, place ^ 1), True)
    value_next.wait_recv()
    pass_next = links.copy(kv_long.at[:, place ^ 2], kv_long.at[:, place ^ 2], 1)
    key_far.wait_recv()
    pass_far = links.copy(kv_long.at[:, place ^ 4], kv_long.at[:, place ^ 4], 1)
    attend(LONG, kv_long, live_long, (place ^ 2, place ^ 4))
    pass_next.wait_recv()
    pass_far.wait_recv()
    attend(LONG, kv_long, live_long, (place ^ 3, place ^ 5))

    def mean(value):
        return jnp.sum(value, axis=-1, keepdims=True) * (1.0 / wide)

    def vec_add(index, value):
        vec[index : index + 1, :wide] += jnp.sum(value, axis=0, keepdims=True)

    tile_rows = 64

    def feed_forward(mb):
        posts[0, mb].wait_recv()
        if mb == SHORT:
            posts[0, mb].wait_send()

        def norm_step(r):
            rows = aligned(r * tile_rows, tile_rows, tile_rows)
            joined = received(0, mb, rows) + param(OUTB) + x[mb, rows, :].astype(F32)
            centred = joined - mean(joined)
            root = lax.rsqrt(mean(centred * centred) + EPSILON)
            normed = centred * root
            norm_one[mb, rows, :] = normed
            root_one[mb, rows, :] = jnp.broadcast_to(root, (tile_rows, 128))
            all_rows = aligned(mb * tok + r * tile_rows, tile_rows, tile_rows)
            hidden[all_rows, :] = (normed * param(GAIN1) + param(BIAS1)).astype(BF16)

        loop(tok // tile_rows, norm_step)

        def col_step(j):
            lanes = aligned(j * 512, 512, 512)
            u = dot(hidden[tokens(mb), :], win[:, lanes]) + params[6:7, lanes]
            square = u * u
            t = jnp.tanh(ROOT * u * (1.0 + CUBIC * square))
            half = 0.5 * (1.0 + t)
            act[tokens(mb), lanes] = (u * half).astype(BF16)
            slope[mb, :, lanes] = half + (0.5 * ROOT) * u * (1.0 - t * t) * (
                1.0 + (3.0 * CUBIC) * square
            )

        loop(ff // 512, col_step)
        post_out[1, mb] = dot(act[tokens(mb), :], wout[...]).astype(BF16)

    key_corner.wait_recv()
    value_corner.wait_recv()
    pass_corner = links.copy(kv_long.at[:, place ^ 6], kv_long.at[:, place ^ 6], 1)
    attend(LONG, kv_long, live_long, (place ^ 6,))
    pass_corner.wait_recv()
    attend(LONG, kv_long, live_long, (place ^ 7,))
    attention_out(LONG)
    for item in (
        key_next, value_far, value_next, key_far, key_corner, value_corner,
        pass_next, pass_far, pass_corner,
    ):
        item.wait_send()
    for item in loads[7:]:
        item.wait()
    feed_forward(SHORT)
    posts[0, LONG].wait_send()
    posts[1, SHORT] = post(1, SHORT)
    feed_forward(LONG)
    posts[1, LONG] = post(1, LONG)

    def norm_back(grad, normed, root):
        return root * (grad - mean(grad) - normed * mean(grad * normed))

    def feed_norm(mb):
        posts[1, mb].wait()

        def norm_step(r):
            rows = aligned(r * tile_rows, tile_rows, tile_rows)
            all_rows = aligned(mb * tok + r * tile_rows, tile_rows, tile_rows)
            hid = norm_one[mb, rows, :] * param(GAIN1) + param(BIAS1)
            second = received(1, mb, rows) + param(BACKB) + hid
            centred = second - mean(second)
            root = lax.rsqrt(mean(centred * centred) + EPSILON)
            normed = centred * root
            out[mb, rows, :] = (normed * param(GAIN2) + param(BIAS2)).astype(BF16)
            g = cot[mb, rows, :].astype(F32)
            vec_add(GAIN2, g * normed)
            vec_add(BIAS2, g)
            grad = norm_back(g * param(GAIN2), normed, root)
            vec_add(BACKB, grad)
            grad_rows[mb, rows, :] = grad
            grad_feed[all_rows, :] = grad.astype(BF16)

        loop(tok // tile_rows, norm_step)
        store(out.at[mb], out_in.at[mb])

    def feed_back(mb):
        def col_step(j):
            lanes = aligned(j * 512, 512, 512)
            grad_act = dot(grad_feed[tokens(mb), :], wout[lanes, :], 1, 1).astype(BF16)
            low = (grad_act.astype(F32) * slope[mb, :, lanes]).astype(BF16)
            grad_inner[tokens(mb), lanes] = low
            vec[6:7, lanes] += jnp.sum(low.astype(F32), axis=0, keepdims=True)

        loop(ff // 512, col_step)
        post_out[0, mb] = dot(grad_inner[tokens(mb), :], win[...], 1, 1).astype(BF16)

    feed_norm(SHORT)
    feed_back(SHORT)

    feed_norm(LONG)

    def reduction(index, part, total, got, order):
        return Reduction(links, part, total, got, order, ups[index], upper, local_sem.at[index])

    near_first, far_first = (1, 2, 4, 8), (1, 4, 8, 2)
    red = {
        "a": reduction(0, part_back_a, sum_back_a, got_back_a, near_first),
        "b": reduction(1, part_back_b, sum_back_b, got_back_b, near_first),
        "c": reduction(2, part_in_a, sum_in_a, got_in_a, near_first),
        "d": reduction(3, part_in_b, sum_in_b, got_in_b, far_first),
        "e": reduction(4, part_query, sum_query, got_query, near_first),
        "f": reduction(5, part_pair, sum_pair, got_pair, near_first),
        "v": reduction(6, part_vec, sum_vec, got_vec, near_first),
    }

    def back_grad(part, start):
        def step(j):
            rows = aligned(j * 256, 256, 256)
            lanes = aligned(start + j * 256, 256, 256)
            part[rows, :] = dot(act[:, lanes], grad_feed[...], 0, 0).astype(BF16)

        loop(ff // 512, step)

    def in_grad_half(part, start):
        def step(j):
            rows = aligned(j * 256, 256, 256)
            inner = grad_inner[:, start : start + ff // 2]
            part[rows, :] = dot(hidden[:, rows], inner, 0, 0).astype(BF16)

        loop(wide // 256, step)

    def norm_one_back(mb):
        posts[2, mb].wait()

        def norm_step(r):
            rows = aligned(r * tile_rows, tile_rows, tile_rows)
            all_rows = aligned(mb * tok + r * tile_rows, tile_rows, tile_rows)
            grad = grad_rows[mb, rows, :] + received(2, mb, rows)
            normed = norm_one[mb, rows, :]
            vec_add(GAIN1, grad * normed)
            vec_add(BIAS1, grad)
            joined = norm_back(grad * param(GAIN1), normed, root_one[mb, rows, :1])
            vec_add(OUTB, joined)
            grad_rows[mb, rows, :] = joined
            grad_attn[all_rows, :] = joined.astype(BF16)

        loop(tok // tile_rows, norm_step)
        low = dot(grad_attn[tokens(mb), :], outw[...], 1, 1).astype(BF16).astype(F32)
        for g in range(pairs):
            pair = low[:, g * 128 : g * 128 + 128]
            turned = pair.T
            g_rows[g] = spread_rows(pair)
            g_cols[g] = spread_cols(turned.astype(BF16))
            product = turned * mixed_cols[mb, g * 128 : g * 128 + 128, :]
            deltas[g] = jnp.concatenate(
                [
                    jnp.sum(product[:HDIM], axis=0, keepdims=True),
                    jnp.sum(product[HDIM:], axis=0, keepdims=True),
                ],
                1,
            )

    def attend_back(mb, kv, live, t, store, first=False):
        def pair_step(g):
            lanes = aligned(g * 128, 128, 128)
            keys = kv[0, t, :, lanes]
            values = kv[1, t, :, lanes]
            mask = live[t]
            scores = dot(keys, q_cols[mb, g]) + jnp.concatenate([mask, mask], 1)
            probs = jnp.exp(scores - tops[mb * pairs + g])
            grad_probs = dot(values, g_cols[g])
            low = (probs * (grad_probs - deltas[g])).astype(BF16)
            store(0, lanes, dot(low, q_rows[mb, g]).astype(BF16))
            store(1, lanes, dot(probs.astype(BF16), g_rows[g]).astype(BF16))
            turned = keys.T
            rows_a = aligned(g * 128, HDIM, HDIM)
            rows_b = aligned(g * 128 + HDIM, HDIM, HDIM)
            acc_a = dot(turned[:HDIM], low[:, :tok])
            acc_b = dot(turned[HDIM:], low[:, tok:])
            if not first:
                acc_a = acc_a + query_cols[rows_a, :]
                acc_b = acc_b + query_cols[rows_b, :]
            query_cols[rows_a, :] = acc_a
            query_cols[rows_b, :] = acc_b

        loop(pairs, pair_step)

    def query_done(mb):
        for g in range(pairs):
            lanes = slice(g * 128, g * 128 + 128)
            grad_proj[tokens(mb), lanes] = (query_cols[lanes, :] * (HDIM**-0.5)).T.astype(BF16)

    def store_short(t):
        def store(which, lanes, value):
            dkv_short[which, t, :, lanes] = value

        return store

    def store_long(j, c):
        def store(which, lanes, value):
            dkv_long[which, j, c, :, lanes] = value

        return store

    mine = (seq >> 1) & 3

    def add_block(which, j, more):
        dkv_long[which, j, core] = (
            dkv_long[which, j, core].astype(F32) + more[...].astype(F32)
        ).astype(BF16)

    def go_far(which, j, slot, delta):
        return links.copy(dkv_long.at[which, j, core], got_far.at[slot], delta)

    core_grads = []
    key_hop = []
    value_hop = []

    def long_back(d):
        j = mine ^ d
        attend_back(LONG, kv_long, live_long, 2 * j + 1 - core, store_long(j, 1 - core), d == 3)
        item = links.copy(dkv_long.at[:, j, 1 - core], got_core.at[:, j], 1)
        core_grads.append(item)
        attend_back(LONG, kv_long, live_long, 2 * j + core, store_long(j, core))
        item.wait_recv()
        for which in range(2):
            add_block(which, j, got_core.at[which, j])
        if d == 1:
            key_hop.extend([go_far(0, mine ^ 3, 0, 2), go_far(0, mine ^ 1, 1, 2)])
        if d == 2:
            value_hop.extend([go_far(1, mine ^ 3, 2, 4), go_far(1, mine ^ 2, 3, 4)])
        if d == 0:
            query_done(LONG)

    def second_hop():
        key_hop[0].wait_recv()
        add_block(0, mine ^ 2, got_far.at[0])
        key_hop.append(go_far(0, mine ^ 2, 4, 4))
        value_hop[0].wait_recv()
        add_block(1, mine ^ 1, got_far.at[2])
        value_hop.append(go_far(1, mine ^ 1, 5, 2))

    half_wide = wide // 2

    def out_step(j):
        lanes = aligned(j * half_wide, half_wide, half_wide)
        rows = aligned(j * col, col, col)
        part_query[rows, 0:col] = dot(mixed[...], grad_attn[:, lanes], 0, 0).astype(BF16)

    def x_grad(items):
        def step(j):
            rows = aligned(j * 256, 256, 256)
            columns = jnp.concatenate([x[0, :, rows], x[1, :, rows]], 0)
            for part, lanes, source in items:
                part[rows, lanes] = dot(columns, grad_proj[:, source], 0, 0).astype(BF16)

        loop(wide // 256, step)

    def input_part(mb):
        rows = tokens(mb)
        total = dot(grad_proj[rows, 0:col], qkvw[0], 1, 1)
        total = total + dot(grad_proj[rows, col : 2 * col], qkvw[1], 1, 1)
        total = total + dot(grad_proj[rows, 2 * col : 3 * col], qkvw[2], 1, 1)
        post_out[1, mb] = total.astype(BF16)
        posts[3, mb] = post(3, mb)

    def input_done(mb):
        posts[3, mb].wait()

        def step(r):
            rows = aligned(r * tile_rows, tile_rows, tile_rows)
            in_grad[mb, rows, :] = (grad_rows[mb, rows, :] + received(3, mb, rows)).astype(BF16)

        loop(tok // tile_rows, step)
        store(in_grad.at[mb], in_grad_in.at[mb])

    short_grads = []

    def short_back():
        attend_back(SHORT, kv_short, live_short, 1 - side, store_short(1 - side), True)
        short_grads.append(links.copy(dkv_short.at[:, 1 - side], got_short, 1))
        attend_back(SHORT, kv_short, live_short, side, store_short(side))
        query_done(SHORT)

    def query_grad():
        loop(2, out_step)
        x_grad([(part_query, slice(col, 2 * col), slice(0, col))])

    def short_done():
        short_grads[0].wait()
        for which in range(2):
            lanes = slice((1 + which) * col, (2 + which) * col)
            total = dkv_short[which, side].astype(F32) + got_short[which].astype(F32)
            grad_proj[tokens(SHORT), lanes] = total.astype(BF16)

    def long_done():
        for hop, which in ((key_hop, 0), (value_hop, 1)):
            lanes = slice((1 + which) * col, (2 + which) * col)
            hop[1].wait_recv()
            hop[2].wait_recv()
            total = dkv_long[which, mine, core].astype(F32) + got_far[2 * which + 1].astype(F32)
            total = total + got_far[4 + which].astype(F32)
            grad_proj[tokens(LONG), lanes] = total.astype(BF16)

    def pair_grad():
        x_grad(
            [
                (part_pair, slice(0, col), slice(col, 2 * col)),
                (part_pair, slice(col, 2 * col), slice(2 * col, 3 * col)),
            ]
        )

    def vectors_done():
        vec[7:8, 0:col] = jnp.sum(grad_proj[:, 0:col].astype(F32), axis=0, keepdims=True)
        vec[7:8, col : 2 * col] = jnp.sum(
            grad_proj[:, 2 * col : 3 * col].astype(F32), axis=0, keepdims=True
        )
        part_vec[...] = jnp.zeros_like(part_vec)
        lines = []
        for index, width in [(i, wide) for i in range(6)] + [(7, 2 * col), (6, ff)]:
            for k in range(width // 128):
                lines.append(vec[index : index + 1, k * 128 : k * 128 + 128])
        while len(lines) % 16:
            lines.append(jnp.zeros((1, 128), F32))
        part_vec[0 : len(lines), :] = jnp.concatenate(lines, 0).astype(BF16)

    def post_now(stage, mb):
        posts[stage, mb] = post(stage, mb)

    steps = {
        "back_a": lambda: back_grad(part_back_a, 0),
        "back_b": lambda: back_grad(part_back_b, ff // 2),
        "feed_long": lambda: feed_back(LONG),
        "post_long": lambda: post_now(2, LONG),
        "in_c": lambda: in_grad_half(part_in_a, 0),
        "in_d": lambda: in_grad_half(part_in_b, ff // 2),
        "norm_long": lambda: norm_one_back(LONG),
        "post_short": lambda: post_now(2, SHORT),
        "long3": lambda: long_back(3),
        "long1": lambda: long_back(1),
        "long2": lambda: long_back(2),
        "long0": lambda: long_back(0),
        "hop": second_hop,
        "norm_short": lambda: norm_one_back(SHORT),
        "short_back": short_back,
        "query_e": query_grad,
        "short_done": short_done,
        "part_short": lambda: input_part(SHORT),
        "long_done": long_done,
        "pair_f": pair_grad,
        "vec_v": vectors_done,
        "part_long": lambda: input_part(LONG),
        "done_short": lambda: input_done(SHORT),
        "done_long": lambda: input_done(LONG),
    }
    for name, item in red.items():
        for i in range(4):
            steps[name + str(i)] = functools.partial(item.step, i)
        steps[name + "t"] = item.total
        for i in range(3):
            steps[name + "r" + str(i)] = functools.partial(item.back, i)
    for name in TAIL:
        steps[name]()
    for item in red.values():
        item.finish()
    for item in core_grads + key_hop + value_hop:
        item.wait_send()
    for item in stores:
        item.wait()


def widen(back_a, back_b, inner_a, inner_b, query, out_low, out_high, pair, vec, out_in, grad_in, *outs):
    out, in_grad, g_back, g_inner, g_qkv, g_out, g_qv, g_in_bias, *vectors = outs
    col = query.shape[1]
    wide = vectors[0].shape[0]
    out[...] = out_in[...]
    in_grad[...] = grad_in[...]
    g_back[0] = back_a[...].astype(F32)
    g_back[1] = back_b[...].astype(F32)
    half = inner_a.shape[1]
    g_inner[:, :half] = inner_a[...].astype(F32)
    g_inner[:, half:] = inner_b[...].astype(F32)
    g_qkv[0] = query[...].astype(F32)
    g_qkv[1] = pair[:, :col].astype(F32)
    g_qkv[2] = pair[:, col:].astype(F32)
    g_out[:, :col] = out_low[...].astype(F32)
    g_out[:, col:] = out_high[...].astype(F32)

    @pl.when(pl.program_id(0) == 0)
    def _():
        full = vec[...].astype(F32)

        def line(row, count):
            return jnp.concatenate([full[r : r + 1, :] for r in range(row, row + count)], 1)

        per = wide // 128
        for i, vector in enumerate(vectors):
            vector[...] = line(i * per, per).reshape(wide)
        row = len(vectors) * per
        g_qv[...] = jnp.concatenate(
            [line(row, col // 128), line(row + col // 128, col // 128)], 0
        )
        g_in_bias[...] = line(row + 2 * col // 128, g_in_bias.shape[0] // 128).reshape(
            g_in_bias.shape[0]
        )


def body(
    seq_count,
    inputs,
    qkv_weight,
    qv_bias,
    out_weight,
    out_bias,
    ln1_gain,
    ln1_bias,
    ffn_in,
    ffn_in_bias,
    ffn_out,
    ffn_out_bias,
    ln2_gain,
    ln2_bias,
    short_lengths,
    long_lengths,
    short_random,
    long_random,
    cotangent,
):
    tok, wide = inputs.shape[1:]
    col = qkv_weight.shape[2]
    ff = ffn_in.shape[1]
    pairs = col // (2 * HDIM)
    short_span = seq_count // short_lengths.shape[0]
    long_span = seq_count // long_lengths.shape[0]
    upper = max(0, seq_count.bit_length() - 5)

    parts = [(ff // 2, wide)] * 2 + [(wide, ff // 2)] * 2 + [(wide, 2 * col)] * 2 + [(VEC_ROWS, 128)]
    vmem = pltpu.VMEM
    scratch = [
        pltpu.SMEM(short_lengths.shape, jnp.int32),
        pltpu.SMEM(long_lengths.shape, jnp.int32),
        pltpu.SMEM(short_random.shape, jnp.int32),
        pltpu.SMEM(long_random.shape, jnp.int32),
        vmem((2, tok, wide), BF16),
        vmem((2, tok, wide), BF16),
        vmem((2, tok, wide), BF16),
        vmem((2, tok, wide), BF16),
        vmem((3, wide, col), BF16),
        vmem((col, wide), BF16),
        vmem((wide, ff), BF16),
        vmem((ff, wide), BF16),
        vmem((8, ff), F32),
        vmem((2, short_span, tok, col), BF16),
        vmem((2, long_span, tok, col), BF16),
        vmem((2, pairs, 128, 2 * tok), BF16),
        vmem((2, pairs, 2 * tok, 128), BF16),
        vmem((short_span, tok, tok), F32),
        vmem((long_span, tok, tok), F32),
        vmem((2, col, tok), F32),
        vmem((2 * tok, col), BF16),
        vmem((2 * pairs, 1, 2 * tok), F32),
        vmem((2 * pairs, 1, 2 * tok), F32),
        vmem((2, 2, tok, wide), BF16),
        vmem((2, 2, tok, wide), BF16),
        vmem((2, tok, wide), F32),
        vmem((2, tok, 128), F32),
        vmem((2 * tok, wide), BF16),
        vmem((2 * tok, ff), BF16),
        vmem((2, tok, ff), F32),
        vmem((2, tok, wide), F32),
        vmem((2 * tok, wide), BF16),
        vmem((2 * tok, ff), BF16),
        vmem((2 * tok, wide), BF16),
        vmem((pairs, 128, 2 * tok), BF16),
        vmem((pairs, 2 * tok, 128), BF16),
        vmem((pairs, 1, 2 * tok), F32),
        vmem((col, tok), F32),
        vmem((2, short_span, tok, col), BF16),
        vmem((2, long_span // 2, 2, tok, col), BF16),
        vmem((2, tok, col), BF16),
        vmem((2, long_span // 2, tok, col), BF16),
        vmem((6, tok, col), BF16),
        vmem((2 * tok, 3 * col), BF16),
    ]
    scratch += [vmem(shape, BF16) for shape in parts]
    scratch += [vmem((8, ff), F32)]
    scratch += [vmem((r - r // 16, w), BF16) for r, w in parts]
    if upper:
        scratch += [vmem((upper, r // 16, w), BF16) for r, w in parts]
    scratch += [
        pltpu.SemaphoreType.DMA((COPIES,)),
        pltpu.SemaphoreType.DMA((COPIES,)),
        pltpu.SemaphoreType.DMA((16,)),
        pltpu.SemaphoreType.DMA((8,)),
    ]
    any_spec = pl.BlockSpec(memory_space=pl.ANY)
    vmem_spec = pl.BlockSpec(memory_space=pltpu.VMEM)
    out, in_grad, s_back_a, s_back_b, s_in_a, s_in_b, s_query, s_pair, s_vec = pl.pallas_call(
        functools.partial(kernel, seq_count),
        out_shape=[
            jax.ShapeDtypeStruct(inputs.shape, BF16),
            jax.ShapeDtypeStruct(inputs.shape, BF16),
        ]
        + [jax.ShapeDtypeStruct(shape, BF16) for shape in parts],
        in_specs=[any_spec] * 6 + [vmem_spec] * 8 + [any_spec] * 4,
        out_specs=[any_spec] * 9,
        scratch_shapes=scratch,
        compiler_params=pltpu.CompilerParams(
            collective_id=0, has_side_effects=True, vmem_limit_bytes=63 * 1024 * 1024
        ),
        cost_estimate=pl.CostEstimate(
            flops=12_000_000_000, bytes_accessed=40_000_000, transcendentals=8_000_000
        ),
        name="layer",
    )(
        inputs,
        cotangent,
        qkv_weight,
        out_weight,
        ffn_in,
        ffn_out,
        qv_bias,
        out_bias,
        ln1_gain,
        ln1_bias,
        ffn_out_bias,
        ln2_gain,
        ln2_bias,
        ffn_in_bias,
        short_lengths,
        long_lengths,
        short_random,
        long_random,
    )
    steps = 8
    vector = jax.ShapeDtypeStruct((wide,), F32)
    whole = pl.BlockSpec(memory_space=pltpu.VMEM)
    rows_spec = pl.BlockSpec((2, tok // steps, wide), lambda i: (0, i, 0))
    out, in_grad, g_back, g_inner, g_qkv, g_out, g_qv, g_in_bias, *vectors = pl.pallas_call(
        widen,
        grid=(steps,),
        out_shape=[
            jax.ShapeDtypeStruct(inputs.shape, BF16),
            jax.ShapeDtypeStruct(inputs.shape, BF16),
            jax.ShapeDtypeStruct((2, ff // 2, wide), F32),
            jax.ShapeDtypeStruct((wide, ff), F32),
            jax.ShapeDtypeStruct((3, wide, col), F32),
            jax.ShapeDtypeStruct((col, wide), F32),
            jax.ShapeDtypeStruct((2, col), F32),
            jax.ShapeDtypeStruct((ff,), F32),
        ]
        + [vector] * 6,
        in_specs=[
            pl.BlockSpec((ff // 2 // steps, wide), lambda i: (i, 0)),
            pl.BlockSpec((ff // 2 // steps, wide), lambda i: (i, 0)),
            pl.BlockSpec((wide // steps, ff // 2), lambda i: (i, 0)),
            pl.BlockSpec((wide // steps, ff // 2), lambda i: (i, 0)),
            pl.BlockSpec((wide // steps, col), lambda i: (i, 1)),
            pl.BlockSpec((col // steps, col), lambda i: (i, 0)),
            pl.BlockSpec((col // steps, col), lambda i: (i + steps, 0)),
            pl.BlockSpec((wide // steps, 2 * col), lambda i: (i, 0)),
            whole,
            rows_spec,
            rows_spec,
        ],
        out_specs=[
            rows_spec,
            rows_spec,
            pl.BlockSpec((2, ff // 2 // steps, wide), lambda i: (0, i, 0)),
            pl.BlockSpec((wide // steps, ff), lambda i: (i, 0)),
            pl.BlockSpec((3, wide // steps, col), lambda i: (0, i, 0)),
            pl.BlockSpec((col // steps, wide), lambda i: (i, 0)),
        ]
        + [whole] * 8,
        compiler_params=pltpu.CompilerParams(vmem_limit_bytes=63 * 1024 * 1024),
        name="widen",
    )(s_back_a, s_back_b, s_in_a, s_in_b, s_query, s_query, s_query, s_pair, s_vec, out, in_grad)
    return (
        out,
        in_grad,
        g_qkv,
        g_qv,
        g_out,
        vectors[0],
        vectors[1],
        vectors[2],
        g_inner,
        g_in_bias,
        g_back.reshape(ff, wide),
        vectors[3],
        vectors[4],
        vectors[5],
    )


def solution(mesh):
    return jax.shard_map(
        functools.partial(body, mesh.shape["seq"]),
        mesh=mesh,
        in_specs=(
            P(None, "seq", None),
            P(None, None, "head"),
            P(None, "head"),
            P("head", None),
            P(),
            P(),
            P(),
            P(None, "head"),
            P("head"),
            P("head", None),
            P(),
            P(),
            P(),
            P(),
            P(),
            P("seq", None),
            P("seq", None),
            P(None, "seq", None),
        ),
        out_specs=(
            P(None, "seq", None),
            P(None, "seq", None),
            P(None, None, "head"),
            P(None, "head"),
            P("head", None),
            P(),
            P(),
            P(),
            P(None, "head"),
            P("head"),
            P("head", None),
            P(),
            P(),
            P(),
        ),
        check_vma=False,
    )
```

```python
import functools
import math

import jax
import jax.numpy as jnp
from jax import lax
from jax.experimental import pallas as pl
from jax.experimental.pallas import tpu as pltpu
from jax.sharding import PartitionSpec as P

MESH = pl.DeviceIdType.MESH
F32 = jnp.float32
BF16 = jnp.bfloat16
EPSILON = 1e-06
NEGATIVE = -1000000000.0
HDIM = 64
BLK = 64
SHORT, LONG = 0, 1
ROOT = math.sqrt(2.0 / math.pi)
CUBIC = 0.044715
COPIES = 112
TAIL = (
    *("feed_long", "post_long", "back_b", "b0", "in_c", "c0", "in_d", "b1", "back_a", "c1"),
    *("a0", "a1", "d0", "norm_long", "long3", "b2", "post_short", "c2", "long1", "a2"),
    *("long2", "d1", "long0", "norm_short", "short_back", "short_done", "a3", "hop", "query_e", "e0"),
    *("at", "part_short", "d2", "e1", "long_done", "b3", "pair_f", "vec_v", "f0", "ar2"),
    *("v0", "d3", "f1", "e2", "v1", "bt", "dt", "ar1", "c3", "f2"),
    *("e3", "br2", "ct", "f3", "v2", "done_short", "et", "dr2", "br1", "ft"),
    *("er2", "dr1", "v3", "part_long", "cr2", "er1", "fr2", "cr1", "br0", "done_long"),
    *("fr1", "vt", "dr0", "vr2", "er0", "cr0", "bs", "ar0", "ds", "vr1"),
    *("fr0", "es", "vr0", "cs", "as", "fs", "vs"),
)
VEC_ROWS = 256


def dot(a, b, ca=1, cb=0):
    return lax.dot_general(a, b, (((ca,), (cb,)), ((), ())), preferred_element_type=F32)


def aligned(start, size, step):
    return pl.ds(pl.multiple_of(start, step), size)


def loop(count, step):
    def run(index, carry):
        step(index)
        return carry

    lax.fori_loop(0, count, run, 0)


class Links:
    def __init__(self, send_sem, recv_sem, seq, head):
        self.send_sem, self.recv_sem, self.seq, self.head = send_sem, recv_sem, seq, head
        self.used = 0

    def copy(self, src, dst, seq_delta=0, head_delta=0):
        index = self.used
        self.used += 1
        item = pltpu.make_async_remote_copy(
            src_ref=src,
            dst_ref=dst,
            send_sem=self.send_sem.at[index],
            recv_sem=self.recv_sem.at[index],
            device_id=(self.seq ^ seq_delta, self.head ^ head_delta),
            device_id_type=MESH,
        )
        item.start()
        return item


def add_rows(into, into_start, more, more_start, rows, tile):
    def step(i):
        a = aligned(into_start + i * tile, tile, 16)
        b = aligned(more_start + i * tile, tile, 16)
        into[a, :] = (into[a, :].astype(F32) + more[b, :].astype(F32)).astype(BF16)

    loop(rows // tile, step)


class Reduction:
    def __init__(self, links, part, out, full, got, deltas, up, upper, local_sem):
        self.links, self.part, self.out, self.got = links, part, out, got
        self.full = full
        self.up, self.upper, self.local_sem = up, upper, local_sem
        self.deltas = deltas
        size = part.shape[0]
        self.tile = min(48, size // 16)
        start = 0
        self.levels = []
        got_at = 0
        for delta in deltas:
            size = size // 2
            upper_half = (links.seq >> (delta.bit_length() - 1)) & 1
            kept, away = start + upper_half * size, start + (1 - upper_half) * size
            self.levels.append((delta, size, start, kept, away, got_at))
            start = kept
            got_at += size
        self.share, self.share_at = size, start
        self.sent = []
        self.last = None

    def rows(self, ref, start, count):
        return ref.at[aligned(start, count, 16), :]

    def go(self, src, dst, delta):
        self.last = self.links.copy(src, dst, delta)
        self.sent.append(self.last)

    def add(self, start, got_start, rows):
        add_rows(self.part, start, self.got, got_start, rows, self.tile)

    def step(self, index):
        delta, size, start, kept, away, got_at = self.levels[index]
        if index:
            self.last.wait_recv()
            got_start = self.levels[index - 1][5]
            self.add(away, got_start + (away - start), size)
        self.go(self.rows(self.part, away, size), self.rows(self.got, got_at, size), delta)
        if index:
            self.add(kept, got_start + (kept - start), size)

    def total(self):
        self.last.wait_recv()
        self.add(self.share_at, self.levels[-1][5], self.share)
        mine = self.rows(self.part, self.share_at, self.share)
        for level, delta in enumerate(self.upper):
            item = self.links.copy(mine, self.up.at[level], delta)
            item.wait()
            add_rows(self.part, self.share_at, self.up.at[level], 0, self.share, self.tile)
        ready = self.rows(self.full, self.share_at, self.share)

        def step(i):
            rows = aligned(self.share_at + i * self.tile, self.tile, 16)
            self.full[rows, :] = self.part[rows, :]

        loop(self.share // self.tile, step)
        self.go(ready, ready, self.deltas[-1])

    def back(self, index):
        self.last.wait_recv()
        delta, size, start, kept, away, got_at = self.levels[index]
        block = self.rows(self.full, kept, size)
        self.go(block, block, delta)

    def keep(self):
        self.last.wait_recv()
        self.kept = pltpu.make_async_copy(self.full, self.out, self.local_sem)
        self.kept.start()

    def finish(self):
        self.kept.wait()
        for item in self.sent:
            item.wait_send()


def kernel(
    seq_count,
    x_in,
    cot_in,
    qkvw_in,
    outw_in,
    win_in,
    wout_in,
    qv_bias,
    out_bias_in,
    gain_one_in,
    bias_one_in,
    back_bias_in,
    gain_two_in,
    bias_two_in,
    in_bias_in,
    short_len_in,
    long_len_in,
    short_table_in,
    long_table_in,
    out_in,
    in_grad_in,
    sum_back_a,
    sum_back_b,
    sum_in_a,
    sum_in_b,
    sum_query,
    sum_pair,
    sum_vec,
    short_len,
    long_len,
    short_table,
    long_table,
    out,
    x,
    cot,
    qkvw,
    outw,
    win,
    wout,
    params,
    kv_short,
    kv_long,
    q_cols,
    q_rows,
    live_short,
    live_long,
    mixed_cols,
    mixed,
    tops,
    totals,
    post_out,
    post_in,
    norm_one,
    root_one,
    hidden,
    act,
    slope,
    grad_rows,
    grad_feed,
    grad_inner,
    grad_attn,
    g_cols,
    g_rows,
    deltas,
    query_cols,
    dkv_short,
    dkv_long,
    got_short,
    got_core,
    got_far,
    grad_proj,
    part_back_a,
    part_back_b,
    part_in_a,
    part_in_b,
    part_query,
    part_pair,
    part_vec,
    vec,
    got_back_a,
    got_back_b,
    got_in_a,
    got_in_b,
    got_query,
    got_pair,
    got_vec,
    *rest,
):
    upper = [16 << i for i in range(max(0, seq_count.bit_length() - 5))]
    if upper:
        ups = rest[:7]
        rest = rest[7:]
    else:
        ups = (None,) * 7
    fulls, (send_sem, recv_sem, load_sem, local_sem) = rest[:7], rest[7:]
    seq, head = lax.axis_index("seq"), lax.axis_index("head")
    links = Links(send_sem, recv_sem, seq, head)
    tok = x.shape[1]
    wide = x.shape[2]
    col = qkvw.shape[2]
    ff = win.shape[1]
    pairs = col // (2 * HDIM)
    blocks = tok // BLK
    short_span = seq_count // short_len.shape[0]
    long_span = seq_count // long_len.shape[0]
    core = seq & 1

    peers = [1, 2, 4, 8] + upper
    barrier = pltpu.get_barrier_semaphore()
    for delta in peers:
        pl.semaphore_signal(barrier, inc=1, device_id=(seq ^ delta, head), device_id_type=MESH)
    pl.semaphore_signal(barrier, inc=1, device_id=(seq, head ^ 1), device_id_type=MESH)

    loads = []
    for i, (src, dst) in enumerate(
        (
            (x_in, x),
            (qkvw_in, qkvw),
            (short_len_in, short_len),
            (long_len_in, long_len),
            (short_table_in, short_table),
            (long_table_in, long_table),
            (outw_in, outw),
            (win_in, win),
            (wout_in, wout),
            (cot_in, cot),
        )
    ):
        loads.append(pltpu.make_async_copy(src, dst, load_sem.at[i]))
    for item in loads[:6]:
        item.start()

    def param(index):
        return params[index : index + 1, :wide]

    OUTB, GAIN1, BIAS1, BACKB, GAIN2, BIAS2 = range(6)

    def tokens(mb):
        return pl.ds(mb * tok, tok)

    loads[0].wait()
    loads[1].wait()

    def project(mb, c):
        return dot(x[mb], qkvw[c])

    place = seq & (long_span - 1)
    side = seq & (short_span - 1)
    def spread_cols(pair):
        zero = jnp.zeros((HDIM, tok), BF16)
        return jnp.concatenate(
            [
                jnp.concatenate([pair[:HDIM], zero], 0),
                jnp.concatenate([zero, pair[HDIM:]], 0),
            ],
            1,
        )

    def spread_rows(pair):
        lane = lax.broadcasted_iota(jnp.int32, (tok, 128), 1)
        return jnp.concatenate(
            [jnp.where(lane < HDIM, pair, 0.0), jnp.where(lane < HDIM, 0.0, pair)], 0
        ).astype(BF16)

    def queries(mb):
        query = (project(mb, 0) + qv_bias[0:1, :]).astype(BF16).astype(F32) * (HDIM**-0.5)
        for g in range(pairs):
            pair = query[:, g * 128 : g * 128 + 128]
            q_rows[mb, g] = spread_rows(pair)
            q_cols[mb, g] = spread_cols(pair.T.astype(BF16))

    def make_live(live, count, spot, table, length):
        lane_block = lax.broadcasted_iota(jnp.int32, (1, tok), 1) >> 6
        row_block = spot * blocks + lane_block
        picks = []
        for k in range(table.shape[1]):
            pick = jnp.full((1, tok), table[0, k], jnp.int32)
            for b in range(1, blocks):
                pick = jnp.where(lane_block == b, table[b, k], pick)
            picks.append(pick)

        def step(t):
            key = t * tok + lax.broadcasted_iota(jnp.int32, (tok, tok), 0)
            key_block = key >> 6
            allowed = (key_block < 2) | (row_block < 2) | (jnp.abs(row_block - key_block) <= 1)
            for pick in picks:
                allowed = allowed | (key_block == pick)
            live[t] = jnp.where(allowed & (key < length), 0.0, NEGATIVE)

        loop(count, step)

    kv_long[0, place] = project(LONG, 1).astype(BF16)
    kv_long[1, place] = (project(LONG, 2) + qv_bias[1:2, :]).astype(BF16)
    kv_short[0, side] = project(SHORT, 1).astype(BF16)
    kv_short[1, side] = (project(SHORT, 2) + qv_bias[1:2, :]).astype(BF16)
    queries(SHORT)
    for item in loads[2:6]:
        item.wait()
    make_live(live_short, short_span, side, short_table, short_len[seq // short_span])
    queries(LONG)

    def block(which, spot):
        return kv_long.at[which, spot]

    pl.semaphore_wait(barrier, len(peers) + 1)
    key_next = links.copy(block(0, place), block(0, place), 2)
    value_far = links.copy(block(1, place), block(1, place), 4)
    short_core = links.copy(kv_short.at[:, side], kv_short.at[:, side], 1)
    long_core = links.copy(kv_long.at[:, place], kv_long.at[:, place], 1)
    for item in loads[6:]:
        item.start()

    def attend(mb, kv, live, spots, first=False, low=0, high=pairs):
        def pair_step(g):
            lanes = aligned(g * 128, 128, 128)
            q2 = q_cols[mb, g]
            index = mb * pairs + g
            scores = []
            for t in spots:
                mask = live[t]
                scores.append(dot(kv[0, t, :, lanes], q2) + jnp.concatenate([mask, mask], 1))
            top = functools.reduce(jnp.maximum, [jnp.max(s, axis=0, keepdims=True) for s in scores])
            if not first:
                old = tops[index]
                top = jnp.maximum(old, top)
            tops[index] = top
            total = 0.0
            acc_a = 0.0
            acc_b = 0.0
            for t, s in zip(spots, scores):
                weights = jnp.exp(s - top)
                total = total + jnp.sum(weights, axis=0, keepdims=True)
                low = weights.astype(BF16)
                turned = kv[1, t, :, lanes].T
                acc_a = acc_a + dot(turned[:HDIM], low[:, :tok])
                acc_b = acc_b + dot(turned[HDIM:], low[:, tok:])
            rows_a = aligned(g * 128, HDIM, HDIM)
            rows_b = aligned(g * 128 + HDIM, HDIM, HDIM)
            if not first:
                scale = jnp.exp(old - top)
                total = total + totals[index] * scale
                acc_a = acc_a + mixed_cols[mb, rows_a, :] * scale[:, :tok]
                acc_b = acc_b + mixed_cols[mb, rows_b, :] * scale[:, tok:]
            totals[index] = total
            mixed_cols[mb, rows_a, :] = acc_a
            mixed_cols[mb, rows_b, :] = acc_b

        loop(high - low, lambda g: pair_step(g + low))

    def post(stage, mb):
        buf = stage % 2
        return links.copy(post_out.at[buf, mb], post_in.at[buf, mb], 0, 1)

    def received(stage, mb, rows):
        buf = stage % 2
        return post_out[buf, mb, rows, :].astype(F32) + post_in[buf, mb, rows, :].astype(F32)

    posts = {}
    stores = []

    def store(src, dst):
        item = pltpu.make_async_copy(src, dst, load_sem.at[len(loads) + len(stores)])
        item.start()
        stores.append(item)

    def attention_out(mb):
        for g in range(pairs):
            index = mb * pairs + g
            lanes = slice(g * 128, g * 128 + 128)
            total = totals[index]
            inverse = 1.0 / total
            pair = jnp.concatenate(
                [
                    mixed_cols[mb, g * 128 : g * 128 + HDIM, :] * inverse[:, :tok],
                    mixed_cols[mb, g * 128 + HDIM : g * 128 + 128, :] * inverse[:, tok:],
                ],
                0,
            )
            mixed_cols[mb, lanes, :] = pair
            mixed[tokens(mb), lanes] = pair.T.astype(BF16)
            tops[index] = tops[index] + jnp.log(total)
        post_out[0, mb] = dot(mixed[tokens(mb), :], outw[...]).astype(BF16)
        posts[0, mb] = post(0, mb)

    short_core.wait()
    short_spots = tuple(range(short_span))
    attend(SHORT, kv_short, live_short, short_spots, True, 0, pairs - 1)
    key_next.wait_send()
    value_far.wait_send()
    value_next = links.copy(block(1, place), block(1, place), 2)
    key_far = links.copy(block(0, place), block(0, place), 4)
    attend(SHORT, kv_short, live_short, short_spots, True, pairs - 1, pairs)
    loads[6].wait()
    attention_out(SHORT)

    make_live(live_long, long_span, place, long_table, long_len[seq // long_span])
    vec[...] = jnp.zeros_like(vec)
    vectors = (out_bias_in, gain_one_in, bias_one_in, back_bias_in, gain_two_in, bias_two_in)
    for i, vector in enumerate(vectors):
        params[i : i + 1, :wide] = vector[...].reshape(1, wide)
    params[6:7, :] = in_bias_in[...].reshape(1, ff)

    key_next.wait_recv()
    key_corner = links.copy(block(0, place ^ 2), block(0, place ^ 2), 4)
    value_far.wait_recv()
    value_corner = links.copy(block(1, place ^ 4), block(1, place ^ 4), 2)
    long_core.wait()
    attend(LONG, kv_long, live_long, (place, place ^ 1), True)
    value_next.wait_recv()
    pass_next = links.copy(kv_long.at[:, place ^ 2], kv_long.at[:, place ^ 2], 1)
    key_far.wait_recv()
    pass_far = links.copy(kv_long.at[:, place ^ 4], kv_long.at[:, place ^ 4], 1)
    attend(LONG, kv_long, live_long, (place ^ 2, place ^ 4))
    pass_next.wait_recv()
    pass_far.wait_recv()
    attend(LONG, kv_long, live_long, (place ^ 3, place ^ 5))

    def mean(value):
        return jnp.sum(value, axis=-1, keepdims=True) * (1.0 / wide)

    def vec_add(index, value):
        vec[index : index + 1, :wide] += jnp.sum(value, axis=0, keepdims=True)

    tile_rows = 64

    def feed_forward(mb):
        posts[0, mb].wait_recv()
        if mb == SHORT:
            posts[0, mb].wait_send()

        def norm_step(r):
            rows = aligned(r * tile_rows, tile_rows, tile_rows)
            joined = received(0, mb, rows) + param(OUTB) + x[mb, rows, :].astype(F32)
            centred = joined - mean(joined)
            root = lax.rsqrt(mean(centred * centred) + EPSILON)
            normed = centred * root
            norm_one[mb, rows, :] = normed
            root_one[mb, rows, :] = jnp.broadcast_to(root, (tile_rows, 128))
            all_rows = aligned(mb * tok + r * tile_rows, tile_rows, tile_rows)
            hidden[all_rows, :] = (normed * param(GAIN1) + param(BIAS1)).astype(BF16)

        loop(tok // tile_rows, norm_step)

        def col_step(j):
            lanes = aligned(j * 512, 512, 512)
            u = dot(hidden[tokens(mb), :], win[:, lanes]) + params[6:7, lanes]
            square = u * u
            t = jnp.tanh(ROOT * u * (1.0 + CUBIC * square))
            half = 0.5 * (1.0 + t)
            act[tokens(mb), lanes] = (u * half).astype(BF16)
            slope[mb, :, lanes] = (
                half + (0.5 * ROOT) * u * (1.0 - t * t) * (1.0 + (3.0 * CUBIC) * square)
            ).astype(BF16)

        loop(ff // 512, col_step)
        post_out[1, mb] = dot(act[tokens(mb), :], wout[...]).astype(BF16)

    key_corner.wait_recv()
    value_corner.wait_recv()
    pass_corner = links.copy(kv_long.at[:, place ^ 6], kv_long.at[:, place ^ 6], 1)
    attend(LONG, kv_long, live_long, (place ^ 6,))
    pass_corner.wait_recv()
    attend(LONG, kv_long, live_long, (place ^ 7,))
    attention_out(LONG)
    for item in (
        value_next, key_far, key_corner, value_corner,
        pass_next, pass_far, pass_corner,
    ):
        item.wait_send()
    for item in loads[7:]:
        item.wait()
    feed_forward(SHORT)
    posts[0, LONG].wait_send()
    posts[1, SHORT] = post(1, SHORT)
    feed_forward(LONG)
    posts[1, LONG] = post(1, LONG)

    def norm_back(grad, normed, root):
        return root * (grad - mean(grad) - normed * mean(grad * normed))

    def feed_norm(mb):
        posts[1, mb].wait()

        def norm_step(r):
            rows = aligned(r * tile_rows, tile_rows, tile_rows)
            all_rows = aligned(mb * tok + r * tile_rows, tile_rows, tile_rows)
            hid = norm_one[mb, rows, :] * param(GAIN1) + param(BIAS1)
            second = received(1, mb, rows) + param(BACKB) + hid
            centred = second - mean(second)
            root = lax.rsqrt(mean(centred * centred) + EPSILON)
            normed = centred * root
            out[mb, rows, :] = (normed * param(GAIN2) + param(BIAS2)).astype(BF16)
            g = cot[mb, rows, :].astype(F32)
            vec_add(GAIN2, g * normed)
            vec_add(BIAS2, g)
            grad = norm_back(g * param(GAIN2), normed, root)
            vec_add(BACKB, grad)
            grad_rows[mb, rows, :] = grad
            grad_feed[all_rows, :] = grad.astype(BF16)

        loop(tok // tile_rows, norm_step)
        store(out.at[mb], out_in.at[mb])

    def feed_back(mb):
        def col_step(j):
            lanes = aligned(j * 512, 512, 512)
            grad_act = dot(grad_feed[tokens(mb), :], wout[lanes, :], 1, 1).astype(BF16)
            low = (grad_act.astype(F32) * slope[mb, :, lanes].astype(F32)).astype(BF16)
            grad_inner[tokens(mb), lanes] = low
            vec[6:7, lanes] += jnp.sum(low.astype(F32), axis=0, keepdims=True)

        loop(ff // 512, col_step)
        post_out[0, mb] = dot(grad_inner[tokens(mb), :], win[...], 1, 1).astype(BF16)

    feed_norm(SHORT)
    feed_back(SHORT)

    feed_norm(LONG)

    def reduction(index, part, total, got, order):
        return Reduction(links, part, total, fulls[index], got, order, ups[index], upper, local_sem.at[index])

    near_first, far_first = (1, 2, 4, 8), (1, 4, 8, 2)
    red = {
        "a": reduction(0, part_back_a, sum_back_a, got_back_a, near_first),
        "b": reduction(1, part_back_b, sum_back_b, got_back_b, near_first),
        "c": reduction(2, part_in_a, sum_in_a, got_in_a, far_first),
        "d": reduction(3, part_in_b, sum_in_b, got_in_b, near_first),
        "e": reduction(4, part_query, sum_query, got_query, near_first),
        "f": reduction(5, part_pair, sum_pair, got_pair, near_first),
        "v": reduction(6, part_vec, sum_vec, got_vec, near_first),
    }

    def back_grad(part, start):
        def step(j):
            rows = aligned(j * 256, 256, 256)
            lanes = aligned(start + j * 256, 256, 256)
            part[rows, :] = dot(act[:, lanes], grad_feed[...], 0, 0).astype(BF16)

        loop(ff // 512, step)

    def in_grad_half(part, start):
        def step(j):
            rows = aligned(j * 256, 256, 256)
            inner = grad_inner[:, start : start + ff // 2]
            part[rows, :] = dot(hidden[:, rows], inner, 0, 0).astype(BF16)

        loop(wide // 256, step)

    def norm_one_back(mb):
        posts[2, mb].wait()

        def norm_step(r):
            rows = aligned(r * tile_rows, tile_rows, tile_rows)
            all_rows = aligned(mb * tok + r * tile_rows, tile_rows, tile_rows)
            grad = grad_rows[mb, rows, :] + received(2, mb, rows)
            normed = norm_one[mb, rows, :]
            vec_add(GAIN1, grad * normed)
            vec_add(BIAS1, grad)
            joined = norm_back(grad * param(GAIN1), normed, root_one[mb, rows, :1])
            vec_add(OUTB, joined)
            grad_rows[mb, rows, :] = joined
            grad_attn[all_rows, :] = joined.astype(BF16)

        loop(tok // tile_rows, norm_step)
        low = dot(grad_attn[tokens(mb), :], outw[...], 1, 1).astype(BF16).astype(F32)
        for g in range(pairs):
            pair = low[:, g * 128 : g * 128 + 128]
            turned = pair.T
            g_rows[g] = spread_rows(pair)
            g_cols[g] = spread_cols(turned.astype(BF16))
            product = turned * mixed_cols[mb, g * 128 : g * 128 + 128, :]
            deltas[g] = jnp.concatenate(
                [
                    jnp.sum(product[:HDIM], axis=0, keepdims=True),
                    jnp.sum(product[HDIM:], axis=0, keepdims=True),
                ],
                1,
            )

    def attend_back(mb, kv, live, t, store, first=False):
        def pair_step(g):
            lanes = aligned(g * 128, 128, 128)
            keys = kv[0, t, :, lanes]
            values = kv[1, t, :, lanes]
            mask = live[t]
            scores = dot(keys, q_cols[mb, g]) + jnp.concatenate([mask, mask], 1)
            probs = jnp.exp(scores - tops[mb * pairs + g])
            grad_probs = dot(values, g_cols[g])
            low = (probs * (grad_probs - deltas[g])).astype(BF16)
            store(0, lanes, dot(low, q_rows[mb, g]).astype(BF16))
            store(1, lanes, dot(probs.astype(BF16), g_rows[g]).astype(BF16))
            turned = keys.T
            rows_a = aligned(g * 128, HDIM, HDIM)
            rows_b = aligned(g * 128 + HDIM, HDIM, HDIM)
            acc_a = dot(turned[:HDIM], low[:, :tok])
            acc_b = dot(turned[HDIM:], low[:, tok:])
            if not first:
                acc_a = acc_a + query_cols[rows_a, :]
                acc_b = acc_b + query_cols[rows_b, :]
            query_cols[rows_a, :] = acc_a
            query_cols[rows_b, :] = acc_b

        loop(pairs, pair_step)

    def query_done(mb):
        for g in range(pairs):
            lanes = slice(g * 128, g * 128 + 128)
            grad_proj[tokens(mb), lanes] = (query_cols[lanes, :] * (HDIM**-0.5)).T.astype(BF16)

    def store_short(t):
        def store(which, lanes, value):
            dkv_short[which, t, :, lanes] = value

        return store

    def store_long(j, c):
        def store(which, lanes, value):
            dkv_long[which, j, c, :, lanes] = value

        return store

    mine = (seq >> 1) & 3

    def add_block(which, j, more):
        dkv_long[which, j, core] = (
            dkv_long[which, j, core].astype(F32) + more[...].astype(F32)
        ).astype(BF16)

    def go_far(which, j, slot, delta):
        return links.copy(dkv_long.at[which, j, core], got_far.at[slot], delta)

    core_grads = []
    key_hop = []
    value_hop = []

    def long_back(d):
        j = mine ^ d
        attend_back(LONG, kv_long, live_long, 2 * j + 1 - core, store_long(j, 1 - core), d == 3)
        item = links.copy(dkv_long.at[:, j, 1 - core], got_core.at[:, j], 1)
        core_grads.append(item)
        attend_back(LONG, kv_long, live_long, 2 * j + core, store_long(j, core))
        item.wait_recv()
        for which in range(2):
            add_block(which, j, got_core.at[which, j])
        if d == 1:
            key_hop.extend([go_far(0, mine ^ 3, 0, 2), go_far(0, mine ^ 1, 1, 2)])
        if d == 2:
            value_hop.extend([go_far(1, mine ^ 3, 2, 4), go_far(1, mine ^ 2, 3, 4)])
        if d == 0:
            query_done(LONG)

    def second_hop():
        key_hop[0].wait_recv()
        add_block(0, mine ^ 2, got_far.at[0])
        key_hop.append(go_far(0, mine ^ 2, 4, 4))
        value_hop[0].wait_recv()
        add_block(1, mine ^ 1, got_far.at[2])
        value_hop.append(go_far(1, mine ^ 1, 5, 2))

    half_wide = wide // 2

    def out_step(j):
        lanes = aligned(j * half_wide, half_wide, half_wide)
        rows = aligned(j * col, col, col)
        part_query[rows, 0:col] = dot(mixed[...], grad_attn[:, lanes], 0, 0).astype(BF16)

    def x_grad(items):
        def step(j):
            rows = aligned(j * 256, 256, 256)
            columns = jnp.concatenate([x[0, :, rows], x[1, :, rows]], 0)
            for part, lanes, source in items:
                part[rows, lanes] = dot(columns, grad_proj[:, source], 0, 0).astype(BF16)

        loop(wide // 256, step)

    def input_part(mb):
        rows = tokens(mb)
        total = dot(grad_proj[rows, 0:col], qkvw[0], 1, 1)
        total = total + dot(grad_proj[rows, col : 2 * col], qkvw[1], 1, 1)
        total = total + dot(grad_proj[rows, 2 * col : 3 * col], qkvw[2], 1, 1)
        post_out[1, mb] = total.astype(BF16)
        posts[3, mb] = post(3, mb)

    def input_done(mb):
        posts[3, mb].wait()
        stores[mb].wait()

        def step(r):
            rows = aligned(r * tile_rows, tile_rows, tile_rows)
            out[mb, rows, :] = (grad_rows[mb, rows, :] + received(3, mb, rows)).astype(BF16)

        loop(tok // tile_rows, step)
        store(out.at[mb], in_grad_in.at[mb])

    short_grads = []

    def short_back():
        attend_back(SHORT, kv_short, live_short, 1 - side, store_short(1 - side), True)
        short_grads.append(links.copy(dkv_short.at[:, 1 - side], got_short, 1))
        attend_back(SHORT, kv_short, live_short, side, store_short(side))
        query_done(SHORT)

    def query_grad():
        loop(2, out_step)
        x_grad([(part_query, slice(col, 2 * col), slice(0, col))])

    def short_done():
        short_grads[0].wait()
        for which in range(2):
            lanes = slice((1 + which) * col, (2 + which) * col)
            total = dkv_short[which, side].astype(F32) + got_short[which].astype(F32)
            grad_proj[tokens(SHORT), lanes] = total.astype(BF16)

    def long_done():
        for hop, which in ((key_hop, 0), (value_hop, 1)):
            lanes = slice((1 + which) * col, (2 + which) * col)
            hop[1].wait_recv()
            hop[2].wait_recv()
            total = dkv_long[which, mine, core].astype(F32) + got_far[2 * which + 1].astype(F32)
            total = total + got_far[4 + which].astype(F32)
            grad_proj[tokens(LONG), lanes] = total.astype(BF16)

    def pair_grad():
        x_grad(
            [
                (part_pair, slice(0, col), slice(col, 2 * col)),
                (part_pair, slice(col, 2 * col), slice(2 * col, 3 * col)),
            ]
        )

    def vectors_done():
        vec[7:8, 0:col] = jnp.sum(grad_proj[:, 0:col].astype(F32), axis=0, keepdims=True)
        vec[7:8, col : 2 * col] = jnp.sum(
            grad_proj[:, 2 * col : 3 * col].astype(F32), axis=0, keepdims=True
        )
        part_vec[...] = jnp.zeros_like(part_vec)
        lines = []
        for index, width in [(i, wide) for i in range(6)] + [(7, 2 * col), (6, ff)]:
            for k in range(width // 128):
                lines.append(vec[index : index + 1, k * 128 : k * 128 + 128])
        while len(lines) % 16:
            lines.append(jnp.zeros((1, 128), F32))
        part_vec[0 : len(lines), :] = jnp.concatenate(lines, 0).astype(BF16)

    def post_now(stage, mb):
        posts[stage, mb] = post(stage, mb)

    steps = {
        "back_a": lambda: back_grad(part_back_a, 0),
        "back_b": lambda: back_grad(part_back_b, ff // 2),
        "feed_long": lambda: feed_back(LONG),
        "post_long": lambda: post_now(2, LONG),
        "in_c": lambda: in_grad_half(part_in_a, 0),
        "in_d": lambda: in_grad_half(part_in_b, ff // 2),
        "norm_long": lambda: norm_one_back(LONG),
        "post_short": lambda: post_now(2, SHORT),
        "long3": lambda: long_back(3),
        "long1": lambda: long_back(1),
        "long2": lambda: long_back(2),
        "long0": lambda: long_back(0),
        "hop": second_hop,
        "norm_short": lambda: norm_one_back(SHORT),
        "short_back": short_back,
        "query_e": query_grad,
        "short_done": short_done,
        "part_short": lambda: input_part(SHORT),
        "long_done": long_done,
        "pair_f": pair_grad,
        "vec_v": vectors_done,
        "part_long": lambda: input_part(LONG),
        "done_short": lambda: input_done(SHORT),
        "done_long": lambda: input_done(LONG),
    }
    for name, item in red.items():
        for i in range(4):
            steps[name + str(i)] = functools.partial(item.step, i)
        steps[name + "t"] = item.total
        steps[name + "s"] = item.keep
        for i in range(3):
            steps[name + "r" + str(i)] = functools.partial(item.back, i)
    for name in TAIL:
        steps[name]()
    for item in red.values():
        item.finish()
    for item in core_grads + key_hop + value_hop:
        item.wait_send()
    for item in stores[2:]:
        item.wait()


def widen(
    sum_back_a,
    sum_back_b,
    sum_in_a,
    sum_in_b,
    sum_query,
    sum_pair,
    sum_vec,
    out_in,
    grad_in,
    out,
    in_grad,
    g_back,
    g_inner,
    g_qkv,
    g_out,
    g_qv,
    g_in_bias,
    *rest,
):
    vectors = rest[:6]
    lows, highs, load_sem, store_sem, copy_sem = rest[6:11], rest[11:15], *rest[15:18]
    low_back, low_in, low_query, low_pair, low_vec = lows
    high_back, high_in, high_qkv, high_out = highs
    col = sum_query.shape[1] // 2
    wide = sum_query.shape[0]
    low_out, low_grad = rest[18:20]
    copies = [
        pltpu.make_async_copy(out_in, low_out, copy_sem.at[0]),
        pltpu.make_async_copy(grad_in, low_grad, copy_sem.at[1]),
    ]
    loads = {}
    half = wide // 2

    def load(name, src, dst):
        loads[name] = pltpu.make_async_copy(src, dst, load_sem.at[len(loads)])
        loads[name].start()

    first, second = pl.ds(0, half), pl.ds(half, half)
    load("vec", sum_vec, low_vec)
    load("query", sum_query, low_query)
    for part, name in ((first, "0"), (second, "1")):
        load("pair" + name, sum_pair.at[part], low_pair.at[part])
    for i, (back, inner) in enumerate(((sum_back_a, sum_in_a), (sum_back_b, sum_in_b))):
        for part, name in ((first, "0"), (second, "1")):
            load("back" + str(i) + name, back.at[part], low_back.at[i, part])
            load("in" + str(i) + name, inner.at[part], low_in.at[i, part])
    for item in copies:
        item.start()
    stores = []

    def store(src, dst):
        item = pltpu.make_async_copy(src, dst, store_sem.at[len(stores)])
        item.start()
        stores.append(item)

    def cast(dst, src, start, rows, lanes, src_lanes, src_start=None):
        shift = 0 if src_start is None else src_start - start

        def step(r):
            here = aligned(start + r * 32, 32, 32)
            there = aligned(start + shift + r * 32, 32, 32)
            dst[here, lanes] = src[there, src_lanes].astype(F32)

        loop(rows // 32, step)

    for item, low, high in zip(copies, (low_out, low_grad), (out, in_grad)):
        item.wait()
        store(low, high)
    loads["vec"].wait()
    full = low_vec[...].astype(F32)

    def line(row, count):
        return jnp.concatenate([full[r : r + 1, :] for r in range(row, row + count)], 1)

    per = wide // 128
    for i, vector in enumerate(vectors):
        vector[...] = line(i * per, per).reshape(wide)
    row = len(vectors) * per
    g_qv[...] = jnp.concatenate([line(row, col // 128), line(row + col // 128, col // 128)], 0)
    bias = line(row + 2 * col // 128, g_in_bias.shape[0] // 128)
    g_in_bias[...] = bias.reshape(g_in_bias.shape[0])
    left, right, every = pl.ds(0, col), pl.ds(col, col), slice(None)
    loads["query"].wait()
    cast(high_out, low_query, 0, col, left, left)
    cast(high_out, low_query, 0, col, right, left, col)
    store(high_out, g_out)
    cast(high_qkv.at[0], low_query, 0, wide, every, right)
    store(high_qkv.at[0], g_qkv.at[0])
    for part, name, start in ((first, "0", 0), (second, "1", half)):
        loads["pair" + name].wait()
        cast(high_qkv.at[1], low_pair, start, half, every, left)
        cast(high_qkv.at[2], low_pair, start, half, every, right)
        store(high_qkv.at[1, part], g_qkv.at[1, part])
        store(high_qkv.at[2, part], g_qkv.at[2, part])
    for i in range(2):
        for part, name, start in ((first, "0", 0), (second, "1", half)):
            loads["back" + str(i) + name].wait()
            cast(high_back.at[i], low_back.at[i], start, half, every, every)
            store(high_back.at[i, part], g_back.at[i, part])
            loads["in" + str(i) + name].wait()
            cast(high_in.at[i], low_in.at[i], start, half, every, every)
            lanes = pl.ds(i * wide, wide)
            store(high_in.at[i, part], g_inner.at[part, lanes])
    for item in stores:
        item.wait()


def body(
    seq_count,
    inputs,
    qkv_weight,
    qv_bias,
    out_weight,
    out_bias,
    ln1_gain,
    ln1_bias,
    ffn_in,
    ffn_in_bias,
    ffn_out,
    ffn_out_bias,
    ln2_gain,
    ln2_bias,
    short_lengths,
    long_lengths,
    short_random,
    long_random,
    cotangent,
):
    tok, wide = inputs.shape[1:]
    col = qkv_weight.shape[2]
    ff = ffn_in.shape[1]
    pairs = col // (2 * HDIM)
    short_span = seq_count // short_lengths.shape[0]
    long_span = seq_count // long_lengths.shape[0]
    upper = max(0, seq_count.bit_length() - 5)

    parts = [(ff // 2, wide)] * 2 + [(wide, ff // 2)] * 2 + [(wide, 2 * col)] * 2 + [(VEC_ROWS, 128)]
    vmem = pltpu.VMEM
    scratch = [
        pltpu.SMEM(short_lengths.shape, jnp.int32),
        pltpu.SMEM(long_lengths.shape, jnp.int32),
        pltpu.SMEM(short_random.shape, jnp.int32),
        pltpu.SMEM(long_random.shape, jnp.int32),
        vmem((2, tok, wide), BF16),
        vmem((2, tok, wide), BF16),
        vmem((2, tok, wide), BF16),
        vmem((3, wide, col), BF16),
        vmem((col, wide), BF16),
        vmem((wide, ff), BF16),
        vmem((ff, wide), BF16),
        vmem((8, ff), F32),
        vmem((2, short_span, tok, col), BF16),
        vmem((2, long_span, tok, col), BF16),
        vmem((2, pairs, 128, 2 * tok), BF16),
        vmem((2, pairs, 2 * tok, 128), BF16),
        vmem((short_span, tok, tok), F32),
        vmem((long_span, tok, tok), F32),
        vmem((2, col, tok), F32),
        vmem((2 * tok, col), BF16),
        vmem((2 * pairs, 1, 2 * tok), F32),
        vmem((2 * pairs, 1, 2 * tok), F32),
        vmem((2, 2, tok, wide), BF16),
        vmem((2, 2, tok, wide), BF16),
        vmem((2, tok, wide), F32),
        vmem((2, tok, 128), F32),
        vmem((2 * tok, wide), BF16),
        vmem((2 * tok, ff), BF16),
        vmem((2, tok, ff), BF16),
        vmem((2, tok, wide), F32),
        vmem((2 * tok, wide), BF16),
        vmem((2 * tok, ff), BF16),
        vmem((2 * tok, wide), BF16),
        vmem((pairs, 128, 2 * tok), BF16),
        vmem((pairs, 2 * tok, 128), BF16),
        vmem((pairs, 1, 2 * tok), F32),
        vmem((col, tok), F32),
        vmem((2, short_span, tok, col), BF16),
        vmem((2, long_span // 2, 2, tok, col), BF16),
        vmem((2, tok, col), BF16),
        vmem((2, long_span // 2, tok, col), BF16),
        vmem((6, tok, col), BF16),
        vmem((2 * tok, 3 * col), BF16),
    ]
    scratch += [vmem(shape, BF16) for shape in parts]
    scratch += [vmem((8, ff), F32)]
    scratch += [vmem((r - r // 16, w), BF16) for r, w in parts]
    if upper:
        scratch += [vmem((upper, r // 16, w), BF16) for r, w in parts]
    scratch += [vmem(shape, BF16) for shape in parts]
    scratch += [
        pltpu.SemaphoreType.DMA((COPIES,)),
        pltpu.SemaphoreType.DMA((COPIES,)),
        pltpu.SemaphoreType.DMA((16,)),
        pltpu.SemaphoreType.DMA((8,)),
    ]
    any_spec = pl.BlockSpec(memory_space=pl.ANY)
    vmem_spec = pl.BlockSpec(memory_space=pltpu.VMEM)
    out, in_grad, s_back_a, s_back_b, s_in_a, s_in_b, s_query, s_pair, s_vec = pl.pallas_call(
        functools.partial(kernel, seq_count),
        out_shape=[
            jax.ShapeDtypeStruct(inputs.shape, BF16),
            jax.ShapeDtypeStruct(inputs.shape, BF16),
        ]
        + [jax.ShapeDtypeStruct(shape, BF16) for shape in parts],
        in_specs=[any_spec] * 6 + [vmem_spec] * 8 + [any_spec] * 4,
        out_specs=[any_spec] * 9,
        scratch_shapes=scratch,
        compiler_params=pltpu.CompilerParams(
            collective_id=0, has_side_effects=True, vmem_limit_bytes=65_000 * 1024
        ),
        cost_estimate=pl.CostEstimate(
            flops=12_000_000_000, bytes_accessed=40_000_000, transcendentals=8_000_000
        ),
        name="layer",
    )(
        inputs,
        cotangent,
        qkv_weight,
        out_weight,
        ffn_in,
        ffn_out,
        qv_bias,
        out_bias,
        ln1_gain,
        ln1_bias,
        ffn_out_bias,
        ln2_gain,
        ln2_bias,
        ffn_in_bias,
        short_lengths,
        long_lengths,
        short_random,
        long_random,
    )
    vector = jax.ShapeDtypeStruct((wide,), F32)
    out, in_grad, g_back, g_inner, g_qkv, g_out, g_qv, g_in_bias, *vectors = pl.pallas_call(
        widen,
        out_shape=[
            jax.ShapeDtypeStruct(inputs.shape, BF16),
            jax.ShapeDtypeStruct(inputs.shape, BF16),
            jax.ShapeDtypeStruct((2, ff // 2, wide), F32),
            jax.ShapeDtypeStruct((wide, ff), F32),
            jax.ShapeDtypeStruct((3, wide, col), F32),
            jax.ShapeDtypeStruct((col, wide), F32),
            jax.ShapeDtypeStruct((2, col), F32),
            jax.ShapeDtypeStruct((ff,), F32),
        ]
        + [vector] * 6,
        in_specs=[any_spec] * 9,
        out_specs=[any_spec] * 6 + [vmem_spec] * 8,
        scratch_shapes=[
            vmem((2, wide, wide), BF16),
            vmem((2, wide, wide), BF16),
            vmem((wide, 2 * col), BF16),
            vmem((wide, 2 * col), BF16),
            vmem((VEC_ROWS, 128), BF16),
            vmem((2, wide, wide), F32),
            vmem((2, wide, wide), F32),
            vmem((3, wide, col), F32),
            vmem((col, wide), F32),
            pltpu.SemaphoreType.DMA((16,)),
            pltpu.SemaphoreType.DMA((20,)),
            pltpu.SemaphoreType.DMA((2,)),
            vmem(inputs.shape, BF16),
            vmem(inputs.shape, BF16),
        ],
        compiler_params=pltpu.CompilerParams(vmem_limit_bytes=63 * 1024 * 1024),
        name="widen",
    )(s_back_a, s_back_b, s_in_a, s_in_b, s_query, s_pair, s_vec, out, in_grad)
    return (
        out,
        in_grad,
        g_qkv,
        g_qv,
        g_out,
        vectors[0],
        vectors[1],
        vectors[2],
        g_inner,
        g_in_bias,
        g_back.reshape(ff, wide),
        vectors[3],
        vectors[4],
        vectors[5],
    )


def solution(mesh):
    return jax.shard_map(
        functools.partial(body, mesh.shape["seq"]),
        mesh=mesh,
        in_specs=(
            P(None, "seq", None),
            P(None, None, "head"),
            P(None, "head"),
            P("head", None),
            P(),
            P(),
            P(),
            P(None, "head"),
            P("head"),
            P("head", None),
            P(),
            P(),
            P(),
            P(),
            P(),
            P("seq", None),
            P("seq", None),
            P(None, "seq", None),
        ),
        out_specs=(
            P(None, "seq", None),
            P(None, "seq", None),
            P(None, None, "head"),
            P(None, "head"),
            P("head", None),
            P(),
            P(),
            P(),
            P(None, "head"),
            P("head"),
            P("head", None),
            P(),
            P(),
            P(),
        ),
        check_vma=False,
    )
```

```python
import functools
import math

import jax
import jax.numpy as jnp
from jax import lax
from jax.experimental import pallas as pl
from jax.experimental.pallas import tpu as pltpu
from jax.sharding import PartitionSpec as P

MESH = pl.DeviceIdType.MESH
F32 = jnp.float32
BF16 = jnp.bfloat16
EPSILON = 1e-06
NEGATIVE = -1000000000.0
HDIM = 64
BLK = 64
SHORT, LONG = 0, 1
ROOT = math.sqrt(2.0 / math.pi)
CUBIC = 0.044715
COPIES = 112
TAIL = (
    *("feed_long", "post_long", "back_b", "b0", "in_c", "c0", "in_d", "b1", "back_a", "c1"),
    *("a0", "a1", "d0", "norm_long", "long3", "b2", "post_short", "c2", "long1", "a2"),
    *("long2", "d1", "long0", "norm_short", "short_back", "short_done", "a3", "hop", "query_e", "e0"),
    *("at", "part_short", "d2", "e1", "long_done", "b3", "pair_f", "vec_v", "f0", "ar2"),
    *("v0", "d3", "f1", "e2", "v1", "bt", "dt", "ar1", "c3", "f2"),
    *("e3", "br2", "ct", "f3", "v2", "done_short", "et", "dr2", "br1", "ft"),
    *("er2", "dr1", "v3", "part_long", "cr2", "er1", "fr2", "cr1", "br0", "done_long"),
    *("fr1", "vt", "dr0", "vr2", "er0", "cr0", "bs", "ar0", "ds", "vr1"),
    *("fr0", "es", "vr0", "cs", "as", "fs", "vs"),
)
VEC_ROWS = 256


def dot(a, b, ca=1, cb=0):
    return lax.dot_general(a, b, (((ca,), (cb,)), ((), ())), preferred_element_type=F32)


def aligned(start, size, step):
    return pl.ds(pl.multiple_of(start, step), size)


def loop(count, step):
    def run(index, carry):
        step(index)
        return carry

    lax.fori_loop(0, count, run, 0)


class Links:
    def __init__(self, send_sem, recv_sem, seq, head):
        self.send_sem, self.recv_sem, self.seq, self.head = send_sem, recv_sem, seq, head
        self.used = 0

    def copy(self, src, dst, seq_delta=0, head_delta=0):
        index = self.used
        self.used += 1
        item = pltpu.make_async_remote_copy(
            src_ref=src,
            dst_ref=dst,
            send_sem=self.send_sem.at[index],
            recv_sem=self.recv_sem.at[index],
            device_id=(self.seq ^ seq_delta, self.head ^ head_delta),
            device_id_type=MESH,
        )
        item.start()
        return item


def add_rows(into, into_start, more, more_start, rows, tile):
    def step(i):
        a = aligned(into_start + i * tile, tile, 16)
        b = aligned(more_start + i * tile, tile, 16)
        into[a, :] = (into[a, :].astype(F32) + more[b, :].astype(F32)).astype(BF16)

    loop(rows // tile, step)


class Reduction:
    def __init__(self, links, part, out, full, got, deltas, up, upper, local_sem):
        self.links, self.part, self.out, self.got = links, part, out, got
        self.full = full
        self.up, self.upper, self.local_sem = up, upper, local_sem
        self.deltas = deltas
        size = part.shape[0]
        self.tile = min(48, size // 16)
        start = 0
        self.levels = []
        got_at = 0
        for delta in deltas:
            size = size // 2
            upper_half = (links.seq >> (delta.bit_length() - 1)) & 1
            kept, away = start + upper_half * size, start + (1 - upper_half) * size
            self.levels.append((delta, size, start, kept, away, got_at))
            start = kept
            got_at += size
        self.share, self.share_at = size, start
        self.sent = []
        self.last = None

    def rows(self, ref, start, count):
        return ref.at[aligned(start, count, 16), :]

    def go(self, src, dst, delta):
        self.last = self.links.copy(src, dst, delta)
        self.sent.append(self.last)

    def add(self, start, got_start, rows):
        add_rows(self.part, start, self.got, got_start, rows, self.tile)

    def step(self, index):
        delta, size, start, kept, away, got_at = self.levels[index]
        if index:
            self.last.wait_recv()
            got_start = self.levels[index - 1][5]
            self.add(away, got_start + (away - start), size)
        self.go(self.rows(self.part, away, size), self.rows(self.got, got_at, size), delta)
        if index:
            self.add(kept, got_start + (kept - start), size)

    def total(self):
        self.last.wait_recv()
        self.add(self.share_at, self.levels[-1][5], self.share)
        mine = self.rows(self.part, self.share_at, self.share)
        for level, delta in enumerate(self.upper):
            item = self.links.copy(mine, self.up.at[level], delta)
            item.wait()
            add_rows(self.part, self.share_at, self.up.at[level], 0, self.share, self.tile)
        ready = self.rows(self.full, self.share_at, self.share)

        def step(i):
            rows = aligned(self.share_at + i * self.tile, self.tile, 16)
            self.full[rows, :] = self.part[rows, :]

        loop(self.share // self.tile, step)
        self.go(ready, ready, self.deltas[-1])

    def back(self, index):
        self.last.wait_recv()
        delta, size, start, kept, away, got_at = self.levels[index]
        block = self.rows(self.full, kept, size)
        self.go(block, block, delta)

    def keep(self):
        self.last.wait_recv()
        self.kept = pltpu.make_async_copy(self.full, self.out, self.local_sem)
        self.kept.start()

    def finish(self):
        self.kept.wait()
        for item in self.sent:
            item.wait_send()


def kernel(
    seq_count,
    x_in,
    cot_in,
    qkvw_in,
    outw_in,
    win_in,
    wout_in,
    qv_bias,
    out_bias_in,
    gain_one_in,
    bias_one_in,
    back_bias_in,
    gain_two_in,
    bias_two_in,
    in_bias_in,
    short_len_in,
    long_len_in,
    short_table_in,
    long_table_in,
    out_in,
    in_grad_in,
    sum_back_a,
    sum_back_b,
    sum_in_a,
    sum_in_b,
    sum_query,
    sum_pair,
    sum_vec,
    short_len,
    long_len,
    short_table,
    long_table,
    out,
    x,
    cot,
    qkvw,
    outw,
    win,
    wout,
    params,
    kv_short,
    kv_long,
    q_cols,
    q_rows,
    live_short,
    live_long,
    mixed_cols,
    mixed,
    tops,
    totals,
    post_out,
    post_in,
    norm_one,
    root_one,
    hidden,
    act,
    slope,
    grad_rows,
    grad_feed,
    grad_inner,
    grad_attn,
    g_cols,
    g_rows,
    deltas,
    query_cols,
    dkv_short,
    dkv_long,
    got_short,
    got_core,
    got_far,
    grad_proj,
    part_back_a,
    part_back_b,
    part_in_a,
    part_in_b,
    part_query,
    part_pair,
    part_vec,
    vec,
    got_back_a,
    got_back_b,
    got_in_a,
    got_in_b,
    got_query,
    got_pair,
    got_vec,
    *rest,
):
    upper = [16 << i for i in range(max(0, seq_count.bit_length() - 5))]
    if upper:
        ups = rest[:7]
        rest = rest[7:]
    else:
        ups = (None,) * 7
    fulls, (send_sem, recv_sem, load_sem, local_sem) = rest[:7], rest[7:]
    seq, head = lax.axis_index("seq"), lax.axis_index("head")
    links = Links(send_sem, recv_sem, seq, head)
    tok = x.shape[1]
    wide = x.shape[2]
    col = qkvw.shape[2]
    ff = win.shape[1]
    pairs = col // (2 * HDIM)
    blocks = tok // BLK
    short_span = seq_count // short_len.shape[0]
    long_span = seq_count // long_len.shape[0]
    core = seq & 1

    peers = [1, 2, 4, 8] + upper
    barrier = pltpu.get_barrier_semaphore()
    for delta in peers:
        pl.semaphore_signal(barrier, inc=1, device_id=(seq ^ delta, head), device_id_type=MESH)
    pl.semaphore_signal(barrier, inc=1, device_id=(seq, head ^ 1), device_id_type=MESH)

    loads = []
    for i, (src, dst) in enumerate(
        (
            (x_in, x),
            (qkvw_in, qkvw),
            (short_len_in, short_len),
            (long_len_in, long_len),
            (short_table_in, short_table),
            (long_table_in, long_table),
            (outw_in, outw),
            (win_in, win),
            (wout_in, wout),
            (cot_in, cot),
        )
    ):
        loads.append(pltpu.make_async_copy(src, dst, load_sem.at[i]))
    for item in loads[:6]:
        item.start()

    def param(index):
        return params[index : index + 1, :wide]

    OUTB, GAIN1, BIAS1, BACKB, GAIN2, BIAS2 = range(6)

    def tokens(mb):
        return pl.ds(mb * tok, tok)

    loads[0].wait()
    loads[1].wait()

    def project(mb, c):
        return dot(x[mb], qkvw[c])

    place = seq & (long_span - 1)
    side = seq & (short_span - 1)
    def spread_cols(pair):
        zero = jnp.zeros((HDIM, tok), BF16)
        return jnp.concatenate(
            [
                jnp.concatenate([pair[:HDIM], zero], 0),
                jnp.concatenate([zero, pair[HDIM:]], 0),
            ],
            1,
        )

    def spread_rows(pair):
        lane = lax.broadcasted_iota(jnp.int32, (tok, 128), 1)
        return jnp.concatenate(
            [jnp.where(lane < HDIM, pair, 0.0), jnp.where(lane < HDIM, 0.0, pair)], 0
        ).astype(BF16)

    def queries(mb):
        query = (project(mb, 0) + qv_bias[0:1, :]).astype(BF16).astype(F32) * (HDIM**-0.5)
        for g in range(pairs):
            pair = query[:, g * 128 : g * 128 + 128]
            q_rows[mb, g] = spread_rows(pair)
            q_cols[mb, g] = spread_cols(pair.T.astype(BF16))

    def make_live(live, count, spot, table, length):
        lane_block = lax.broadcasted_iota(jnp.int32, (1, tok), 1) >> 6
        row_block = spot * blocks + lane_block
        picks = []
        for k in range(table.shape[1]):
            pick = jnp.full((1, tok), table[0, k], jnp.int32)
            for b in range(1, blocks):
                pick = jnp.where(lane_block == b, table[b, k], pick)
            picks.append(pick)

        def step(t):
            key = t * tok + lax.broadcasted_iota(jnp.int32, (tok, tok), 0)
            key_block = key >> 6
            allowed = (key_block < 2) | (row_block < 2) | (jnp.abs(row_block - key_block) <= 1)
            for pick in picks:
                allowed = allowed | (key_block == pick)
            live[t] = jnp.where(allowed & (key < length), 0.0, NEGATIVE)

        loop(count, step)

    kv_long[0, place] = project(LONG, 1).astype(BF16)
    kv_long[1, place] = (project(LONG, 2) + qv_bias[1:2, :]).astype(BF16)
    kv_short[0, side] = project(SHORT, 1).astype(BF16)
    kv_short[1, side] = (project(SHORT, 2) + qv_bias[1:2, :]).astype(BF16)
    queries(SHORT)
    for item in loads[2:6]:
        item.wait()
    make_live(live_short, short_span, side, short_table, short_len[seq // short_span])
    queries(LONG)

    def block(which, spot):
        return kv_long.at[which, spot]

    pl.semaphore_wait(barrier, len(peers) + 1)
    key_next = links.copy(block(0, place), block(0, place), 2)
    value_far = links.copy(block(1, place), block(1, place), 4)
    short_core = links.copy(kv_short.at[:, side], kv_short.at[:, side], 1)
    long_core = links.copy(kv_long.at[:, place], kv_long.at[:, place], 1)
    for item in loads[6:]:
        item.start()

    def attend(mb, kv, live, spots, first=False, low=0, high=pairs):
        def pair_step(g):
            lanes = aligned(g * 128, 128, 128)
            q2 = q_cols[mb, g]
            index = mb * pairs + g
            scores = []
            for t in spots:
                mask = live[t]
                scores.append(dot(kv[0, t, :, lanes], q2) + jnp.concatenate([mask, mask], 1))
            top = functools.reduce(jnp.maximum, [jnp.max(s, axis=0, keepdims=True) for s in scores])
            if not first:
                old = tops[index]
                top = jnp.maximum(old, top)
            tops[index] = top
            total = 0.0
            acc_a = 0.0
            acc_b = 0.0
            for t, s in zip(spots, scores):
                weights = jnp.exp(s - top)
                total = total + jnp.sum(weights, axis=0, keepdims=True)
                low = weights.astype(BF16)
                turned = kv[1, t, :, lanes].T
                acc_a = acc_a + dot(turned[:HDIM], low[:, :tok])
                acc_b = acc_b + dot(turned[HDIM:], low[:, tok:])
            rows_a = aligned(g * 128, HDIM, HDIM)
            rows_b = aligned(g * 128 + HDIM, HDIM, HDIM)
            if not first:
                scale = jnp.exp(old - top)
                total = total + totals[index] * scale
                acc_a = acc_a + mixed_cols[mb, rows_a, :] * scale[:, :tok]
                acc_b = acc_b + mixed_cols[mb, rows_b, :] * scale[:, tok:]
            totals[index] = total
            mixed_cols[mb, rows_a, :] = acc_a
            mixed_cols[mb, rows_b, :] = acc_b

        loop(high - low, lambda g: pair_step(g + low))

    def post(stage, mb):
        buf = stage % 2
        return links.copy(post_out.at[buf, mb], post_in.at[buf, mb], 0, 1)

    def received(stage, mb, rows):
        buf = stage % 2
        return post_out[buf, mb, rows, :].astype(F32) + post_in[buf, mb, rows, :].astype(F32)

    posts = {}
    stores = []

    def store(src, dst):
        item = pltpu.make_async_copy(src, dst, load_sem.at[len(loads) + len(stores)])
        item.start()
        stores.append(item)

    def attention_out(mb):
        for g in range(pairs):
            index = mb * pairs + g
            lanes = slice(g * 128, g * 128 + 128)
            total = totals[index]
            inverse = 1.0 / total
            pair = jnp.concatenate(
                [
                    mixed_cols[mb, g * 128 : g * 128 + HDIM, :] * inverse[:, :tok],
                    mixed_cols[mb, g * 128 + HDIM : g * 128 + 128, :] * inverse[:, tok:],
                ],
                0,
            )
            mixed_cols[mb, lanes, :] = pair
            mixed[tokens(mb), lanes] = pair.T.astype(BF16)
            tops[index] = tops[index] + jnp.log(total)
        post_out[0, mb] = dot(mixed[tokens(mb), :], outw[...]).astype(BF16)
        posts[0, mb] = post(0, mb)

    short_core.wait()
    short_spots = tuple(range(short_span))
    attend(SHORT, kv_short, live_short, short_spots, True, 0, pairs - 1)
    key_next.wait_send()
    value_far.wait_send()
    value_next = links.copy(block(1, place), block(1, place), 2)
    key_far = links.copy(block(0, place), block(0, place), 4)
    attend(SHORT, kv_short, live_short, short_spots, True, pairs - 1, pairs)
    loads[6].wait()
    attention_out(SHORT)

    make_live(live_long, long_span, place, long_table, long_len[seq // long_span])
    vec[...] = jnp.zeros_like(vec)
    vectors = (out_bias_in, gain_one_in, bias_one_in, back_bias_in, gain_two_in, bias_two_in)
    for i, vector in enumerate(vectors):
        params[i : i + 1, :wide] = vector[...].reshape(1, wide)
    params[6:7, :] = in_bias_in[...].reshape(1, ff)

    key_next.wait_recv()
    key_corner = links.copy(block(0, place ^ 2), block(0, place ^ 2), 4)
    value_far.wait_recv()
    value_corner = links.copy(block(1, place ^ 4), block(1, place ^ 4), 2)
    long_core.wait()
    attend(LONG, kv_long, live_long, (place, place ^ 1), True)
    value_next.wait_recv()
    pass_next = links.copy(kv_long.at[:, place ^ 2], kv_long.at[:, place ^ 2], 1)
    key_far.wait_recv()
    pass_far = links.copy(kv_long.at[:, place ^ 4], kv_long.at[:, place ^ 4], 1)
    attend(LONG, kv_long, live_long, (place ^ 2, place ^ 4))
    pass_next.wait_recv()
    pass_far.wait_recv()
    attend(LONG, kv_long, live_long, (place ^ 3, place ^ 5))

    def mean(value):
        return jnp.sum(value, axis=-1, keepdims=True) * (1.0 / wide)

    def vec_add(index, value):
        vec[index : index + 1, :wide] += jnp.sum(value, axis=0, keepdims=True)

    tile_rows = 64

    def feed_forward(mb):
        posts[0, mb].wait_recv()
        if mb == SHORT:
            posts[0, mb].wait_send()

        def norm_step(r):
            rows = aligned(r * tile_rows, tile_rows, tile_rows)
            joined = received(0, mb, rows) + param(OUTB) + x[mb, rows, :].astype(F32)
            centred = joined - mean(joined)
            root = lax.rsqrt(mean(centred * centred) + EPSILON)
            normed = centred * root
            norm_one[mb, rows, :] = normed
            root_one[mb, rows, :] = jnp.broadcast_to(root, (tile_rows, 128))
            all_rows = aligned(mb * tok + r * tile_rows, tile_rows, tile_rows)
            hidden[all_rows, :] = (normed * param(GAIN1) + param(BIAS1)).astype(BF16)

        loop(tok // tile_rows, norm_step)

        def col_step(j):
            lanes = aligned(j * 512, 512, 512)
            u = dot(hidden[tokens(mb), :], win[:, lanes]) + params[6:7, lanes]
            square = u * u
            t = jnp.tanh(ROOT * u * (1.0 + CUBIC * square))
            half = 0.5 * (1.0 + t)
            act[tokens(mb), lanes] = (u * half).astype(BF16)
            slope[mb, :, lanes] = (
                half + (0.5 * ROOT) * u * (1.0 - t * t) * (1.0 + (3.0 * CUBIC) * square)
            ).astype(BF16)

        loop(ff // 512, col_step)
        post_out[1, mb] = dot(act[tokens(mb), :], wout[...]).astype(BF16)

    key_corner.wait_recv()
    value_corner.wait_recv()
    pass_corner = links.copy(kv_long.at[:, place ^ 6], kv_long.at[:, place ^ 6], 1)
    attend(LONG, kv_long, live_long, (place ^ 6,))
    pass_corner.wait_recv()
    attend(LONG, kv_long, live_long, (place ^ 7,))
    attention_out(LONG)
    for item in (
        value_next, key_far, key_corner, value_corner,
        pass_next, pass_far, pass_corner,
    ):
        item.wait_send()
    for item in loads[7:]:
        item.wait()
    feed_forward(SHORT)
    posts[0, LONG].wait_send()
    posts[1, SHORT] = post(1, SHORT)
    feed_forward(LONG)
    posts[1, SHORT].wait_send()
    posts[1, LONG] = post(1, LONG)

    def norm_back(grad, normed, root):
        return root * (grad - mean(grad) - normed * mean(grad * normed))

    def feed_norm(mb):
        posts[1, mb].wait_recv()
        if mb == LONG:
            posts[1, mb].wait_send()

        def norm_step(r):
            rows = aligned(r * tile_rows, tile_rows, tile_rows)
            all_rows = aligned(mb * tok + r * tile_rows, tile_rows, tile_rows)
            hid = norm_one[mb, rows, :] * param(GAIN1) + param(BIAS1)
            second = received(1, mb, rows) + param(BACKB) + hid
            centred = second - mean(second)
            root = lax.rsqrt(mean(centred * centred) + EPSILON)
            normed = centred * root
            out[mb, rows, :] = (normed * param(GAIN2) + param(BIAS2)).astype(BF16)
            g = cot[mb, rows, :].astype(F32)
            vec_add(GAIN2, g * normed)
            vec_add(BIAS2, g)
            grad = norm_back(g * param(GAIN2), normed, root)
            vec_add(BACKB, grad)
            grad_rows[mb, rows, :] = grad
            grad_feed[all_rows, :] = grad.astype(BF16)

        loop(tok // tile_rows, norm_step)
        store(out.at[mb], out_in.at[mb])

    def feed_back(mb):
        def col_step(j):
            lanes = aligned(j * 512, 512, 512)
            grad_act = dot(grad_feed[tokens(mb), :], wout[lanes, :], 1, 1).astype(BF16)
            low = (grad_act.astype(F32) * slope[mb, :, lanes].astype(F32)).astype(BF16)
            grad_inner[tokens(mb), lanes] = low
            vec[6:7, lanes] += jnp.sum(low.astype(F32), axis=0, keepdims=True)

        loop(ff // 512, col_step)
        post_out[0, mb] = dot(grad_inner[tokens(mb), :], win[...], 1, 1).astype(BF16)

    feed_norm(SHORT)
    feed_back(SHORT)

    feed_norm(LONG)

    def reduction(index, part, total, got, order):
        return Reduction(links, part, total, fulls[index], got, order, ups[index], upper, local_sem.at[index])

    near_first, far_first = (1, 2, 4, 8), (1, 4, 8, 2)
    red = {
        "a": reduction(0, part_back_a, sum_back_a, got_back_a, near_first),
        "b": reduction(1, part_back_b, sum_back_b, got_back_b, near_first),
        "c": reduction(2, part_in_a, sum_in_a, got_in_a, far_first),
        "d": reduction(3, part_in_b, sum_in_b, got_in_b, near_first),
        "e": reduction(4, part_query, sum_query, got_query, near_first),
        "f": reduction(5, part_pair, sum_pair, got_pair, near_first),
        "v": reduction(6, part_vec, sum_vec, got_vec, near_first),
    }

    def back_grad(part, start):
        def step(j):
            rows = aligned(j * 256, 256, 256)
            lanes = aligned(start + j * 256, 256, 256)
            part[rows, :] = dot(act[:, lanes], grad_feed[...], 0, 0).astype(BF16)

        loop(ff // 512, step)

    def in_grad_half(part, start):
        def step(j):
            rows = aligned(j * 256, 256, 256)
            inner = grad_inner[:, start : start + ff // 2]
            part[rows, :] = dot(hidden[:, rows], inner, 0, 0).astype(BF16)

        loop(wide // 256, step)

    def norm_one_back(mb):
        posts[2, mb].wait()

        def norm_step(r):
            rows = aligned(r * tile_rows, tile_rows, tile_rows)
            all_rows = aligned(mb * tok + r * tile_rows, tile_rows, tile_rows)
            grad = grad_rows[mb, rows, :] + received(2, mb, rows)
            normed = norm_one[mb, rows, :]
            vec_add(GAIN1, grad * normed)
            vec_add(BIAS1, grad)
            joined = norm_back(grad * param(GAIN1), normed, root_one[mb, rows, :1])
            vec_add(OUTB, joined)
            grad_rows[mb, rows, :] = joined
            grad_attn[all_rows, :] = joined.astype(BF16)

        loop(tok // tile_rows, norm_step)
        low = dot(grad_attn[tokens(mb), :], outw[...], 1, 1).astype(BF16).astype(F32)
        for g in range(pairs):
            pair = low[:, g * 128 : g * 128 + 128]
            turned = pair.T
            g_rows[g] = spread_rows(pair)
            g_cols[g] = spread_cols(turned.astype(BF16))
            product = turned * mixed_cols[mb, g * 128 : g * 128 + 128, :]
            deltas[g] = jnp.concatenate(
                [
                    jnp.sum(product[:HDIM], axis=0, keepdims=True),
                    jnp.sum(product[HDIM:], axis=0, keepdims=True),
                ],
                1,
            )

    def attend_back(mb, kv, live, t, store, first=False):
        def pair_step(g):
            lanes = aligned(g * 128, 128, 128)
            keys = kv[0, t, :, lanes]
            values = kv[1, t, :, lanes]
            mask = live[t]
            scores = dot(keys, q_cols[mb, g]) + jnp.concatenate([mask, mask], 1)
            probs = jnp.exp(scores - tops[mb * pairs + g])
            grad_probs = dot(values, g_cols[g])
            low = (probs * (grad_probs - deltas[g])).astype(BF16)
            store(0, lanes, dot(low, q_rows[mb, g]).astype(BF16))
            store(1, lanes, dot(probs.astype(BF16), g_rows[g]).astype(BF16))
            turned = keys.T
            rows_a = aligned(g * 128, HDIM, HDIM)
            rows_b = aligned(g * 128 + HDIM, HDIM, HDIM)
            acc_a = dot(turned[:HDIM], low[:, :tok])
            acc_b = dot(turned[HDIM:], low[:, tok:])
            if not first:
                acc_a = acc_a + query_cols[rows_a, :]
                acc_b = acc_b + query_cols[rows_b, :]
            query_cols[rows_a, :] = acc_a
            query_cols[rows_b, :] = acc_b

        loop(pairs, pair_step)

    def query_done(mb):
        for g in range(pairs):
            lanes = slice(g * 128, g * 128 + 128)
            grad_proj[tokens(mb), lanes] = (query_cols[lanes, :] * (HDIM**-0.5)).T.astype(BF16)

    def store_short(t):
        def store(which, lanes, value):
            dkv_short[which, t, :, lanes] = value

        return store

    def store_long(j, c):
        def store(which, lanes, value):
            dkv_long[which, j, c, :, lanes] = value

        return store

    mine = (seq >> 1) & 3

    def add_block(which, j, more):
        dkv_long[which, j, core] = (
            dkv_long[which, j, core].astype(F32) + more[...].astype(F32)
        ).astype(BF16)

    def go_far(which, j, slot, delta):
        return links.copy(dkv_long.at[which, j, core], got_far.at[slot], delta)

    core_grads = []
    key_hop = []
    value_hop = []

    def long_back(d):
        j = mine ^ d
        attend_back(LONG, kv_long, live_long, 2 * j + 1 - core, store_long(j, 1 - core), d == 3)
        item = links.copy(dkv_long.at[:, j, 1 - core], got_core.at[:, j], 1)
        core_grads.append(item)
        attend_back(LONG, kv_long, live_long, 2 * j + core, store_long(j, core))
        item.wait_recv()
        for which in range(2):
            add_block(which, j, got_core.at[which, j])
        if d == 1:
            key_hop.extend([go_far(0, mine ^ 3, 0, 2), go_far(0, mine ^ 1, 1, 2)])
        if d == 2:
            value_hop.extend([go_far(1, mine ^ 3, 2, 4), go_far(1, mine ^ 2, 3, 4)])
        if d == 0:
            query_done(LONG)

    def second_hop():
        key_hop[0].wait_recv()
        add_block(0, mine ^ 2, got_far.at[0])
        key_hop.append(go_far(0, mine ^ 2, 4, 4))
        value_hop[0].wait_recv()
        add_block(1, mine ^ 1, got_far.at[2])
        value_hop.append(go_far(1, mine ^ 1, 5, 2))

    half_wide = wide // 2

    def out_step(j):
        lanes = aligned(j * half_wide, half_wide, half_wide)
        rows = aligned(j * col, col, col)
        part_query[rows, 0:col] = dot(mixed[...], grad_attn[:, lanes], 0, 0).astype(BF16)

    def x_grad(items):
        def step(j):
            rows = aligned(j * 256, 256, 256)
            columns = jnp.concatenate([x[0, :, rows], x[1, :, rows]], 0)
            for part, lanes, source in items:
                part[rows, lanes] = dot(columns, grad_proj[:, source], 0, 0).astype(BF16)

        loop(wide // 256, step)

    def input_part(mb):
        rows = tokens(mb)
        total = dot(grad_proj[rows, 0:col], qkvw[0], 1, 1)
        total = total + dot(grad_proj[rows, col : 2 * col], qkvw[1], 1, 1)
        total = total + dot(grad_proj[rows, 2 * col : 3 * col], qkvw[2], 1, 1)
        post_out[1, mb] = total.astype(BF16)
        posts[3, mb] = post(3, mb)

    def input_done(mb):
        posts[3, mb].wait()
        stores[mb].wait()

        def step(r):
            rows = aligned(r * tile_rows, tile_rows, tile_rows)
            out[mb, rows, :] = (grad_rows[mb, rows, :] + received(3, mb, rows)).astype(BF16)

        loop(tok // tile_rows, step)
        store(out.at[mb], in_grad_in.at[mb])

    short_grads = []

    def short_back():
        attend_back(SHORT, kv_short, live_short, 1 - side, store_short(1 - side), True)
        short_grads.append(links.copy(dkv_short.at[:, 1 - side], got_short, 1))
        attend_back(SHORT, kv_short, live_short, side, store_short(side))
        query_done(SHORT)

    def query_grad():
        loop(2, out_step)
        x_grad([(part_query, slice(col, 2 * col), slice(0, col))])

    def short_done():
        short_grads[0].wait()
        for which in range(2):
            lanes = slice((1 + which) * col, (2 + which) * col)
            total = dkv_short[which, side].astype(F32) + got_short[which].astype(F32)
            grad_proj[tokens(SHORT), lanes] = total.astype(BF16)

    def long_done():
        for hop, which in ((key_hop, 0), (value_hop, 1)):
            lanes = slice((1 + which) * col, (2 + which) * col)
            hop[1].wait_recv()
            hop[2].wait_recv()
            total = dkv_long[which, mine, core].astype(F32) + got_far[2 * which + 1].astype(F32)
            total = total + got_far[4 + which].astype(F32)
            grad_proj[tokens(LONG), lanes] = total.astype(BF16)

    def pair_grad():
        x_grad(
            [
                (part_pair, slice(0, col), slice(col, 2 * col)),
                (part_pair, slice(col, 2 * col), slice(2 * col, 3 * col)),
            ]
        )

    def vectors_done():
        vec[7:8, 0:col] = jnp.sum(grad_proj[:, 0:col].astype(F32), axis=0, keepdims=True)
        vec[7:8, col : 2 * col] = jnp.sum(
            grad_proj[:, 2 * col : 3 * col].astype(F32), axis=0, keepdims=True
        )
        part_vec[...] = jnp.zeros_like(part_vec)
        lines = []
        for index, width in [(i, wide) for i in range(6)] + [(7, 2 * col), (6, ff)]:
            for k in range(width // 128):
                lines.append(vec[index : index + 1, k * 128 : k * 128 + 128])
        while len(lines) % 16:
            lines.append(jnp.zeros((1, 128), F32))
        part_vec[0 : len(lines), :] = jnp.concatenate(lines, 0).astype(BF16)

    def post_now(stage, mb):
        posts[stage, mb] = post(stage, mb)

    steps = {
        "back_a": lambda: back_grad(part_back_a, 0),
        "back_b": lambda: back_grad(part_back_b, ff // 2),
        "feed_long": lambda: feed_back(LONG),
        "post_long": lambda: post_now(2, LONG),
        "in_c": lambda: in_grad_half(part_in_a, 0),
        "in_d": lambda: in_grad_half(part_in_b, ff // 2),
        "norm_long": lambda: norm_one_back(LONG),
        "post_short": lambda: post_now(2, SHORT),
        "long3": lambda: long_back(3),
        "long1": lambda: long_back(1),
        "long2": lambda: long_back(2),
        "long0": lambda: long_back(0),
        "hop": second_hop,
        "norm_short": lambda: norm_one_back(SHORT),
        "short_back": short_back,
        "query_e": query_grad,
        "short_done": short_done,
        "part_short": lambda: input_part(SHORT),
        "long_done": long_done,
        "pair_f": pair_grad,
        "vec_v": vectors_done,
        "part_long": lambda: input_part(LONG),
        "done_short": lambda: input_done(SHORT),
        "done_long": lambda: input_done(LONG),
    }
    for name, item in red.items():
        for i in range(4):
            steps[name + str(i)] = functools.partial(item.step, i)
        steps[name + "t"] = item.total
        steps[name + "s"] = item.keep
        for i in range(3):
            steps[name + "r" + str(i)] = functools.partial(item.back, i)
    for name in TAIL:
        steps[name]()
    for item in red.values():
        item.finish()
    for item in core_grads + key_hop + value_hop:
        item.wait_send()
    for item in stores[2:]:
        item.wait()


def widen(
    sum_back_a,
    sum_back_b,
    sum_in_a,
    sum_in_b,
    sum_query,
    sum_pair,
    sum_vec,
    out_in,
    grad_in,
    out,
    in_grad,
    g_back,
    g_inner,
    g_qkv,
    g_out,
    g_qv,
    g_in_bias,
    *rest,
):
    vectors = rest[:6]
    lows, highs, load_sem, store_sem, copy_sem = rest[6:11], rest[11:15], *rest[15:18]
    low_back, low_in, low_query, low_pair, low_vec = lows
    high_back, high_in, high_qkv, high_out = highs
    col = sum_query.shape[1] // 2
    wide = sum_query.shape[0]
    low_out, low_grad = rest[18:20]
    copies = [
        pltpu.make_async_copy(out_in, low_out, copy_sem.at[0]),
        pltpu.make_async_copy(grad_in, low_grad, copy_sem.at[1]),
    ]
    loads = {}
    half = wide // 2

    def load(name, src, dst):
        loads[name] = pltpu.make_async_copy(src, dst, load_sem.at[len(loads)])
        loads[name].start()

    first, second = pl.ds(0, half), pl.ds(half, half)
    load("vec", sum_vec, low_vec)
    load("query", sum_query, low_query)
    for part, name in ((first, "0"), (second, "1")):
        load("pair" + name, sum_pair.at[part], low_pair.at[part])
    for i, (back, inner) in enumerate(((sum_back_a, sum_in_a), (sum_back_b, sum_in_b))):
        for part, name in ((first, "0"), (second, "1")):
            load("back" + str(i) + name, back.at[part], low_back.at[i, part])
            load("in" + str(i) + name, inner.at[part], low_in.at[i, part])
    for item in copies:
        item.start()
    stores = []

    def store(src, dst):
        item = pltpu.make_async_copy(src, dst, store_sem.at[len(stores)])
        item.start()
        stores.append(item)

    def cast(dst, src, start, rows, lanes, src_lanes, src_start=None):
        shift = 0 if src_start is None else src_start - start

        def step(r):
            here = aligned(start + r * 32, 32, 32)
            there = aligned(start + shift + r * 32, 32, 32)
            dst[here, lanes] = src[there, src_lanes].astype(F32)

        loop(rows // 32, step)

    for item, low, high in zip(copies, (low_out, low_grad), (out, in_grad)):
        item.wait()
        store(low, high)
    loads["vec"].wait()
    full = low_vec[...].astype(F32)

    def line(row, count):
        return jnp.concatenate([full[r : r + 1, :] for r in range(row, row + count)], 1)

    per = wide // 128
    for i, vector in enumerate(vectors):
        vector[...] = line(i * per, per).reshape(wide)
    row = len(vectors) * per
    g_qv[...] = jnp.concatenate([line(row, col // 128), line(row + col // 128, col // 128)], 0)
    bias = line(row + 2 * col // 128, g_in_bias.shape[0] // 128)
    g_in_bias[...] = bias.reshape(g_in_bias.shape[0])
    left, right, every = pl.ds(0, col), pl.ds(col, col), slice(None)
    loads["query"].wait()
    cast(high_out, low_query, 0, col, left, left)
    cast(high_out, low_query, 0, col, right, left, col)
    store(high_out, g_out)
    cast(high_qkv.at[0], low_query, 0, wide, every, right)
    store(high_qkv.at[0], g_qkv.at[0])
    for part, name, start in ((first, "0", 0), (second, "1", half)):
        loads["pair" + name].wait()
        cast(high_qkv.at[1], low_pair, start, half, every, left)
        cast(high_qkv.at[2], low_pair, start, half, every, right)
        store(high_qkv.at[1, part], g_qkv.at[1, part])
        store(high_qkv.at[2, part], g_qkv.at[2, part])
    for i in range(2):
        for part, name, start in ((first, "0", 0), (second, "1", half)):
            loads["back" + str(i) + name].wait()
            cast(high_back.at[i], low_back.at[i], start, half, every, every)
            store(high_back.at[i, part], g_back.at[i, part])
            loads["in" + str(i) + name].wait()
            cast(high_in.at[i], low_in.at[i], start, half, every, every)
            lanes = pl.ds(i * wide, wide)
            store(high_in.at[i, part], g_inner.at[part, lanes])
    for item in stores:
        item.wait()


def body(
    seq_count,
    inputs,
    qkv_weight,
    qv_bias,
    out_weight,
    out_bias,
    ln1_gain,
    ln1_bias,
    ffn_in,
    ffn_in_bias,
    ffn_out,
    ffn_out_bias,
    ln2_gain,
    ln2_bias,
    short_lengths,
    long_lengths,
    short_random,
    long_random,
    cotangent,
):
    tok, wide = inputs.shape[1:]
    col = qkv_weight.shape[2]
    ff = ffn_in.shape[1]
    pairs = col // (2 * HDIM)
    short_span = seq_count // short_lengths.shape[0]
    long_span = seq_count // long_lengths.shape[0]
    upper = max(0, seq_count.bit_length() - 5)

    parts = [(ff // 2, wide)] * 2 + [(wide, ff // 2)] * 2 + [(wide, 2 * col)] * 2 + [(VEC_ROWS, 128)]
    vmem = pltpu.VMEM
    scratch = [
        pltpu.SMEM(short_lengths.shape, jnp.int32),
        pltpu.SMEM(long_lengths.shape, jnp.int32),
        pltpu.SMEM(short_random.shape, jnp.int32),
        pltpu.SMEM(long_random.shape, jnp.int32),
        vmem((2, tok, wide), BF16),
        vmem((2, tok, wide), BF16),
        vmem((2, tok, wide), BF16),
        vmem((3, wide, col), BF16),
        vmem((col, wide), BF16),
        vmem((wide, ff), BF16),
        vmem((ff, wide), BF16),
        vmem((8, ff), F32),
        vmem((2, short_span, tok, col), BF16),
        vmem((2, long_span, tok, col), BF16),
        vmem((2, pairs, 128, 2 * tok), BF16),
        vmem((2, pairs, 2 * tok, 128), BF16),
        vmem((short_span, tok, tok), F32),
        vmem((long_span, tok, tok), F32),
        vmem((2, col, tok), F32),
        vmem((2 * tok, col), BF16),
        vmem((2 * pairs, 1, 2 * tok), F32),
        vmem((2 * pairs, 1, 2 * tok), F32),
        vmem((2, 2, tok, wide), BF16),
        vmem((2, 2, tok, wide), BF16),
        vmem((2, tok, wide), F32),
        vmem((2, tok, 128), F32),
        vmem((2 * tok, wide), BF16),
        vmem((2 * tok, ff), BF16),
        vmem((2, tok, ff), BF16),
        vmem((2, tok, wide), F32),
        vmem((2 * tok, wide), BF16),
        vmem((2 * tok, ff), BF16),
        vmem((2 * tok, wide), BF16),
        vmem((pairs, 128, 2 * tok), BF16),
        vmem((pairs, 2 * tok, 128), BF16),
        vmem((pairs, 1, 2 * tok), F32),
        vmem((col, tok), F32),
        vmem((2, short_span, tok, col), BF16),
        vmem((2, long_span // 2, 2, tok, col), BF16),
        vmem((2, tok, col), BF16),
        vmem((2, long_span // 2, tok, col), BF16),
        vmem((6, tok, col), BF16),
        vmem((2 * tok, 3 * col), BF16),
    ]
    scratch += [vmem(shape, BF16) for shape in parts]
    scratch += [vmem((8, ff), F32)]
    scratch += [vmem((r - r // 16, w), BF16) for r, w in parts]
    if upper:
        scratch += [vmem((upper, r // 16, w), BF16) for r, w in parts]
    scratch += [vmem(shape, BF16) for shape in parts]
    scratch += [
        pltpu.SemaphoreType.DMA((COPIES,)),
        pltpu.SemaphoreType.DMA((COPIES,)),
        pltpu.SemaphoreType.DMA((16,)),
        pltpu.SemaphoreType.DMA((8,)),
    ]
    any_spec = pl.BlockSpec(memory_space=pl.ANY)
    vmem_spec = pl.BlockSpec(memory_space=pltpu.VMEM)
    out, in_grad, s_back_a, s_back_b, s_in_a, s_in_b, s_query, s_pair, s_vec = pl.pallas_call(
        functools.partial(kernel, seq_count),
        out_shape=[
            jax.ShapeDtypeStruct(inputs.shape, BF16),
            jax.ShapeDtypeStruct(inputs.shape, BF16),
        ]
        + [jax.ShapeDtypeStruct(shape, BF16) for shape in parts],
        in_specs=[any_spec] * 6 + [vmem_spec] * 8 + [any_spec] * 4,
        out_specs=[any_spec] * 9,
        scratch_shapes=scratch,
        compiler_params=pltpu.CompilerParams(
            collective_id=0, has_side_effects=True, vmem_limit_bytes=65_000 * 1024
        ),
        cost_estimate=pl.CostEstimate(
            flops=12_000_000_000, bytes_accessed=40_000_000, transcendentals=8_000_000
        ),
        name="layer",
    )(
        inputs,
        cotangent,
        qkv_weight,
        out_weight,
        ffn_in,
        ffn_out,
        qv_bias,
        out_bias,
        ln1_gain,
        ln1_bias,
        ffn_out_bias,
        ln2_gain,
        ln2_bias,
        ffn_in_bias,
        short_lengths,
        long_lengths,
        short_random,
        long_random,
    )
    vector = jax.ShapeDtypeStruct((wide,), F32)
    out, in_grad, g_back, g_inner, g_qkv, g_out, g_qv, g_in_bias, *vectors = pl.pallas_call(
        widen,
        out_shape=[
            jax.ShapeDtypeStruct(inputs.shape, BF16),
            jax.ShapeDtypeStruct(inputs.shape, BF16),
            jax.ShapeDtypeStruct((2, ff // 2, wide), F32),
            jax.ShapeDtypeStruct((wide, ff), F32),
            jax.ShapeDtypeStruct((3, wide, col), F32),
            jax.ShapeDtypeStruct((col, wide), F32),
            jax.ShapeDtypeStruct((2, col), F32),
            jax.ShapeDtypeStruct((ff,), F32),
        ]
        + [vector] * 6,
        in_specs=[any_spec] * 9,
        out_specs=[any_spec] * 6 + [vmem_spec] * 8,
        scratch_shapes=[
            vmem((2, wide, wide), BF16),
            vmem((2, wide, wide), BF16),
            vmem((wide, 2 * col), BF16),
            vmem((wide, 2 * col), BF16),
            vmem((VEC_ROWS, 128), BF16),
            vmem((2, wide, wide), F32),
            vmem((2, wide, wide), F32),
            vmem((3, wide, col), F32),
            vmem((col, wide), F32),
            pltpu.SemaphoreType.DMA((16,)),
            pltpu.SemaphoreType.DMA((20,)),
            pltpu.SemaphoreType.DMA((2,)),
            vmem(inputs.shape, BF16),
            vmem(inputs.shape, BF16),
        ],
        compiler_params=pltpu.CompilerParams(vmem_limit_bytes=63 * 1024 * 1024),
        name="widen",
    )(s_back_a, s_back_b, s_in_a, s_in_b, s_query, s_pair, s_vec, out, in_grad)
    return (
        out,
        in_grad,
        g_qkv,
        g_qv,
        g_out,
        vectors[0],
        vectors[1],
        vectors[2],
        g_inner,
        g_in_bias,
        g_back.reshape(ff, wide),
        vectors[3],
        vectors[4],
        vectors[5],
    )


def solution(mesh):
    return jax.shard_map(
        functools.partial(body, mesh.shape["seq"]),
        mesh=mesh,
        in_specs=(
            P(None, "seq", None),
            P(None, None, "head"),
            P(None, "head"),
            P("head", None),
            P(),
            P(),
            P(),
            P(None, "head"),
            P("head"),
            P("head", None),
            P(),
            P(),
            P(),
            P(),
            P(),
            P("seq", None),
            P("seq", None),
            P(None, "seq", None),
        ),
        out_specs=(
            P(None, "seq", None),
            P(None, "seq", None),
            P(None, None, "head"),
            P(None, "head"),
            P("head", None),
            P(),
            P(),
            P(),
            P(None, "head"),
            P("head"),
            P("head", None),
            P(),
            P(),
            P(),
        ),
        check_vma=False,
    )
```
